512 devices in a mesh: ctx: 32 (over y, x, core), tp: 16 (over z).
Axes of the slice: x: 4, y: 4, z: 16, core: 2. Of those that a mesh axis runs over, the one named last changes fastest.
Arguments:
- queries: bfloat16 [8192, 2048], P('ctx', 'tp'), may hold values from -6 to 6
- key_vectors: bfloat16 [8192, 2048], P('ctx', 'tp'), may hold values from -4 to 4
- value_vectors: bfloat16 [8192, 4096], P('ctx', 'tp'), may hold values from -6 to 6
- output_gate: bfloat16 [8192, 4096], P('ctx', 'tp'), may hold values from -6 to 6
- write_rate: float32 [8192, 32], P('ctx', 'tp'), may hold values from 0 to 1, as said below
- log_decay: float32 [8192, 32], P('ctx', 'tp'), may hold values from -1 to 0, as said below
- norm_gain: float32 [128], replicated, may hold values from 0.5 to 2
- out_weight: bfloat16 [4096, 2048], P('tp'), may hold values from -0.09375 to 0.09375
Outputs:
- mixed: bfloat16 [8192, 2048], P(('ctx', 'tp'))
The draws below stay inside these ranges and needn't reach their ends.
Inputs may be any that keep to these rules, and one draw needn't show every extreme that they name: `write_rate`: write strengths are positive. `log_decay`: log decays are negative.
All inputs are finite; a program needn't handle non-finite values.
Results may differ from the reference program's by a relative error of at most 0.025.
Values may be sent and summed in bfloat16 or wider, within the bound.
No kernel may reach another device: no remote copies, remote signals or barrier semaphores. Data moves between devices by JAX's collectives and lax.ppermute only.
A program may use at most 64 MiB of HBM per device.

```python
import jax
import jax.numpy as jnp
from jax import lax

DK = 128
DV = 128
HK = 16
VALUE_HEAD_COUNT = 32
D = 2048
TOK_DEV = 256
SEQUENCE_TOKENS = 8192
N_TP = 16


def draw_key_vectors(key, part):
    key = jax.random.fold_in(key, 37)
    sequence_parts = jax.random.split(key, 2)
    sub_count = min(16, DK // 2)
    block_rows = 16
    block_count = SEQUENCE_TOKENS // block_rows
    head_keys = jax.random.split(sequence_parts[0], block_count * HK)
    orders = jax.vmap(lambda single: jax.random.permutation(single, DK))(head_keys)
    inside = (orders < sub_count).reshape(block_count, 1, HK * DK)
    weight_map = jnp.where(inside, 1.0, 0.4 * DK ** (-0.5)).astype(jnp.float32)
    weight_map = jnp.broadcast_to(weight_map, (block_count, block_rows, HK * DK)).reshape(SEQUENCE_TOKENS, HK * DK)
    raw_entries = jnp.clip(jax.random.normal(sequence_parts[1], (SEQUENCE_TOKENS, HK * DK), jnp.float32), -4.0, 4.0)
    return (raw_entries * weight_map).astype(jnp.bfloat16)


def draw_write_rate(key, part):
    key = jax.random.fold_in(key, 11)
    sequence_parts = jax.random.split(key, 2)
    levels = jnp.exp(jax.random.uniform(sequence_parts[0], (VALUE_HEAD_COUNT,), jnp.float32, -2.5, -1.05))
    jitter_factor = jax.random.uniform(sequence_parts[1], (SEQUENCE_TOKENS, VALUE_HEAD_COUNT), jnp.float32, 0.5, 1.5)
    return (levels[None, :] * jitter_factor).astype(jnp.float32)


def draw_log_decay(key, part):
    key = jax.random.fold_in(key, 23)
    sequence_parts = jax.random.split(key, 7)
    quick_share = 0.5
    jitter_factor = jax.random.uniform(sequence_parts[4], (SEQUENCE_TOKENS, VALUE_HEAD_COUNT), jnp.float32, 0.5, 1.5)
    quick_heads = jax.random.uniform(sequence_parts[0], (VALUE_HEAD_COUNT,), jnp.float32) < quick_share
    slow_rate = jax.random.uniform(sequence_parts[1], (VALUE_HEAD_COUNT,), jnp.float32, 0.05, 0.5) / SEQUENCE_TOKENS
    quick_rate = 1.0 / jax.random.uniform(sequence_parts[2], (VALUE_HEAD_COUNT,), jnp.float32, 30.0, 50.0)
    baseline = jnp.where(quick_heads, quick_rate, slow_rate)
    shard_scale = jnp.exp(jax.random.uniform(sequence_parts[3], (SEQUENCE_TOKENS // TOK_DEV, VALUE_HEAD_COUNT), jnp.float32, -0.7, 0.7))
    shard_scale = jnp.repeat(shard_scale, TOK_DEV, axis=0)
    spike_position = jax.random.randint(sequence_parts[5], (3,), 0, SEQUENCE_TOKENS)
    struck_value = jnp.any(jnp.arange(SEQUENCE_TOKENS)[:, None] == spike_position[None, :], axis=1)
    spike_penalty = jnp.log(jax.random.uniform(sequence_parts[6], (SEQUENCE_TOKENS, VALUE_HEAD_COUNT), jnp.float32, 0.55, 0.8))
    steady_decay = -baseline[None, :] * shard_scale * jitter_factor
    return (steady_decay + jnp.where(struck_value[:, None], spike_penalty, 0.0)).astype(jnp.float32)


def block_scale(key, extent, shards, least, largest):
    factor_of, own = 1.0, jax.random.fold_in(key, 6)
    for position, shards_of in shards:
        steps = jnp.exp(jax.random.uniform(jax.random.fold_in(own, position), (shards_of,), jnp.float32, least / len(shards), largest / len(shards)))
        factor_of = factor_of * jnp.repeat(steps, extent[position] // shards_of).reshape([-1 if axis == position else 1 for axis in range(len(extent))])
    return factor_of


def scatter_about(own_key, extent, deviation, reach, pieces=(), kind=jnp.bfloat16):
    drawn = jax.random.normal(own_key, extent, jnp.float32) * deviation
    if len(pieces) > 0:
        drawn = block_scale(own_key, extent, pieces, -0.22, 0.18) * drawn
    return jnp.clip(drawn, min=-reach, max=reach).astype(kind)


def setup_inputs(seed: int = 0) -> dict:
    splits = jax.random.split(jax.random.key(seed), 9)
    queries = scatter_about(splits[0], (SEQUENCE_TOKENS, HK * DK), 1.0, 6.0, ((0, 32), (1, 16)))
    key_vectors = draw_key_vectors(jax.random.fold_in(splits[8], 71), 0)
    value_vectors = scatter_about(splits[2], (SEQUENCE_TOKENS, VALUE_HEAD_COUNT * DV), 1.0, 6.0, ((0, 32), (1, 16)))
    output_gate = scatter_about(splits[3], (SEQUENCE_TOKENS, VALUE_HEAD_COUNT * DV), 1.0, 6.0, ((0, 32), (1, 16)))
    write_rate = draw_write_rate(jax.random.fold_in(splits[8], 71), 0)
    log_decay = draw_log_decay(jax.random.fold_in(splits[8], 71), 0)
    norm_gain = jnp.clip(jax.random.uniform(splits[6], (DV,), jnp.float32, 0.5, 2.0), 0.5, 2.0)
    out_weight = scatter_about(splits[7], (VALUE_HEAD_COUNT * DV, D), (VALUE_HEAD_COUNT * DV) ** -0.5, 0.09375, ((0, 16),))
    return {"queries": queries, "key_vectors": key_vectors, "value_vectors": value_vectors, "output_gate": output_gate, "write_rate": write_rate, "log_decay": log_decay, "norm_gain": norm_gain, "out_weight": out_weight}


highest_precision = lax.Precision.HIGHEST

def unit_vectors(source, count_heads, size_head):
    values_f = source.astype(jnp.float32).reshape(count_heads, size_head)
    return values_f * lax.rsqrt(lax.optimization_barrier(jnp.sum(values_f * values_f, axis=-1, keepdims=True)) + 1e-06)

def reference(queries, key_vectors, value_vectors, output_gate, write_rate, log_decay, norm_gain, out_weight):
    sharing = VALUE_HEAD_COUNT // HK

    def advance(carried_state, inputs):
        query_row, key_row, value_row, gate_row, rate_row, decay_row = inputs
        normalized_query = jnp.repeat(unit_vectors(query_row, HK, DK), sharing, axis=0)
        normalized_key = jnp.repeat(unit_vectors(key_row, HK, DK), sharing, axis=0)
        value_full = value_row.astype(jnp.float32).reshape(VALUE_HEAD_COUNT, DV)
        memory_readout = jnp.einsum('ns,nsd->nd', normalized_key, carried_state, precision=highest_precision)
        strength = rate_row[:, None, None]
        erased = carried_state - strength * normalized_key[:, :, None] * memory_readout[:, None, :]
        carried_state = jnp.exp(decay_row)[:, None, None] * erased + strength * normalized_key[:, :, None] * value_full[:, None, :]
        attention_core = jnp.einsum('ns,nsd->nd', normalized_query, carried_state, precision=highest_precision)
        square_mean = lax.optimization_barrier(jnp.mean(attention_core * attention_core, axis=-1, keepdims=True))
        gate_full = gate_row.astype(jnp.float32).reshape(VALUE_HEAD_COUNT, DV)
        normed = attention_core * lax.rsqrt(square_mean + 1e-06) * norm_gain * jax.nn.silu(gate_full)
        return (carried_state, normed.reshape(VALUE_HEAD_COUNT * DV).astype(jnp.bfloat16))
    initial = jnp.zeros((VALUE_HEAD_COUNT, DK, DV), jnp.float32)
    _, normed_all = lax.scan(advance, initial, (queries, key_vectors, value_vectors, output_gate, write_rate, log_decay))
    group_width = VALUE_HEAD_COUNT * DV // N_TP
    total = jnp.zeros((SEQUENCE_TOKENS, D), jnp.float32)
    for group_index in range(N_TP):
        lower_edge = group_index * group_width
        part_sum = jnp.dot(normed_all[:, lower_edge:lower_edge + group_width], out_weight[lower_edge:lower_edge + group_width], preferred_element_type=jnp.float32).astype(jnp.bfloat16)
        part_sum = lax.optimization_barrier(part_sum)
        total = total + part_sum.astype(jnp.float32)
    return total.astype(jnp.bfloat16)
```

```python
import jax
import jax.numpy as jnp
from jax import lax
from jax.experimental import pallas as pl
from jax.experimental.pallas import tpu as pltpu
from jax.sharding import PartitionSpec as P

F32 = jnp.float32
BF = jnp.bfloat16
TOK = 256
DK = 128
DV = 128
HALF = 128


def dot(a, b, dims=((1,), (0,))):
    return lax.dot_general(a, b, (dims, ((), ())), preferred_element_type=F32)


def split(a):
    hi = a.astype(BF)
    return hi, (a - hi.astype(F32)).astype(BF)


def dot_fine(a, b, dims=((1,), (0,))):
    ah, al = split(a)
    bh, bl = split(b)
    return dot(ah, bh, dims) + (dot(ah, bl, dims) + dot(al, bh, dims))


def dot_left(a, b, dims=((1,), (0,))):
    ah, al = split(a)
    return dot(ah, b, dims) + dot(al, b, dims)


def dot_right(a, b, dims=((1,), (0,))):
    bh, bl = split(b)
    return dot(a, bh, dims) + dot(a, bl, dims)


def grid_iota(rows, cols):
    return (
        lax.broadcasted_iota(jnp.int32, (rows, cols), 0),
        lax.broadcasted_iota(jnp.int32, (rows, cols), 1),
    )


def to_row(eye, column):
    return jnp.sum(jnp.where(eye, column, 0.0), axis=0, keepdims=True)


def decay_columns(decay):
    row, col = grid_iota(TOK, TOK)
    ones = jnp.where(row >= col, 1.0, 0.0).astype(BF)
    hi = decay.astype(BF).astype(F32)
    rest = decay - hi
    mid = rest.astype(BF).astype(F32)
    low = rest - mid
    lane = lax.broadcasted_iota(jnp.int32, (TOK, 128), 1)
    parts = jnp.zeros((TOK, 128), F32)
    for place, piece in enumerate((hi, mid, low)):
        for head in range(2):
            parts = jnp.where(lane == 2 * place + head, piece[:, head : head + 1], parts)
    sums = dot(ones, parts.astype(BF))
    return [
        sums[:, head : head + 1] + (sums[:, 2 + head : 3 + head] + sums[:, 4 + head : 5 + head])
        for head in range(2)
    ]


def unit_scale(source):
    full = source.astype(F32)
    return lax.rsqrt(jnp.sum(full * full, axis=1, keepdims=True) + 1e-06)


def map_kernel(k_ref, v_ref, rate_ref, decay_ref, maps_ref, solved_ref):
    keys = k_ref[...]
    keys_f = keys.astype(F32)
    values = v_ref[...].astype(F32)
    rate = rate_ref[...]
    row, col = grid_iota(TOK, TOK)
    eye = row == col
    strict = row > col
    gram = dot(keys, keys, ((1,), (1,)))
    scale = unit_scale(keys)
    gram = gram * scale * to_row(eye, scale)
    sums = decay_columns(decay_ref[...])
    r_s, c_s = grid_iota(HALF, HALF)
    eye_s = jnp.where(r_s == c_s, 1.0, 0.0).astype(F32)

    lowers, corners = [], []
    for head in range(2):
        fall = jnp.exp(jnp.minimum(sums[head] - to_row(eye, sums[head]), 0.0))
        low = jnp.where(strict, rate[:, head : head + 1] * gram * fall, 0.0)
        lowers += [low[:HALF, :HALF], low[HALF:, HALF:]]
        corners.append(low[HALF:, :HALF])

    small = (r_s // 8) == (c_s // 8)
    first = [jnp.where(small, low, 0.0) for low in lowers]
    first_b = [a.astype(BF) for a in first]
    square = [dot(a, a).astype(BF) for a in first_b]
    fourth = [dot(a, a).astype(BF) for a in square]
    inv = [eye_s - a for a in first]
    inv = [x + dot(x.astype(BF), a) for x, a in zip(inv, square)]
    inv = [x + dot(x.astype(BF), a) for x, a in zip(inv, fourth)]
    size = 8
    while size < HALF:
        off = ((r_s // (2 * size)) == (c_s // (2 * size))) & ((r_s // size) > (c_s // size))
        inv_b = [x.astype(BF) for x in inv]
        part = [jnp.where(off, low, 0.0).astype(BF) for low in lowers]
        part = [dot(a, x).astype(BF) for a, x in zip(part, inv_b)]
        inv = [x - dot(xb, a) for x, xb, a in zip(inv, inv_b, part)]
        size *= 2
    inv_b = [x.astype(BF) for x in inv]
    gap = [
        eye_s - xb.astype(F32) - dot_left(low, xb) for low, xb in zip(lowers, inv_b)
    ]
    inv = [xb.astype(F32) + dot(xb, g.astype(BF)) for xb, g in zip(inv_b, gap)]

    eye_k = jnp.where(r_s == c_s, 1.0, 0.0).astype(F32)
    solved = []
    for head in range(2):
        b = rate[:, head : head + 1]
        grow = b * jnp.exp(sums[head]) * scale
        right = jnp.concatenate(
            [grow * keys_f, b * values[:, head * DV : (head + 1) * DV]], axis=1
        )
        top = dot_fine(inv[2 * head], right[:HALF])
        solved.append((top, right[HALF:]))
    for head in range(2):
        top, below = solved[head]
        below = below - dot_fine(corners[head], top)
        below = dot_fine(inv[2 * head + 1], below)
        solved[head] = jnp.concatenate([top, below], axis=0)
    maps = []
    for head in range(2):
        closing = sums[head][TOK - 1 :, :]
        weight = scale * jnp.exp(closing - sums[head])
        moved = dot_right(keys, weight * solved[head], ((0,), (0,)))
        transit = eye_k * jnp.exp(closing) - moved[:, :DK]
        maps.append(jnp.concatenate([transit, moved[:, DK:]], axis=1).astype(BF))
    for place in range(maps_ref.shape[0]):
        maps_ref[place] = maps[place % 2]
    for head in range(2):
        solved_ref[head] = solved[head]


def read_kernel(
    q_ref, k_ref, decay_ref, gate_ref, gain_ref, solved_ref, inner_ref, outer_ref, gated_ref
):
    queries = q_ref[...]
    keys = k_ref[...]
    row, col = grid_iota(TOK, TOK)
    eye = row == col
    inclusive = row >= col
    unit_q = unit_scale(queries)
    scores = dot(queries, keys, ((1,), (1,))) * unit_q * to_row(eye, unit_scale(keys))
    sums = decay_columns(decay_ref[...])
    for head in range(2):
        fall = jnp.exp(jnp.minimum(sums[head] - to_row(eye, sums[head]), 0.0))
        weights = jnp.where(inclusive, scores * fall, 0.0)
        both = dot_fine(weights, solved_ref[head])
        outer_ref[head] = jnp.exp(sums[head]) * unit_q * queries.astype(F32) - both[:, :DK]
        inner_ref[head] = both[:, DK:]
        gate = gate_ref[:, head * DV : (head + 1) * DV].astype(F32)
        gated_ref[head] = gain_ref[...] * (gate / (1.0 + jnp.exp(-gate)))


def after(later_t, later_h, earlier, fine):
    moved = dot_fine(later_t, earlier) if fine else dot_right(later_t, earlier)
    return jnp.concatenate([moved[:, :DK], moved[:, DK:] + later_h], axis=1)


def row_kernel(place_ref, parts_ref, total_ref, ahead_ref, first_ref):
    x = place_ref[1]

    def pair(i):
        later = parts_ref[2 * i + 1]
        moved = dot(later[:, :DK], parts_ref[2 * i])
        return jnp.concatenate(
            [moved[:, :DK], moved[:, DK:] + later[:, DK:].astype(F32)], axis=1
        )

    pairs = [pair(i) for i in range(4)]
    upto2 = pairs[0]
    upto4 = after(pairs[1][:, :DK], pairs[1][:, DK:], upto2, True)
    last2 = after(pairs[3][:, :DK], pairs[3][:, DK:], pairs[2], True)
    upto6 = after(pairs[2][:, :DK], pairs[2][:, DK:], upto4, True)
    total = after(last2[:, :DK], last2[:, DK:], upto4, True).astype(BF)
    for place in range(4):
        total_ref[place] = total
    row, col = grid_iota(DK, DK + DV)
    none = jnp.where(row == col, 1.0, 0.0).astype(F32)
    ahead_ref[...] = jnp.where(
        x == 0, none, jnp.where(x == 1, upto2, jnp.where(x == 2, upto4, upto6))
    )
    first_ref[...] = parts_ref[2 * x]


def state_kernel(place_ref, rows_ref, ahead_ref, first_ref, send_ref, mine_ref):
    y = place_ref[0]
    core = place_ref[2]

    def onward(later, state):
        return dot_right(later[:, :DK], state) + later[:, DK:].astype(F32)

    one = rows_ref[0][:, DK:].astype(F32)
    two = onward(rows_ref[1], one)
    three = onward(rows_ref[2], two)
    start = jnp.where(
        y == 0, jnp.zeros_like(one), jnp.where(y == 1, one, jnp.where(y == 2, two, three))
    )
    ahead = ahead_ref[...]
    chip = dot_fine(ahead[:, :DK], start) + ahead[:, DK:]
    second = onward(first_ref[...], chip)
    send_ref[...] = jnp.where(core == 0, second, chip).astype(BF)
    mine_ref[...] = jnp.where(core == 0, chip, second).astype(BF)


def out_kernel(place_ref, mine_ref, came_ref, inner_ref, outer_ref, gated_ref, out_ref):
    core = place_ref[2]
    mine = mine_ref[...].astype(F32)
    came = came_ref[...].astype(F32)
    for head in range(2):
        state = jnp.where(core == head, mine, came).astype(BF)
        reached = inner_ref[head] + dot_left(outer_ref[head], state)
        mean = jnp.sum(reached * reached, axis=1, keepdims=True) * (1.0 / DV)
        normed = (reached * lax.rsqrt(mean + 1e-06) * gated_ref[head]).astype(BF)
        for group in range(4):
            for near in range(4):
                piece = normed[(4 * group + near) * 16 : (4 * group + near + 1) * 16]
                for c in range(2):
                    out_ref[
                        4 * c + near,
                        group * 16 : (group + 1) * 16,
                        head * DV : (head + 1) * DV,
                    ] = piece


def project_kernel(normed_ref, weight_ref, out_ref):
    for core in range(2):
        total = None
        for near in range(4):
            term = dot(normed_ref[4 * core + near], weight_ref[near * 256 : (near + 1) * 256])
            total = term if total is None else total + term
        total = total.astype(BF)
        for group in range(4):
            out_ref[4 * core + group] = total[group * 16 : (group + 1) * 16]


def sum_kernel(parts_ref, out_ref):
    width = parts_ref.shape[2]
    for core in range(2):
        total = parts_ref[4 * core].astype(F32)
        for group in range(1, 4):
            total = total + parts_ref[4 * core + group].astype(F32)
        out_ref[:, core * width : (core + 1) * width] = total.astype(BF)


def in_vmem():
    return pl.BlockSpec(memory_space=pltpu.VMEM)


def call(kernel, outs, *args, scalars=0, flops=10**8, name=None):
    return pl.pallas_call(
        kernel,
        out_shape=outs,
        in_specs=[pl.BlockSpec(memory_space=pltpu.SMEM)] * scalars
        + [in_vmem()] * (len(args) - scalars),
        out_specs=jax.tree.map(lambda _: in_vmem(), outs),
        compiler_params=pltpu.CompilerParams(vmem_limit_bytes=32 * 1024 * 1024),
        cost_estimate=pl.CostEstimate(flops=flops, bytes_accessed=10**6, transcendentals=0),
        name=name,
    )(*args)


def shape(dims, kind):
    return jax.ShapeDtypeStruct(dims, kind)


def local(
    queries, key_vectors, value_vectors, output_gate, write_rate, log_decay, norm_gain, out_weight
):
    at = lax.axis_index("ctx")
    core = at % 2
    place = jnp.stack([at // 8, (at // 2) % 4, core]).astype(jnp.int32)
    width = out_weight.shape[1] // 2

    own_half = lax.dynamic_slice_in_dim(out_weight, core * width, width, axis=1)
    near = [[4 * g + j for j in range(4)] for g in range(4)]
    weight = lax.all_gather(own_half, "tp", axis_index_groups=near, tiled=True)

    maps, solved = call(
        map_kernel,
        (shape((8, DK, DK + DV), BF), shape((2, TOK, DK + DV), F32)),
        key_vectors,
        value_vectors,
        write_rate,
        log_decay,
        flops=10**9,
        name="shard_maps",
    )
    lines = [[8 * y + i for i in range(8)] for y in range(4)]
    parts = lax.all_to_all(maps, "ctx", 0, 0, axis_index_groups=lines)
    inner, outer, gated = call(
        read_kernel,
        (shape((2, TOK, DV), F32), shape((2, TOK, DK), F32), shape((2, TOK, DV), F32)),
        queries,
        key_vectors,
        log_decay,
        output_gate,
        norm_gain.reshape(1, DV),
        solved,
        flops=10**9,
        name="read_parts",
    )
    total, ahead, first = call(
        row_kernel,
        (shape((4, DK, DK + DV), BF), shape((DK, DK + DV), F32), shape((DK, DK + DV), BF)),
        place,
        parts,
        scalars=1,
        name="row_maps",
    )
    columns = [[8 * y + i for y in range(4)] for i in range(8)]
    rows = lax.all_to_all(total, "ctx", 0, 0, axis_index_groups=columns)
    send, mine = call(
        state_kernel,
        (shape((DK, DV), BF), shape((DK, DV), BF)),
        place,
        rows,
        ahead,
        first,
        scalars=1,
        name="states",
    )
    came = lax.ppermute(send, "ctx", [(i, i ^ 1) for i in range(32)])
    normed = call(
        out_kernel,
        shape((8, 64, 2 * DV), BF),
        place,
        mine,
        came,
        inner,
        outer,
        gated,
        scalars=1,
        name="gated_norm",
    )
    close, far = [], []
    for chip in range(16):
        for i in range(4):
            close.append([(2 * chip + c) * 16 + 4 * i + j for c in range(2) for j in range(4)])
            far.append([(2 * chip + c) * 16 + 4 * j + i for c in range(2) for j in range(4)])
    both = ("ctx", "tp")
    gathered = lax.all_to_all(normed, both, 0, 0, axis_index_groups=close)
    partial = call(
        project_kernel,
        shape((8, 16, width), BF),
        gathered,
        weight,
        name="project",
    )
    shares = lax.all_to_all(partial, both, 0, 0, axis_index_groups=far)
    return call(sum_kernel, shape((16, 2 * width), BF), shares, name="sum_shares")


def solution(mesh):
    placed = (
        P("ctx", "tp"),
        P("ctx", "tp"),
        P("ctx", "tp"),
        P("ctx", "tp"),
        P("ctx", "tp"),
        P("ctx", "tp"),
        P(),
        P("tp", None),
    )
    return jax.shard_map(
        local, mesh=mesh, in_specs=placed, out_specs=P(("ctx", "tp"), None), check_vma=False
    )
```

```python
import jax
import jax.numpy as jnp
from jax import lax
from jax.experimental import pallas as pl
from jax.experimental.pallas import tpu as pltpu
from jax.sharding import PartitionSpec as P

F32 = jnp.float32
BF = jnp.bfloat16
TOK = 256
DK = 128
DV = 128
HALF = 128


def dot(a, b, dims=((1,), (0,))):
    return lax.dot_general(a, b, (dims, ((), ())), preferred_element_type=F32)


def split(a):
    hi = a.astype(BF)
    return hi, (a - hi.astype(F32)).astype(BF)


def dot_fine(a, b, dims=((1,), (0,))):
    ah, al = split(a)
    bh, bl = split(b)
    return dot(ah, bh, dims) + (dot(ah, bl, dims) + dot(al, bh, dims))


def dot_left(a, b, dims=((1,), (0,))):
    ah, al = split(a)
    return dot(ah, b, dims) + dot(al, b, dims)


def dot_right(a, b, dims=((1,), (0,))):
    bh, bl = split(b)
    return dot(a, bh, dims) + dot(a, bl, dims)


def grid_iota(rows, cols):
    return (
        lax.broadcasted_iota(jnp.int32, (rows, cols), 0),
        lax.broadcasted_iota(jnp.int32, (rows, cols), 1),
    )


def to_row(eye, column):
    return jnp.sum(jnp.where(eye, column, 0.0), axis=0, keepdims=True)


def to_column(eye, row):
    return jnp.sum(jnp.where(eye, row, 0.0), axis=1, keepdims=True)


def decay_sums(decay):
    row, col = grid_iota(TOK, TOK)
    ones = jnp.where(row <= col, 1.0, 0.0).astype(BF)
    eye = row == col
    hi = decay.astype(BF).astype(F32)
    rest = decay - hi
    mid = rest.astype(BF).astype(F32)
    low = rest - mid
    parts = jnp.concatenate([hi, mid, low, jnp.zeros((2, TOK), F32)], axis=0)
    sums = dot(parts.astype(BF), ones)
    rows = sums[0:2] + (sums[2:4] + sums[4:6])
    return [(rows[h : h + 1], to_column(eye, rows[h : h + 1])) for h in range(2)]


def unit_scale(source):
    full = source.astype(F32)
    return lax.rsqrt(jnp.sum(full * full, axis=1, keepdims=True) + 1e-06)


def map_kernel(
    place_ref,
    k_far,
    v_far,
    rate_far,
    decay_far,
    weight_far,
    maps_ref,
    solved_ref,
    half_ref,
    k_ref,
    v_ref,
    rate_ref,
    decay_ref,
    sems,
):
    rows = half_ref.shape[0]
    begin = pl.multiple_of(place_ref[2] * rows, rows)
    copies = [
        pltpu.make_async_copy(k_far, k_ref, sems.at[0]),
        pltpu.make_async_copy(decay_far, decay_ref, sems.at[1]),
        pltpu.make_async_copy(rate_far, rate_ref, sems.at[2]),
        pltpu.make_async_copy(v_far, v_ref, sems.at[3]),
        pltpu.make_async_copy(weight_far.at[pl.ds(begin, rows)], half_ref, sems.at[4]),
    ]
    for copy in copies:
        copy.start()
    for copy in copies[:4]:
        copy.wait()
    keys = k_ref[...]
    keys_f = keys.astype(F32)
    values = v_ref[...].astype(F32)
    row, col = grid_iota(TOK, TOK)
    eye = row == col
    strict = row > col
    rate = [to_column(eye, rate_ref[h : h + 1, :]) for h in range(2)]
    gram = dot(keys, keys, ((1,), (1,)))
    scale = unit_scale(keys)
    gram = gram * scale * to_row(eye, scale)
    sum_rows, sums = zip(*decay_sums(decay_ref[...]))
    r_s, c_s = grid_iota(HALF, HALF)
    eye_s = jnp.where(r_s == c_s, 1.0, 0.0).astype(F32)

    lowers, corners = [], []
    for head in range(2):
        fall = jnp.exp(jnp.minimum(sums[head] - sum_rows[head], 0.0))
        low = jnp.where(strict, rate[head] * gram * fall, 0.0)
        lowers += [low[:HALF, :HALF], low[HALF:, HALF:]]
        corners.append(low[HALF:, :HALF])

    small = (r_s // 8) == (c_s // 8)
    first = [jnp.where(small, low, 0.0) for low in lowers]
    first_b = [a.astype(BF) for a in first]
    square = [dot(a, a).astype(BF) for a in first_b]
    fourth = [dot(a, a).astype(BF) for a in square]
    inv = [eye_s - a for a in first]
    inv = [x + dot(x.astype(BF), a) for x, a in zip(inv, square)]
    inv = [x + dot(x.astype(BF), a) for x, a in zip(inv, fourth)]
    size = 8
    while size < HALF:
        off = ((r_s // (2 * size)) == (c_s // (2 * size))) & ((r_s // size) > (c_s // size))
        inv_b = [x.astype(BF) for x in inv]
        part = [jnp.where(off, low, 0.0).astype(BF) for low in lowers]
        part = [dot(a, x).astype(BF) for a, x in zip(part, inv_b)]
        inv = [x - dot(xb, a) for x, xb, a in zip(inv, inv_b, part)]
        size *= 2
    inv_b = [x.astype(BF) for x in inv]
    gap = [
        eye_s - xb.astype(F32) - dot_left(low, xb) for low, xb in zip(lowers, inv_b)
    ]
    inv = [xb.astype(F32) + dot(xb, g.astype(BF)) for xb, g in zip(inv_b, gap)]

    eye_k = jnp.where(r_s == c_s, 1.0, 0.0).astype(F32)
    solved = []
    for head in range(2):
        b = rate[head]
        grow = b * jnp.exp(sums[head]) * scale
        right = jnp.concatenate(
            [grow * keys_f, b * values[:, head * DV : (head + 1) * DV]], axis=1
        )
        top = dot_fine(inv[2 * head], right[:HALF])
        solved.append((top, right[HALF:]))
    for head in range(2):
        top, below = solved[head]
        below = below - dot_fine(corners[head], top)
        below = dot_fine(inv[2 * head + 1], below)
        solved[head] = jnp.concatenate([top, below], axis=0)
    maps = []
    for head in range(2):
        closing = sums[head][TOK - 1 :, :]
        weight = scale * jnp.exp(closing - sums[head])
        moved = dot_right(keys, weight * solved[head], ((0,), (0,)))
        transit = eye_k * jnp.exp(closing) - moved[:, :DK]
        maps.append(jnp.concatenate([transit, moved[:, DK:]], axis=1).astype(BF))
    for place in range(maps_ref.shape[0]):
        maps_ref[place] = maps[place % 2]
    for head in range(2):
        solved_ref[head] = solved[head]
    copies[4].wait()


def read_kernel(
    place_ref, q_ref, k_ref, decay_ref, gate_ref, gain_ref, solved_ref, keep_ref, send_ref
):
    core = place_ref[2]
    queries = q_ref[...]
    keys = k_ref[...]
    row, col = grid_iota(TOK, TOK)
    eye = row == col
    inclusive = row >= col
    unit_q = unit_scale(queries)
    scores = dot(queries, keys, ((1,), (1,))) * unit_q * to_row(eye, unit_scale(keys))
    sums = decay_sums(decay_ref[...])
    read = []
    for head in range(2):
        sum_row, sum_column = sums[head]
        fall = jnp.exp(jnp.minimum(sum_column - sum_row, 0.0))
        weights = jnp.where(inclusive, scores * fall, 0.0)
        both = dot_fine(weights, solved_ref[head])
        outer = jnp.exp(sum_column) * unit_q * queries.astype(F32) - both[:, :DK]
        gate = gate_ref[:, head * DV : (head + 1) * DV].astype(F32)
        gated = gain_ref[...] * (gate / (1.0 + jnp.exp(-gate)))
        read.append((both[:, DK:], outer, gated))
    for i in range(3):
        keep_ref[i] = jnp.where(core == 0, read[0][i], read[1][i])
        send_ref[i] = jnp.where(core == 0, read[1][i], read[0][i]).astype(BF)


def after(later_t, later_h, earlier, fine):
    moved = dot_fine(later_t, earlier) if fine else dot_right(later_t, earlier)
    return jnp.concatenate([moved[:, :DK], moved[:, DK:] + later_h], axis=1)


def row_kernel(place_ref, parts_ref, total_ref, ahead_ref, first_ref):
    x = place_ref[1]

    def pair(i):
        later = parts_ref[2 * i + 1]
        moved = dot(later[:, :DK], parts_ref[2 * i])
        return jnp.concatenate(
            [moved[:, :DK], moved[:, DK:] + later[:, DK:].astype(F32)], axis=1
        )

    pairs = [pair(i) for i in range(4)]
    upto2 = pairs[0]
    upto4 = after(pairs[1][:, :DK], pairs[1][:, DK:], upto2, True)
    last2 = after(pairs[3][:, :DK], pairs[3][:, DK:], pairs[2], True)
    upto6 = after(pairs[2][:, :DK], pairs[2][:, DK:], upto4, True)
    total = after(last2[:, :DK], last2[:, DK:], upto4, True).astype(BF)
    for place in range(4):
        total_ref[place] = total
    row, col = grid_iota(DK, DK + DV)
    none = jnp.where(row == col, 1.0, 0.0).astype(F32)
    ahead_ref[...] = jnp.where(
        x == 0, none, jnp.where(x == 1, upto2, jnp.where(x == 2, upto4, upto6))
    )
    first_ref[...] = parts_ref[2 * x]


def token_of(group, label):
    return 4 * group + (label if group < 2 else 3 - label)


def out_kernel(place_ref, rows_ref, ahead_ref, first_ref, keep_ref, came_ref, out_ref):
    y = place_ref[0]
    core = place_ref[2]

    def onward(later, state):
        return dot_right(later[:, :DK], state) + later[:, DK:].astype(F32)

    one = rows_ref[0][:, DK:].astype(F32)
    two = onward(rows_ref[1], one)
    three = onward(rows_ref[2], two)
    start = jnp.where(
        y == 0, jnp.zeros_like(one), jnp.where(y == 1, one, jnp.where(y == 2, two, three))
    )
    ahead = ahead_ref[...]
    chip = dot_fine(ahead[:, :DK], start) + ahead[:, DK:]
    second = onward(first_ref[...], chip)

    def finish(state, inner, outer, gated):
        reached = inner + dot_left(outer, state.astype(BF))
        mean = jnp.sum(reached * reached, axis=1, keepdims=True) * (1.0 / DV)
        return (reached * lax.rsqrt(mean + 1e-06) * gated).astype(BF)

    own = finish(jnp.where(core == 0, chip, second), keep_ref[0], keep_ref[1], keep_ref[2])
    came = [came_ref[i].astype(F32) for i in range(3)]
    other = finish(jnp.where(core == 0, second, chip), *came)
    shards = (jnp.where(core == 0, own, other), jnp.where(core == 0, other, own))
    for label in range(4):
        for shard in range(2):
            for group in range(4):
                source = 16 * token_of(group, label)
                target = 64 * shard + 16 * group
                out_ref[label, target : target + 16] = shards[shard][source : source + 16]


def project_kernel(place_ref, normed_ref, w0_ref, w1_ref, w2_ref, w3_ref, keep_ref, send_ref):
    core = place_ref[2]
    total = None
    for i, weight_ref in enumerate((w0_ref, w1_ref, w2_ref, w3_ref)):
        term = dot(normed_ref[place_ref[4 + i]], weight_ref[...])
        total = term if total is None else total + term
    keep_ref[...] = jnp.where(core == 0, total[:64], total[64:])
    send_ref[...] = jnp.where(core == 0, total[64:], total[:64]).astype(BF)


def join_kernel(keep_ref, came_ref, out_ref):
    total = (keep_ref[...] + came_ref[...].astype(F32)).astype(BF)
    for group in range(4):
        out_ref[group] = total[16 * group : 16 * (group + 1)]


def sum_kernel(parts_ref, out_ref):
    total = parts_ref[0].astype(F32)
    for group in range(1, 4):
        total = total + parts_ref[group].astype(F32)
    out_ref[...] = total.astype(BF)


def in_vmem():
    return pl.BlockSpec(memory_space=pltpu.VMEM)


def in_hbm():
    return pl.BlockSpec(memory_space=pltpu.HBM)


def call(kernel, outs, *args, scalars=0, flops=10**8, name=None, ins=None, out_specs=None, scratch=(), room=32):
    if ins is None:
        ins = [in_vmem()] * (len(args) - scalars)
    return pl.pallas_call(
        kernel,
        out_shape=outs,
        in_specs=[pl.BlockSpec(memory_space=pltpu.SMEM)] * scalars + ins,
        out_specs=jax.tree.map(lambda _: in_vmem(), outs) if out_specs is None else out_specs,
        scratch_shapes=scratch,
        compiler_params=pltpu.CompilerParams(vmem_limit_bytes=room * 1024 * 1024),
        cost_estimate=pl.CostEstimate(flops=flops, bytes_accessed=10**6, transcendentals=0),
        name=name,
    )(*args)


def shape(dims, kind):
    return jax.ShapeDtypeStruct(dims, kind)


def local(
    queries, key_vectors, value_vectors, output_gate, write_rate, log_decay, norm_gain, out_weight
):
    at = lax.axis_index("ctx")
    along = lax.axis_index("tp")
    near = along % 4
    label = [jnp.where(along < 8, near ^ i, 3 - (near ^ i)) for i in range(4)]
    place = jnp.stack([at // 8, (at // 2) % 4, at % 2, along] + label).astype(jnp.int32)
    width = out_weight.shape[1]
    rate, decay = write_rate.T, log_decay.T

    maps, solved, w0 = call(
        map_kernel,
        (
            shape((8, DK, DK + DV), BF),
            shape((2, TOK, DK + DV), F32),
            shape((DV, width), BF),
        ),
        place,
        key_vectors,
        value_vectors,
        rate,
        decay,
        out_weight,
        scalars=1,
        ins=[in_hbm()] * 5,
        out_specs=(in_vmem(), in_vmem(), in_hbm()),
        scratch=[
            pltpu.VMEM((TOK, DK), BF),
            pltpu.VMEM((TOK, 2 * DV), BF),
            pltpu.VMEM((2, TOK), F32),
            pltpu.VMEM((2, TOK), F32),
            pltpu.SemaphoreType.DMA((5,)),
        ],
        flops=10**9,
        room=60,
        name="shard_maps",
    )
    lines = [[8 * y + i for i in range(8)] for y in range(4)]
    parts = lax.all_to_all(maps, "ctx", 0, 0, axis_index_groups=lines)
    keep, send = call(
        read_kernel,
        (shape((3, TOK, DV), F32), shape((3, TOK, DV), BF)),
        place,
        queries,
        key_vectors,
        decay,
        output_gate,
        norm_gain.reshape(1, DV),
        solved,
        scalars=1,
        flops=10**9,
        name="read_parts",
    )
    across = [(i, i ^ 1) for i in range(32)]
    came = lax.ppermute(send, "ctx", across)

    w1 = lax.ppermute(w0, "tp", [(j, j ^ 1) for j in range(16)])
    w2 = lax.ppermute(w0, "tp", [(j, j ^ 2) for j in range(16)])
    w3 = lax.ppermute(w2, "tp", [(j, j ^ 1) for j in range(16)])

    total, ahead, first = call(
        row_kernel,
        (shape((4, DK, DK + DV), BF), shape((DK, DK + DV), F32), shape((DK, DK + DV), BF)),
        place,
        parts,
        scalars=1,
        name="row_maps",
    )
    columns = [[8 * y + i for y in range(4)] for i in range(8)]
    rows = lax.all_to_all(total, "ctx", 0, 0, axis_index_groups=columns)
    normed = call(
        out_kernel,
        shape((4, 128, DV), BF),
        place,
        rows,
        ahead,
        first,
        keep,
        came,
        scalars=1,
        name="gated_norm",
    )
    close = [[token_of(g, m) for m in range(4)] for g in range(4)]
    gathered = lax.all_to_all(normed, "tp", 0, 0, axis_index_groups=close)
    half, other_half = call(
        project_kernel,
        (shape((64, width), F32), shape((64, width), BF)),
        place,
        gathered,
        w0,
        w1,
        w2,
        w3,
        scalars=1,
        name="project",
    )
    other_half = lax.ppermute(other_half, "ctx", across)
    partial = call(join_kernel, shape((4, 16, width), BF), half, other_half, name="join")
    far = [[token_of(g, m) for g in range(4)] for m in range(4)]
    shares = lax.all_to_all(partial, "tp", 0, 0, axis_index_groups=far)
    return call(sum_kernel, shape((16, width), BF), shares, name="sum_shares")


def solution(mesh):
    placed = (
        P("ctx", "tp"),
        P("ctx", "tp"),
        P("ctx", "tp"),
        P("ctx", "tp"),
        P("ctx", "tp"),
        P("ctx", "tp"),
        P(),
        P("tp", None),
    )
    return jax.shard_map(
        local, mesh=mesh, in_specs=placed, out_specs=P(("ctx", "tp"), None), check_vma=False
    )
```

```python
import jax
import jax.numpy as jnp
from jax import lax
from jax.experimental import pallas as pl
from jax.experimental.pallas import tpu as pltpu
from jax.sharding import PartitionSpec as P

F32 = jnp.float32
BF = jnp.bfloat16
TOK = 256
DK = 128
DV = 128
HALF = 128


def dot(a, b, dims=((1,), (0,))):
    return lax.dot_general(a, b, (dims, ((), ())), preferred_element_type=F32)


def split(a):
    hi = a.astype(BF)
    return hi, (a - hi.astype(F32)).astype(BF)


def dot_fine(a, b, dims=((1,), (0,))):
    ah, al = split(a)
    bh, bl = split(b)
    return dot(ah, bh, dims) + (dot(ah, bl, dims) + dot(al, bh, dims))


def dot_left(a, b, dims=((1,), (0,))):
    ah, al = split(a)
    return dot(ah, b, dims) + dot(al, b, dims)


def dot_right(a, b, dims=((1,), (0,))):
    bh, bl = split(b)
    return dot(a, bh, dims) + dot(a, bl, dims)


def grid_iota(rows, cols):
    return (
        lax.broadcasted_iota(jnp.int32, (rows, cols), 0),
        lax.broadcasted_iota(jnp.int32, (rows, cols), 1),
    )


def to_row(eye, column):
    return jnp.sum(jnp.where(eye, column, 0.0), axis=0, keepdims=True)


def to_column(eye, row):
    return jnp.sum(jnp.where(eye, row, 0.0), axis=1, keepdims=True)


def decay_sums(decay):
    row, col = grid_iota(TOK, TOK)
    ones = jnp.where(row <= col, 1.0, 0.0).astype(BF)
    eye = row == col
    hi = decay.astype(BF).astype(F32)
    rest = decay - hi
    mid = rest.astype(BF).astype(F32)
    low = rest - mid
    parts = jnp.concatenate([hi, mid, low, jnp.zeros((2, TOK), F32)], axis=0)
    sums = dot(parts.astype(BF), ones)
    rows = sums[0:2] + (sums[2:4] + sums[4:6])
    return [(rows[h : h + 1], to_column(eye, rows[h : h + 1])) for h in range(2)]


def unit_scale(source):
    full = source.astype(F32)
    return lax.rsqrt(jnp.sum(full * full, axis=1, keepdims=True) + 1e-06)


def map_kernel(
    k_far,
    v_far,
    rate_far,
    decay_far,
    weight_far,
    maps_ref,
    solved_ref,
    half_ref,
    k_ref,
    v_ref,
    rate_ref,
    decay_ref,
    sems,
):
    rows = half_ref.shape[0]
    begin = pl.multiple_of(places()[2] * rows, rows)
    copies = [
        pltpu.make_async_copy(k_far, k_ref, sems.at[0]),
        pltpu.make_async_copy(decay_far, decay_ref, sems.at[1]),
        pltpu.make_async_copy(rate_far, rate_ref, sems.at[2]),
        pltpu.make_async_copy(v_far, v_ref, sems.at[3]),
        pltpu.make_async_copy(weight_far.at[pl.ds(begin, rows)], half_ref, sems.at[4]),
    ]
    for copy in copies:
        copy.start()
    for copy in copies[:4]:
        copy.wait()
    keys = k_ref[...]
    keys_f = keys.astype(F32)
    values = v_ref[...].astype(F32)
    row, col = grid_iota(TOK, TOK)
    eye = row == col
    strict = row > col
    rate = [to_column(eye, rate_ref[h : h + 1, :]) for h in range(2)]
    gram = dot(keys, keys, ((1,), (1,)))
    scale = unit_scale(keys)
    gram = gram * scale * to_row(eye, scale)
    sum_rows, sums = zip(*decay_sums(decay_ref[...]))
    r_s, c_s = grid_iota(HALF, HALF)
    eye_s = jnp.where(r_s == c_s, 1.0, 0.0).astype(F32)

    lowers, corners = [], []
    for head in range(2):
        fall = jnp.exp(jnp.minimum(sums[head] - sum_rows[head], 0.0))
        low = jnp.where(strict, rate[head] * gram * fall, 0.0)
        lowers += [low[:HALF, :HALF], low[HALF:, HALF:]]
        corners.append(low[HALF:, :HALF])

    small = (r_s // 8) == (c_s // 8)
    first = [jnp.where(small, low, 0.0) for low in lowers]
    first_b = [a.astype(BF) for a in first]
    square = [dot(a, a).astype(BF) for a in first_b]
    fourth = [dot(a, a).astype(BF) for a in square]
    inv = [eye_s - a for a in first]
    inv = [x + dot(x.astype(BF), a) for x, a in zip(inv, square)]
    inv = [x + dot(x.astype(BF), a) for x, a in zip(inv, fourth)]
    size = 8
    while size < HALF:
        off = ((r_s // (2 * size)) == (c_s // (2 * size))) & ((r_s // size) > (c_s // size))
        inv_b = [x.astype(BF) for x in inv]
        part = [jnp.where(off, low, 0.0).astype(BF) for low in lowers]
        part = [dot(a, x).astype(BF) for a, x in zip(part, inv_b)]
        inv = [x - dot(xb, a) for x, xb, a in zip(inv, inv_b, part)]
        size *= 2
    inv_b = [x.astype(BF) for x in inv]
    gap = [
        eye_s - xb.astype(F32) - dot_left(low, xb) for low, xb in zip(lowers, inv_b)
    ]
    inv = [xb.astype(F32) + dot(xb, g.astype(BF)) for xb, g in zip(inv_b, gap)]

    eye_k = jnp.where(r_s == c_s, 1.0, 0.0).astype(F32)
    solved = []
    for head in range(2):
        b = rate[head]
        grow = b * jnp.exp(sums[head]) * scale
        right = jnp.concatenate(
            [grow * keys_f, b * values[:, head * DV : (head + 1) * DV]], axis=1
        )
        top = dot_fine(inv[2 * head], right[:HALF])
        solved.append((top, right[HALF:]))
    for head in range(2):
        top, below = solved[head]
        below = below - dot_fine(corners[head], top)
        below = dot_fine(inv[2 * head + 1], below)
        solved[head] = jnp.concatenate([top, below], axis=0)
    maps = []
    for head in range(2):
        closing = sums[head][TOK - 1 :, :]
        weight = scale * jnp.exp(closing - sums[head])
        moved = dot_right(keys, weight * solved[head], ((0,), (0,)))
        transit = eye_k * jnp.exp(closing) - moved[:, :DK]
        maps.append(jnp.concatenate([transit, moved[:, DK:]], axis=1).astype(BF))
    for place in range(maps_ref.shape[0]):
        maps_ref[place] = maps[place % 2]
    for head in range(2):
        solved_ref[head] = solved[head]
    copies[4].wait()


def read_kernel(
    q_ref, k_ref, decay_ref, gate_ref, gain_ref, solved_ref, keep_ref, send_ref
):
    core = places()[2]
    queries = q_ref[...]
    keys = k_ref[...]
    row, col = grid_iota(TOK, TOK)
    eye = row == col
    inclusive = row >= col
    unit_q = unit_scale(queries)
    scores = dot(queries, keys, ((1,), (1,))) * unit_q * to_row(eye, unit_scale(keys))
    sums = decay_sums(decay_ref[...])
    read = []
    for head in range(2):
        sum_row, sum_column = sums[head]
        fall = jnp.exp(jnp.minimum(sum_column - sum_row, 0.0))
        weights = jnp.where(inclusive, scores * fall, 0.0)
        both = dot_fine(weights, solved_ref[head])
        outer = jnp.exp(sum_column) * unit_q * queries.astype(F32) - both[:, :DK]
        gate = gate_ref[:, head * DV : (head + 1) * DV].astype(F32)
        gated = gain_ref[...] * (gate / (1.0 + jnp.exp(-gate)))
        read.append((both[:, DK:], outer, gated))
    for i in range(3):
        keep_ref[i] = jnp.where(core == 0, read[0][i], read[1][i])
        send_ref[i] = jnp.where(core == 0, read[1][i], read[0][i]).astype(BF)


def after(later_t, later_h, earlier, fine):
    moved = dot_fine(later_t, earlier) if fine else dot_right(later_t, earlier)
    return jnp.concatenate([moved[:, :DK], moved[:, DK:] + later_h], axis=1)


def row_kernel(parts_ref, total_ref, ahead_ref, first_ref):
    x = places()[1]

    def pair(i):
        later = parts_ref[2 * i + 1]
        moved = dot(later[:, :DK], parts_ref[2 * i])
        return jnp.concatenate(
            [moved[:, :DK], moved[:, DK:] + later[:, DK:].astype(F32)], axis=1
        )

    pairs = [pair(i) for i in range(4)]
    upto2 = pairs[0]
    upto4 = after(pairs[1][:, :DK], pairs[1][:, DK:], upto2, True)
    last2 = after(pairs[3][:, :DK], pairs[3][:, DK:], pairs[2], True)
    upto6 = after(pairs[2][:, :DK], pairs[2][:, DK:], upto4, True)
    total = after(last2[:, :DK], last2[:, DK:], upto4, True).astype(BF)
    for place in range(4):
        total_ref[place] = total
    row, col = grid_iota(DK, DK + DV)
    none = jnp.where(row == col, 1.0, 0.0).astype(F32)
    ahead_ref[...] = jnp.where(
        x == 0, none, jnp.where(x == 1, upto2, jnp.where(x == 2, upto4, upto6))
    )
    first_ref[...] = parts_ref[2 * x]


def token_of(group, label):
    return 4 * group + (label if group < 2 else 3 - label)


def out_kernel(rows_ref, ahead_ref, first_ref, keep_ref, came_ref, out_ref):
    y, _, core = places()

    def onward(later, state):
        return dot_right(later[:, :DK], state) + later[:, DK:].astype(F32)

    one = rows_ref[0][:, DK:].astype(F32)
    two = onward(rows_ref[1], one)
    three = onward(rows_ref[2], two)
    start = jnp.where(
        y == 0, jnp.zeros_like(one), jnp.where(y == 1, one, jnp.where(y == 2, two, three))
    )
    ahead = ahead_ref[...]
    chip = dot_fine(ahead[:, :DK], start) + ahead[:, DK:]
    second = onward(first_ref[...], chip)

    def finish(state, inner, outer, gated):
        reached = inner + dot_left(outer, state.astype(BF))
        mean = jnp.sum(reached * reached, axis=1, keepdims=True) * (1.0 / DV)
        return (reached * lax.rsqrt(mean + 1e-06) * gated).astype(BF)

    own = finish(jnp.where(core == 0, chip, second), keep_ref[0], keep_ref[1], keep_ref[2])
    came = [came_ref[i].astype(F32) for i in range(3)]
    other = finish(jnp.where(core == 0, second, chip), *came)
    shards = (jnp.where(core == 0, own, other), jnp.where(core == 0, other, own))
    for label in range(4):
        for shard in range(2):
            for group in range(4):
                source = 16 * token_of(group, label)
                target = 64 * shard + 16 * group
                out_ref[label, target : target + 16] = shards[shard][source : source + 16]


def project_kernel(normed_ref, w0_ref, w1_ref, w2_ref, w3_ref, keep_ref, send_ref):
    core = places()[2]
    along = lax.axis_index("tp")
    total = None
    for i, weight_ref in enumerate((w0_ref, w1_ref, w2_ref, w3_ref)):
        near = (along % 4) ^ i
        term = dot(normed_ref[jnp.where(along < 8, near, 3 - near)], weight_ref[...])
        total = term if total is None else total + term
    keep_ref[...] = jnp.where(core == 0, total[:64], total[64:])
    send_ref[...] = jnp.where(core == 0, total[64:], total[:64]).astype(BF)


def join_kernel(keep_ref, came_ref, out_ref):
    total = (keep_ref[...] + came_ref[...].astype(F32)).astype(BF)
    for group in range(4):
        out_ref[group] = total[16 * group : 16 * (group + 1)]


def sum_kernel(parts_ref, out_ref):
    total = parts_ref[0].astype(F32)
    for group in range(1, 4):
        total = total + parts_ref[group].astype(F32)
    out_ref[...] = total.astype(BF)


def places():
    at = lax.axis_index("ctx")
    return at // 8, (at // 2) % 4, at % 2


def in_vmem():
    return pl.BlockSpec(memory_space=pltpu.VMEM)


def in_hbm():
    return pl.BlockSpec(memory_space=pltpu.HBM)


def call(kernel, outs, *args, flops=10**8, name=None, ins=None, out_specs=None, scratch=(), room=32):
    if ins is None:
        ins = [in_vmem()] * len(args)
    return pl.pallas_call(
        kernel,
        out_shape=outs,
        in_specs=ins,
        out_specs=jax.tree.map(lambda _: in_vmem(), outs) if out_specs is None else out_specs,
        scratch_shapes=scratch,
        compiler_params=pltpu.CompilerParams(vmem_limit_bytes=room * 1024 * 1024),
        cost_estimate=pl.CostEstimate(flops=flops, bytes_accessed=10**6, transcendentals=0),
        name=name,
    )(*args)


def shape(dims, kind):
    return jax.ShapeDtypeStruct(dims, kind)


def local(
    queries, key_vectors, value_vectors, output_gate, write_rate, log_decay, norm_gain, out_weight
):
    width = out_weight.shape[1]
    rate, decay = write_rate.T, log_decay.T

    maps, solved, w0 = call(
        map_kernel,
        (
            shape((8, DK, DK + DV), BF),
            shape((2, TOK, DK + DV), F32),
            shape((DV, width), BF),
        ),
        key_vectors,
        value_vectors,
        rate,
        decay,
        out_weight,
        ins=[in_hbm()] * 5,
        out_specs=(in_vmem(), in_vmem(), in_vmem()),
        scratch=[
            pltpu.VMEM((TOK, DK), BF),
            pltpu.VMEM((TOK, 2 * DV), BF),
            pltpu.VMEM((2, TOK), F32),
            pltpu.VMEM((2, TOK), F32),
            pltpu.SemaphoreType.DMA((5,)),
        ],
        flops=10**9,
        room=60,
        name="shard_maps",
    )
    lines = [[8 * y + i for i in range(8)] for y in range(4)]
    parts = lax.all_to_all(maps, "ctx", 0, 0, axis_index_groups=lines)
    keep, send = call(
        read_kernel,
        (shape((3, TOK, DV), F32), shape((3, TOK, DV), BF)),
        queries,
        key_vectors,
        decay,
        output_gate,
        norm_gain.reshape(1, DV),
        solved,
        flops=10**9,
        name="read_parts",
    )
    across = [(i, i ^ 1) for i in range(32)]
    came = lax.ppermute(send, "ctx", across)

    w1 = lax.ppermute(w0, "tp", [(j, j ^ 1) for j in range(16)])
    w2 = lax.ppermute(w0, "tp", [(j, j ^ 2) for j in range(16)])
    w1, w2 = lax.optimization_barrier((w1, w2))
    w3 = lax.ppermute(w2, "tp", [(j, j ^ 1) for j in range(16)])

    total, ahead, first = call(
        row_kernel,
        (shape((4, DK, DK + DV), BF), shape((DK, DK + DV), F32), shape((DK, DK + DV), BF)),
        parts,
        name="row_maps",
    )
    columns = [[8 * y + i for y in range(4)] for i in range(8)]
    rows = lax.all_to_all(total, "ctx", 0, 0, axis_index_groups=columns)
    normed = call(
        out_kernel,
        shape((4, 128, DV), BF),
        rows,
        ahead,
        first,
        keep,
        came,
        name="gated_norm",
    )
    close = [[token_of(g, m) for m in range(4)] for g in range(4)]
    gathered = lax.all_to_all(normed, "tp", 0, 0, axis_index_groups=close)
    half, other_half = call(
        project_kernel,
        (shape((64, width), F32), shape((64, width), BF)),
        gathered,
        w0,
        w1,
        w2,
        w3,
        name="project",
    )
    other_half = lax.ppermute(other_half, "ctx", across)
    partial = call(join_kernel, shape((4, 16, width), BF), half, other_half, name="join")
    far = [[token_of(g, m) for g in range(4)] for m in range(4)]
    shares = lax.all_to_all(partial, "tp", 0, 0, axis_index_groups=far)
    return call(sum_kernel, shape((16, width), BF), shares, name="sum_shares")


def solution(mesh):
    placed = (
        P("ctx", "tp"),
        P("ctx", "tp"),
        P("ctx", "tp"),
        P("ctx", "tp"),
        P("ctx", "tp"),
        P("ctx", "tp"),
        P(),
        P("tp", None),
    )
    return jax.shard_map(
        local, mesh=mesh, in_specs=placed, out_specs=P(("ctx", "tp"), None), check_vma=False
    )
```

```python
import jax
import jax.numpy as jnp
from jax import lax
from jax.experimental import pallas as pl
from jax.experimental.pallas import tpu as pltpu
from jax.sharding import PartitionSpec as P

F32 = jnp.float32
BF = jnp.bfloat16
TOK = 256
DK = 128
DV = 128
HALF = 128


def dot(a, b, dims=((1,), (0,))):
    return lax.dot_general(a, b, (dims, ((), ())), preferred_element_type=F32)


def split(a):
    hi = a.astype(BF)
    return hi, (a - hi.astype(F32)).astype(BF)


def dot_fine(a, b, dims=((1,), (0,))):
    ah, al = split(a)
    bh, bl = split(b)
    return dot(ah, bh, dims) + (dot(ah, bl, dims) + dot(al, bh, dims))


def dot_left(a, b, dims=((1,), (0,))):
    ah, al = split(a)
    return dot(ah, b, dims) + dot(al, b, dims)


def dot_right(a, b, dims=((1,), (0,))):
    bh, bl = split(b)
    return dot(a, bh, dims) + dot(a, bl, dims)


def grid_iota(rows, cols):
    return (
        lax.broadcasted_iota(jnp.int32, (rows, cols), 0),
        lax.broadcasted_iota(jnp.int32, (rows, cols), 1),
    )


def to_row(eye, column):
    return jnp.sum(jnp.where(eye, column, 0.0), axis=0, keepdims=True)


def to_column(eye, row):
    return jnp.sum(jnp.where(eye, row, 0.0), axis=1, keepdims=True)


def decay_sums(decay):
    row, col = grid_iota(TOK, TOK)
    ones = jnp.where(row <= col, 1.0, 0.0).astype(BF)
    eye = row == col
    hi = decay.astype(BF).astype(F32)
    rest = decay - hi
    mid = rest.astype(BF).astype(F32)
    low = rest - mid
    parts = jnp.concatenate([hi, mid, low, jnp.zeros((2, TOK), F32)], axis=0)
    sums = dot(parts.astype(BF), ones)
    rows = sums[0:2] + (sums[2:4] + sums[4:6])
    return [(rows[h : h + 1], to_column(eye, rows[h : h + 1])) for h in range(2)]


def unit_scale(source):
    full = source.astype(F32)
    return lax.rsqrt(jnp.sum(full * full, axis=1, keepdims=True) + 1e-06)


def map_kernel(
    k_far,
    v_far,
    rate_far,
    decay_far,
    weight_far,
    maps_ref,
    solved_ref,
    half_ref,
    k_ref,
    v_ref,
    rate_ref,
    decay_ref,
    sems,
):
    rows = half_ref.shape[0]
    begin = pl.multiple_of(places()[2] * rows, rows)
    copies = [
        pltpu.make_async_copy(k_far, k_ref, sems.at[0]),
        pltpu.make_async_copy(decay_far, decay_ref, sems.at[1]),
        pltpu.make_async_copy(rate_far, rate_ref, sems.at[2]),
        pltpu.make_async_copy(v_far, v_ref, sems.at[3]),
        pltpu.make_async_copy(weight_far.at[pl.ds(begin, rows)], half_ref, sems.at[4]),
    ]
    for copy in copies:
        copy.start()
    for copy in copies[:4]:
        copy.wait()
    keys = k_ref[...]
    keys_f = keys.astype(F32)
    values = v_ref[...].astype(F32)
    row, col = grid_iota(TOK, TOK)
    eye = row == col
    strict = row > col
    rate = [to_column(eye, rate_ref[h : h + 1, :]) for h in range(2)]
    gram = dot(keys, keys, ((1,), (1,)))
    scale = unit_scale(keys)
    gram = gram * scale * to_row(eye, scale)
    sum_rows, sums = zip(*decay_sums(decay_ref[...]))
    r_s, c_s = grid_iota(HALF, HALF)
    eye_s = jnp.where(r_s == c_s, 1.0, 0.0).astype(F32)

    lowers, corners = [], []
    for head in range(2):
        fall = jnp.exp(jnp.minimum(sums[head] - sum_rows[head], 0.0))
        low = jnp.where(strict, rate[head] * gram * fall, 0.0)
        lowers += [low[:HALF, :HALF], low[HALF:, HALF:]]
        corners.append(low[HALF:, :HALF])

    small = (r_s // 8) == (c_s // 8)
    first = [jnp.where(small, low, 0.0) for low in lowers]
    first_b = [a.astype(BF) for a in first]
    square = [dot(a, a).astype(BF) for a in first_b]
    fourth = [dot(a, a).astype(BF) for a in square]
    inv = [eye_s - a for a in first]
    inv = [x + dot(x.astype(BF), a) for x, a in zip(inv, square)]
    inv = [x + dot(x.astype(BF), a) for x, a in zip(inv, fourth)]
    size = 8
    while size < HALF:
        off = ((r_s // (2 * size)) == (c_s // (2 * size))) & ((r_s // size) > (c_s // size))
        inv_b = [x.astype(BF) for x in inv]
        part = [jnp.where(off, low, 0.0).astype(BF) for low in lowers]
        part = [dot(a, x).astype(BF) for a, x in zip(part, inv_b)]
        inv = [x - dot(xb, a) for x, xb, a in zip(inv, inv_b, part)]
        size *= 2
    inv_b = [x.astype(BF) for x in inv]
    gap = [
        eye_s - xb.astype(F32) - dot_left(low, xb) for low, xb in zip(lowers, inv_b)
    ]
    inv = [xb.astype(F32) + dot(xb, g.astype(BF)) for xb, g in zip(inv_b, gap)]

    eye_k = jnp.where(r_s == c_s, 1.0, 0.0).astype(F32)
    solved = []
    for head in range(2):
        b = rate[head]
        grow = b * jnp.exp(sums[head]) * scale
        right = jnp.concatenate(
            [grow * keys_f, b * values[:, head * DV : (head + 1) * DV]], axis=1
        )
        top = dot_fine(inv[2 * head], right[:HALF])
        solved.append((top, right[HALF:]))
    for head in range(2):
        top, below = solved[head]
        below = below - dot_fine(corners[head], top)
        below = dot_fine(inv[2 * head + 1], below)
        solved[head] = jnp.concatenate([top, below], axis=0)
    maps = []
    for head in range(2):
        closing = sums[head][TOK - 1 :, :]
        weight = scale * jnp.exp(closing - sums[head])
        moved = dot_right(keys, weight * solved[head], ((0,), (0,)))
        transit = eye_k * jnp.exp(closing) - moved[:, :DK]
        maps.append(jnp.concatenate([transit, moved[:, DK:]], axis=1).astype(BF))
    for place in range(maps_ref.shape[0]):
        maps_ref[place] = maps[place % 2]
    for head in range(2):
        solved_ref[head] = solved[head]
    copies[4].wait()


def read_kernel(
    q_ref, k_ref, decay_ref, gate_ref, gain_ref, solved_ref, keep_ref, send_ref
):
    core = places()[2]
    queries = q_ref[...]
    keys = k_ref[...]
    row, col = grid_iota(TOK, TOK)
    eye = row == col
    inclusive = row >= col
    unit_q = unit_scale(queries)
    scores = dot(queries, keys, ((1,), (1,))) * unit_q * to_row(eye, unit_scale(keys))
    sums = decay_sums(decay_ref[...])
    read = []
    for head in range(2):
        sum_row, sum_column = sums[head]
        fall = jnp.exp(jnp.minimum(sum_column - sum_row, 0.0))
        weights = jnp.where(inclusive, scores * fall, 0.0)
        both = dot_fine(weights, solved_ref[head])
        outer = jnp.exp(sum_column) * unit_q * queries.astype(F32) - both[:, :DK]
        gate = gate_ref[:, head * DV : (head + 1) * DV].astype(F32)
        gated = gain_ref[...] * (gate / (1.0 + jnp.exp(-gate)))
        read.append((both[:, DK:], outer, gated))
    for i in range(3):
        keep_ref[i] = jnp.where(core == 0, read[0][i], read[1][i])
        send_ref[i] = jnp.where(core == 0, read[1][i], read[0][i]).astype(BF)


def after(later_t, later_h, earlier, fine):
    moved = dot_fine(later_t, earlier) if fine else dot_right(later_t, earlier)
    return jnp.concatenate([moved[:, :DK], moved[:, DK:] + later_h], axis=1)


def row_kernel(parts_ref, total_ref, ahead_ref, first_ref):
    x = places()[1]

    def pair(i):
        later = parts_ref[2 * i + 1]
        moved = dot(later[:, :DK], parts_ref[2 * i])
        return jnp.concatenate(
            [moved[:, :DK], moved[:, DK:] + later[:, DK:].astype(F32)], axis=1
        )

    pairs = [pair(i) for i in range(4)]
    upto2 = pairs[0]
    upto4 = after(pairs[1][:, :DK], pairs[1][:, DK:], upto2, True)
    last2 = after(pairs[3][:, :DK], pairs[3][:, DK:], pairs[2], True)
    upto6 = after(pairs[2][:, :DK], pairs[2][:, DK:], upto4, True)
    total = after(last2[:, :DK], last2[:, DK:], upto4, True).astype(BF)
    for place in range(4):
        total_ref[place] = total
    row, col = grid_iota(DK, DK + DV)
    none = jnp.where(row == col, 1.0, 0.0).astype(F32)
    ahead_ref[...] = jnp.where(
        x == 0, none, jnp.where(x == 1, upto2, jnp.where(x == 2, upto4, upto6))
    )
    first_ref[...] = parts_ref[2 * x]


def token_of(group, label):
    return 4 * group + (label if group < 2 else 3 - label)


def out_kernel(rows_ref, ahead_ref, first_ref, keep_ref, came_ref, out_ref):
    y, _, core = places()

    def onward(later, state):
        return dot_right(later[:, :DK], state) + later[:, DK:].astype(F32)

    one = rows_ref[0][:, DK:].astype(F32)
    two = onward(rows_ref[1], one)
    three = onward(rows_ref[2], two)
    start = jnp.where(
        y == 0, jnp.zeros_like(one), jnp.where(y == 1, one, jnp.where(y == 2, two, three))
    )
    ahead = ahead_ref[...]
    chip = dot_fine(ahead[:, :DK], start) + ahead[:, DK:]
    second = onward(first_ref[...], chip)

    def finish(state, inner, outer, gated):
        reached = inner + dot_left(outer, state.astype(BF))
        mean = jnp.sum(reached * reached, axis=1, keepdims=True) * (1.0 / DV)
        return (reached * lax.rsqrt(mean + 1e-06) * gated).astype(BF)

    own = finish(jnp.where(core == 0, chip, second), keep_ref[0], keep_ref[1], keep_ref[2])
    came = [came_ref[i].astype(F32) for i in range(3)]
    other = finish(jnp.where(core == 0, second, chip), *came)
    shards = (jnp.where(core == 0, own, other), jnp.where(core == 0, other, own))
    for label in range(4):
        for shard in range(2):
            for group in range(4):
                source = 16 * token_of(group, label)
                target = 64 * shard + 16 * group
                out_ref[label, target : target + 16] = shards[shard][source : source + 16]


def project_kernel(normed_ref, w0_ref, w1_ref, w2_ref, w3_ref, keep_ref, send_ref):
    core = places()[2]
    along = lax.axis_index("tp")
    total = None
    for i, weight_ref in enumerate((w0_ref, w1_ref, w2_ref, w3_ref)):
        near = (along % 4) ^ i
        term = dot(normed_ref[jnp.where(along < 8, near, 3 - near)], weight_ref[...])
        total = term if total is None else total + term
    keep_ref[...] = jnp.where(core == 0, total[:64], total[64:])
    send_ref[...] = jnp.where(core == 0, total[64:], total[:64]).astype(BF)


def join_kernel(keep_ref, came_ref, out_ref):
    total = (keep_ref[...] + came_ref[...].astype(F32)).astype(BF)
    for group in range(4):
        out_ref[group] = total[16 * group : 16 * (group + 1)]


def sum_kernel(parts_ref, out_ref):
    total = parts_ref[0].astype(F32)
    for group in range(1, 4):
        total = total + parts_ref[group].astype(F32)
    out_ref[...] = total.astype(BF)


def places():
    at = lax.axis_index("ctx")
    return at // 8, (at // 2) % 4, at % 2


def in_vmem():
    return pl.BlockSpec(memory_space=pltpu.VMEM)


def in_hbm():
    return pl.BlockSpec(memory_space=pltpu.HBM)


def call(kernel, outs, *args, flops=10**8, name=None, ins=None, out_specs=None, scratch=(), room=32):
    if ins is None:
        ins = [in_vmem()] * len(args)
    return pl.pallas_call(
        kernel,
        out_shape=outs,
        in_specs=ins,
        out_specs=jax.tree.map(lambda _: in_vmem(), outs) if out_specs is None else out_specs,
        scratch_shapes=scratch,
        compiler_params=pltpu.CompilerParams(vmem_limit_bytes=room * 1024 * 1024),
        cost_estimate=pl.CostEstimate(flops=flops, bytes_accessed=10**6, transcendentals=0),
        name=name,
    )(*args)


def shape(dims, kind):
    return jax.ShapeDtypeStruct(dims, kind)


def local(
    queries, key_vectors, value_vectors, output_gate, write_rate, log_decay, norm_gain, out_weight
):
    width = out_weight.shape[1]
    rate, decay = write_rate.T, log_decay.T

    maps, solved, w0 = call(
        map_kernel,
        (
            shape((8, DK, DK + DV), BF),
            shape((2, TOK, DK + DV), F32),
            shape((DV, width), BF),
        ),
        key_vectors,
        value_vectors,
        rate,
        decay,
        out_weight,
        ins=[in_hbm()] * 5,
        out_specs=(in_vmem(), in_vmem(), in_vmem()),
        scratch=[
            pltpu.VMEM((TOK, DK), BF),
            pltpu.VMEM((TOK, 2 * DV), BF),
            pltpu.VMEM((2, TOK), F32),
            pltpu.VMEM((2, TOK), F32),
            pltpu.SemaphoreType.DMA((5,)),
        ],
        flops=10**9,
        room=60,
        name="shard_maps",
    )
    lines = [[8 * y + i for i in range(8)] for y in range(4)]
    parts = lax.all_to_all(maps, "ctx", 0, 0, axis_index_groups=lines)
    keep, send = call(
        read_kernel,
        (shape((3, TOK, DV), F32), shape((3, TOK, DV), BF)),
        queries,
        key_vectors,
        decay,
        output_gate,
        norm_gain.reshape(1, DV),
        solved,
        flops=10**9,
        name="read_parts",
    )
    across = [(i, i ^ 1) for i in range(32)]
    came = lax.ppermute(send, "ctx", across)

    w1 = lax.ppermute(w0, "tp", [(j, j ^ 1) for j in range(16)])
    w2 = lax.ppermute(w0, "tp", [(j, j ^ 2) for j in range(16)])

    total, ahead, first = call(
        row_kernel,
        (shape((4, DK, DK + DV), BF), shape((DK, DK + DV), F32), shape((DK, DK + DV), BF)),
        parts,
        name="row_maps",
    )
    columns = [[8 * y + i for y in range(4)] for i in range(8)]
    rows = lax.all_to_all(total, "ctx", 0, 0, axis_index_groups=columns)
    normed = call(
        out_kernel,
        shape((4, 128, DV), BF),
        rows,
        ahead,
        first,
        keep,
        came,
        name="gated_norm",
    )
    w2, normed = lax.optimization_barrier((w2, normed))
    w3 = lax.ppermute(w2, "tp", [(j, j ^ 1) for j in range(16)])
    close = [[token_of(g, m) for m in range(4)] for g in range(4)]
    gathered = lax.all_to_all(normed, "tp", 0, 0, axis_index_groups=close)
    half, other_half = call(
        project_kernel,
        (shape((64, width), F32), shape((64, width), BF)),
        gathered,
        w0,
        w1,
        w2,
        w3,
        name="project",
    )
    other_half = lax.ppermute(other_half, "ctx", across)
    partial = call(join_kernel, shape((4, 16, width), BF), half, other_half, name="join")
    far = [[token_of(g, m) for g in range(4)] for m in range(4)]
    shares = lax.all_to_all(partial, "tp", 0, 0, axis_index_groups=far)
    return call(sum_kernel, shape((16, width), BF), shares, name="sum_shares")


def solution(mesh):
    placed = (
        P("ctx", "tp"),
        P("ctx", "tp"),
        P("ctx", "tp"),
        P("ctx", "tp"),
        P("ctx", "tp"),
        P("ctx", "tp"),
        P(),
        P("tp", None),
    )
    return jax.shard_map(
        local, mesh=mesh, in_specs=placed, out_specs=P(("ctx", "tp"), None), check_vma=False
    )
```

```python
import jax
import jax.numpy as jnp
from jax import lax
from jax.experimental import pallas as pl
from jax.experimental.pallas import tpu as pltpu
from jax.sharding import PartitionSpec as P

F32 = jnp.float32
BF = jnp.bfloat16
TOK = 256
DK = 128
DV = 128
HALF = 128


def dot(a, b, dims=((1,), (0,))):
    return lax.dot_general(a, b, (dims, ((), ())), preferred_element_type=F32)


def split(a):
    hi = a.astype(BF)
    return hi, (a - hi.astype(F32)).astype(BF)


def dot_fine(a, b, dims=((1,), (0,))):
    ah, al = split(a)
    bh, bl = split(b)
    return dot(ah, bh, dims) + (dot(ah, bl, dims) + dot(al, bh, dims))


def dot_left(a, b, dims=((1,), (0,))):
    ah, al = split(a)
    return dot(ah, b, dims) + dot(al, b, dims)


def dot_right(a, b, dims=((1,), (0,))):
    bh, bl = split(b)
    return dot(a, bh, dims) + dot(a, bl, dims)


def grid_iota(rows, cols):
    return (
        lax.broadcasted_iota(jnp.int32, (rows, cols), 0),
        lax.broadcasted_iota(jnp.int32, (rows, cols), 1),
    )


def to_row(eye, column):
    return jnp.sum(jnp.where(eye, column, 0.0), axis=0, keepdims=True)


def to_column(eye, row):
    return jnp.sum(jnp.where(eye, row, 0.0), axis=1, keepdims=True)


def decay_sums(decay):
    row, col = grid_iota(TOK, TOK)
    ones = jnp.where(row <= col, 1.0, 0.0).astype(BF)
    eye = row == col
    hi = decay.astype(BF).astype(F32)
    rest = decay - hi
    mid = rest.astype(BF).astype(F32)
    low = rest - mid
    parts = jnp.concatenate([hi, mid, low, jnp.zeros((2, TOK), F32)], axis=0)
    sums = dot(parts.astype(BF), ones)
    rows = sums[0:2] + (sums[2:4] + sums[4:6])
    return [(rows[h : h + 1], to_column(eye, rows[h : h + 1])) for h in range(2)]


def unit_scale(source):
    full = source.astype(F32)
    return lax.rsqrt(jnp.sum(full * full, axis=1, keepdims=True) + 1e-06)


def slice_kernel(weight_far, half_ref, sem):
    rows = half_ref.shape[0]
    begin = pl.multiple_of(places()[2] * rows, rows)
    copy = pltpu.make_async_copy(weight_far.at[pl.ds(begin, rows)], half_ref, sem)
    copy.start()
    copy.wait()


def map_kernel(
    k_far,
    v_far,
    rate_far,
    decay_far,
    ahead_of,
    maps_ref,
    solved_ref,
    k_ref,
    v_ref,
    rate_ref,
    decay_ref,
    sems,
):
    copies = [
        pltpu.make_async_copy(k_far, k_ref, sems.at[0]),
        pltpu.make_async_copy(decay_far, decay_ref, sems.at[1]),
        pltpu.make_async_copy(rate_far, rate_ref, sems.at[2]),
        pltpu.make_async_copy(v_far, v_ref, sems.at[3]),
    ]
    for copy in copies:
        copy.start()
    for copy in copies:
        copy.wait()
    keys = k_ref[...]
    keys_f = keys.astype(F32)
    values = v_ref[...].astype(F32)
    row, col = grid_iota(TOK, TOK)
    eye = row == col
    strict = row > col
    rate = [to_column(eye, rate_ref[h : h + 1, :]) for h in range(2)]
    gram = dot(keys, keys, ((1,), (1,)))
    scale = unit_scale(keys)
    gram = gram * scale * to_row(eye, scale)
    sum_rows, sums = zip(*decay_sums(decay_ref[...]))
    r_s, c_s = grid_iota(HALF, HALF)
    eye_s = jnp.where(r_s == c_s, 1.0, 0.0).astype(F32)

    lowers, corners = [], []
    for head in range(2):
        fall = jnp.exp(jnp.minimum(sums[head] - sum_rows[head], 0.0))
        low = jnp.where(strict, rate[head] * gram * fall, 0.0)
        lowers += [low[:HALF, :HALF], low[HALF:, HALF:]]
        corners.append(low[HALF:, :HALF])

    small = (r_s // 8) == (c_s // 8)
    first = [jnp.where(small, low, 0.0) for low in lowers]
    first_b = [a.astype(BF) for a in first]
    square = [dot(a, a).astype(BF) for a in first_b]
    fourth = [dot(a, a).astype(BF) for a in square]
    inv = [eye_s - a for a in first]
    inv = [x + dot(x.astype(BF), a) for x, a in zip(inv, square)]
    inv = [x + dot(x.astype(BF), a) for x, a in zip(inv, fourth)]
    size = 8
    while size < HALF:
        off = ((r_s // (2 * size)) == (c_s // (2 * size))) & ((r_s // size) > (c_s // size))
        inv_b = [x.astype(BF) for x in inv]
        part = [jnp.where(off, low, 0.0).astype(BF) for low in lowers]
        part = [dot(a, x).astype(BF) for a, x in zip(part, inv_b)]
        inv = [x - dot(xb, a) for x, xb, a in zip(inv, inv_b, part)]
        size *= 2
    inv_b = [x.astype(BF) for x in inv]
    gap = [
        eye_s - xb.astype(F32) - dot_left(low, xb) for low, xb in zip(lowers, inv_b)
    ]
    inv = [xb.astype(F32) + dot(xb, g.astype(BF)) for xb, g in zip(inv_b, gap)]

    eye_k = jnp.where(r_s == c_s, 1.0, 0.0).astype(F32)
    solved = []
    for head in range(2):
        b = rate[head]
        grow = b * jnp.exp(sums[head]) * scale
        right = jnp.concatenate(
            [grow * keys_f, b * values[:, head * DV : (head + 1) * DV]], axis=1
        )
        top = dot_fine(inv[2 * head], right[:HALF])
        solved.append((top, right[HALF:]))
    for head in range(2):
        top, below = solved[head]
        below = below - dot_fine(corners[head], top)
        below = dot_fine(inv[2 * head + 1], below)
        solved[head] = jnp.concatenate([top, below], axis=0)
    maps = []
    for head in range(2):
        closing = sums[head][TOK - 1 :, :]
        weight = scale * jnp.exp(closing - sums[head])
        moved = dot_right(keys, weight * solved[head], ((0,), (0,)))
        transit = eye_k * jnp.exp(closing) - moved[:, :DK]
        maps.append(jnp.concatenate([transit, moved[:, DK:]], axis=1).astype(BF))
    for place in range(maps_ref.shape[0]):
        maps_ref[place] = maps[place % 2]
    for head in range(2):
        solved_ref[head] = solved[head]


def read_kernel(
    q_ref, k_ref, decay_ref, gate_ref, gain_ref, solved_ref, keep_ref, send_ref
):
    core = places()[2]
    queries = q_ref[...]
    keys = k_ref[...]
    row, col = grid_iota(TOK, TOK)
    eye = row == col
    inclusive = row >= col
    unit_q = unit_scale(queries)
    scores = dot(queries, keys, ((1,), (1,))) * unit_q * to_row(eye, unit_scale(keys))
    sums = decay_sums(decay_ref[...])
    read = []
    for head in range(2):
        sum_row, sum_column = sums[head]
        fall = jnp.exp(jnp.minimum(sum_column - sum_row, 0.0))
        weights = jnp.where(inclusive, scores * fall, 0.0)
        both = dot_fine(weights, solved_ref[head])
        outer = jnp.exp(sum_column) * unit_q * queries.astype(F32) - both[:, :DK]
        gate = gate_ref[:, head * DV : (head + 1) * DV].astype(F32)
        gated = gain_ref[...] * (gate / (1.0 + jnp.exp(-gate)))
        read.append((both[:, DK:], outer, gated))
    for i in range(3):
        keep_ref[i] = jnp.where(core == 0, read[0][i], read[1][i])
        send_ref[i] = jnp.where(core == 0, read[1][i], read[0][i]).astype(BF)


def after(later_t, later_h, earlier, fine):
    moved = dot_fine(later_t, earlier) if fine else dot_right(later_t, earlier)
    return jnp.concatenate([moved[:, :DK], moved[:, DK:] + later_h], axis=1)


def row_kernel(parts_ref, total_ref, ahead_ref, first_ref):
    x = places()[1]

    def pair(i):
        later = parts_ref[2 * i + 1]
        moved = dot(later[:, :DK], parts_ref[2 * i])
        return jnp.concatenate(
            [moved[:, :DK], moved[:, DK:] + later[:, DK:].astype(F32)], axis=1
        )

    pairs = [pair(i) for i in range(4)]
    upto2 = pairs[0]
    upto4 = after(pairs[1][:, :DK], pairs[1][:, DK:], upto2, True)
    last2 = after(pairs[3][:, :DK], pairs[3][:, DK:], pairs[2], True)
    upto6 = after(pairs[2][:, :DK], pairs[2][:, DK:], upto4, True)
    total = after(last2[:, :DK], last2[:, DK:], upto4, True).astype(BF)
    for place in range(4):
        total_ref[place] = total
    row, col = grid_iota(DK, DK + DV)
    none = jnp.where(row == col, 1.0, 0.0).astype(F32)
    ahead_ref[...] = jnp.where(
        x == 0, none, jnp.where(x == 1, upto2, jnp.where(x == 2, upto4, upto6))
    )
    first_ref[...] = parts_ref[2 * x]


def token_of(group, label):
    return 4 * group + (label if group < 2 else 3 - label)


def out_kernel(rows_ref, ahead_ref, first_ref, keep_ref, came_ref, out_ref):
    y, _, core = places()

    def onward(later, state):
        return dot_right(later[:, :DK], state) + later[:, DK:].astype(F32)

    one = rows_ref[0][:, DK:].astype(F32)
    two = onward(rows_ref[1], one)
    three = onward(rows_ref[2], two)
    start = jnp.where(
        y == 0, jnp.zeros_like(one), jnp.where(y == 1, one, jnp.where(y == 2, two, three))
    )
    ahead = ahead_ref[...]
    chip = dot_fine(ahead[:, :DK], start) + ahead[:, DK:]
    second = onward(first_ref[...], chip)

    def finish(state, inner, outer, gated):
        reached = inner + dot_left(outer, state.astype(BF))
        mean = jnp.sum(reached * reached, axis=1, keepdims=True) * (1.0 / DV)
        return (reached * lax.rsqrt(mean + 1e-06) * gated).astype(BF)

    own = finish(jnp.where(core == 0, chip, second), keep_ref[0], keep_ref[1], keep_ref[2])
    came = [came_ref[i].astype(F32) for i in range(3)]
    other = finish(jnp.where(core == 0, second, chip), *came)
    shards = (jnp.where(core == 0, own, other), jnp.where(core == 0, other, own))
    for label in range(4):
        for shard in range(2):
            for group in range(4):
                source = 16 * token_of(group, label)
                target = 64 * shard + 16 * group
                out_ref[label, target : target + 16] = shards[shard][source : source + 16]


def project_kernel(normed_ref, w0_ref, w1_ref, w2_ref, w3_ref, keep_ref, send_ref):
    core = places()[2]
    along = lax.axis_index("tp")
    total = None
    for i, weight_ref in enumerate((w0_ref, w1_ref, w2_ref, w3_ref)):
        near = (along % 4) ^ i
        term = dot(normed_ref[jnp.where(along < 8, near, 3 - near)], weight_ref[...])
        total = term if total is None else total + term
    keep_ref[...] = jnp.where(core == 0, total[:64], total[64:])
    send_ref[...] = jnp.where(core == 0, total[64:], total[:64]).astype(BF)


def join_kernel(keep_ref, came_ref, out_ref):
    total = (keep_ref[...] + came_ref[...].astype(F32)).astype(BF)
    for group in range(4):
        out_ref[group] = total[16 * group : 16 * (group + 1)]


def sum_kernel(parts_ref, out_ref):
    total = parts_ref[0].astype(F32)
    for group in range(1, 4):
        total = total + parts_ref[group].astype(F32)
    out_ref[...] = total.astype(BF)


def places():
    at = lax.axis_index("ctx")
    return at // 8, (at // 2) % 4, at % 2


def in_vmem():
    return pl.BlockSpec(memory_space=pltpu.VMEM)


def in_hbm():
    return pl.BlockSpec(memory_space=pltpu.HBM)


def call(kernel, outs, *args, flops=10**3, name=None, ins=None, out_specs=None, scratch=(), room=32):
    if ins is None:
        ins = [in_vmem()] * len(args)
    return pl.pallas_call(
        kernel,
        out_shape=outs,
        in_specs=ins,
        out_specs=jax.tree.map(lambda _: in_vmem(), outs) if out_specs is None else out_specs,
        scratch_shapes=scratch,
        compiler_params=pltpu.CompilerParams(vmem_limit_bytes=room * 1024 * 1024),
        cost_estimate=pl.CostEstimate(flops=flops, bytes_accessed=10**3, transcendentals=0),
        name=name,
    )(*args)


def shape(dims, kind):
    return jax.ShapeDtypeStruct(dims, kind)


def local(
    queries, key_vectors, value_vectors, output_gate, write_rate, log_decay, norm_gain, out_weight
):
    width = out_weight.shape[1]
    rate, decay = write_rate.T, log_decay.T

    w0 = call(
        slice_kernel,
        shape((DV, width), BF),
        out_weight,
        ins=[in_hbm()],
        scratch=[pltpu.SemaphoreType.DMA],
        room=60,
        name="own_rows",
    )
    w2 = lax.ppermute(w0, "tp", [(j, j ^ 2) for j in range(16)])
    maps, solved = call(
        map_kernel,
        (
            shape((8, DK, DK + DV), BF),
            shape((2, TOK, DK + DV), F32),
        ),
        key_vectors,
        value_vectors,
        rate,
        decay,
        w0,
        ins=[in_hbm()] * 4 + [pl.BlockSpec(memory_space=pl.ANY)],
        scratch=[
            pltpu.VMEM((TOK, DK), BF),
            pltpu.VMEM((TOK, 2 * DV), BF),
            pltpu.VMEM((2, TOK), F32),
            pltpu.VMEM((2, TOK), F32),
            pltpu.SemaphoreType.DMA((4,)),
        ],
        flops=10**10,
        room=60,
        name="shard_maps",
    )
    lines = [[8 * y + i for i in range(8)] for y in range(4)]
    parts = lax.all_to_all(maps, "ctx", 0, 0, axis_index_groups=lines)
    keep, send = call(
        read_kernel,
        (shape((3, TOK, DV), F32), shape((3, TOK, DV), BF)),
        queries,
        key_vectors,
        decay,
        output_gate,
        norm_gain.reshape(1, DV),
        solved,
        flops=10**3,
        name="read_parts",
    )
    across = [(i, i ^ 1) for i in range(32)]
    came = lax.ppermute(send, "ctx", across)

    w0_later, solved = lax.optimization_barrier((w0, solved))
    w1 = lax.ppermute(w0_later, "tp", [(j, j ^ 1) for j in range(16)])

    parts, w2 = lax.optimization_barrier((parts, w2))
    total, ahead, first = call(
        row_kernel,
        (shape((4, DK, DK + DV), BF), shape((DK, DK + DV), F32), shape((DK, DK + DV), BF)),
        parts,
        name="row_maps",
    )
    w1, w2, ahead = lax.optimization_barrier((w1, w2, ahead))
    w3 = lax.ppermute(w2, "tp", [(j, j ^ 1) for j in range(16)])
    columns = [[8 * y + i for y in range(4)] for i in range(8)]
    rows = lax.all_to_all(total, "ctx", 0, 0, axis_index_groups=columns)
    normed = call(
        out_kernel,
        shape((4, 128, DV), BF),
        rows,
        ahead,
        first,
        keep,
        came,
        name="gated_norm",
    )
    close = [[token_of(g, m) for m in range(4)] for g in range(4)]
    gathered = lax.all_to_all(normed, "tp", 0, 0, axis_index_groups=close)
    half, other_half = call(
        project_kernel,
        (shape((64, width), F32), shape((64, width), BF)),
        gathered,
        w0,
        w1,
        w2,
        w3,
        name="project",
    )
    other_half = lax.ppermute(other_half, "ctx", across)
    partial = call(join_kernel, shape((4, 16, width), BF), half, other_half, name="join")
    far = [[token_of(g, m) for g in range(4)] for m in range(4)]
    shares = lax.all_to_all(partial, "tp", 0, 0, axis_index_groups=far)
    return call(sum_kernel, shape((16, width), BF), shares, name="sum_shares")


def solution(mesh):
    placed = (
        P("ctx", "tp"),
        P("ctx", "tp"),
        P("ctx", "tp"),
        P("ctx", "tp"),
        P("ctx", "tp"),
        P("ctx", "tp"),
        P(),
        P("tp", None),
    )
    return jax.shard_map(
        local, mesh=mesh, in_specs=placed, out_specs=P(("ctx", "tp"), None), check_vma=False
    )
```

```python
import jax
import jax.numpy as jnp
from jax import lax
from jax.experimental import pallas as pl
from jax.experimental.pallas import tpu as pltpu
from jax.sharding import PartitionSpec as P

F32 = jnp.float32
BF = jnp.bfloat16
TOK = 256
DK = 128
DV = 128
HALF = 128


def dot(a, b, dims=((1,), (0,))):
    return lax.dot_general(a, b, (dims, ((), ())), preferred_element_type=F32)


def split(a):
    hi = a.astype(BF)
    return hi, (a - hi.astype(F32)).astype(BF)


def dot_fine(a, b, dims=((1,), (0,))):
    ah, al = split(a)
    bh, bl = split(b)
    return dot(ah, bh, dims) + (dot(ah, bl, dims) + dot(al, bh, dims))


def dot_left(a, b, dims=((1,), (0,))):
    ah, al = split(a)
    return dot(ah, b, dims) + dot(al, b, dims)


def dot_right(a, b, dims=((1,), (0,))):
    bh, bl = split(b)
    return dot(a, bh, dims) + dot(a, bl, dims)


def grid_iota(rows, cols):
    return (
        lax.broadcasted_iota(jnp.int32, (rows, cols), 0),
        lax.broadcasted_iota(jnp.int32, (rows, cols), 1),
    )


def to_row(eye, column):
    return jnp.sum(jnp.where(eye, column, 0.0), axis=0, keepdims=True)


def to_column(eye, row):
    return jnp.sum(jnp.where(eye, row, 0.0), axis=1, keepdims=True)


def decay_sums(decay):
    row, col = grid_iota(TOK, TOK)
    ones = jnp.where(row <= col, 1.0, 0.0).astype(BF)
    eye = row == col
    hi = decay.astype(BF).astype(F32)
    rest = decay - hi
    mid = rest.astype(BF).astype(F32)
    low = rest - mid
    parts = jnp.concatenate([hi, mid, low, jnp.zeros((2, TOK), F32)], axis=0)
    sums = dot(parts.astype(BF), ones)
    rows = sums[0:2] + (sums[2:4] + sums[4:6])
    return [(rows[h : h + 1], to_column(eye, rows[h : h + 1])) for h in range(2)]


def unit_scale(source):
    full = source.astype(F32)
    return lax.rsqrt(jnp.sum(full * full, axis=1, keepdims=True) + 1e-06)


def map_kernel(
    k_far,
    v_far,
    rate_far,
    decay_far,
    weight_far,
    maps_ref,
    solved_ref,
    rows_ref,
    half_ref,
    k_ref,
    v_ref,
    rate_ref,
    decay_ref,
    sems,
):
    _, x, core = places()
    rows, some = rows_ref.shape[0], half_ref.shape[0]
    begin = pl.multiple_of(core * rows, rows)
    begin_half = pl.multiple_of(core * rows + (x % 2) * some, some)
    copies = [
        pltpu.make_async_copy(k_far, k_ref, sems.at[0]),
        pltpu.make_async_copy(decay_far, decay_ref, sems.at[1]),
        pltpu.make_async_copy(rate_far, rate_ref, sems.at[2]),
        pltpu.make_async_copy(v_far, v_ref, sems.at[3]),
        pltpu.make_async_copy(weight_far.at[pl.ds(begin, rows)], rows_ref, sems.at[4]),
        pltpu.make_async_copy(weight_far.at[pl.ds(begin_half, some)], half_ref, sems.at[5]),
    ]
    for copy in copies:
        copy.start()
    for copy in copies[:4]:
        copy.wait()
    keys = k_ref[...]
    keys_f = keys.astype(F32)
    values = v_ref[...].astype(F32)
    row, col = grid_iota(TOK, TOK)
    eye = row == col
    strict = row > col
    rate = [to_column(eye, rate_ref[h : h + 1, :]) for h in range(2)]
    gram = dot(keys, keys, ((1,), (1,)))
    scale = unit_scale(keys)
    gram = gram * scale * to_row(eye, scale)
    sum_rows, sums = zip(*decay_sums(decay_ref[...]))
    r_s, c_s = grid_iota(HALF, HALF)
    eye_s = jnp.where(r_s == c_s, 1.0, 0.0).astype(F32)

    lowers, corners = [], []
    for head in range(2):
        fall = jnp.exp(jnp.minimum(sums[head] - sum_rows[head], 0.0))
        low = jnp.where(strict, rate[head] * gram * fall, 0.0)
        lowers += [low[:HALF, :HALF], low[HALF:, HALF:]]
        corners.append(low[HALF:, :HALF])

    small = (r_s // 8) == (c_s // 8)
    first = [jnp.where(small, low, 0.0) for low in lowers]
    first_b = [a.astype(BF) for a in first]
    square = [dot(a, a).astype(BF) for a in first_b]
    fourth = [dot(a, a).astype(BF) for a in square]
    inv = [eye_s - a for a in first]
    inv = [x + dot(x.astype(BF), a) for x, a in zip(inv, square)]
    inv = [x + dot(x.astype(BF), a) for x, a in zip(inv, fourth)]
    size = 8
    while size < HALF:
        off = ((r_s // (2 * size)) == (c_s // (2 * size))) & ((r_s // size) > (c_s // size))
        inv_b = [x.astype(BF) for x in inv]
        part = [jnp.where(off, low, 0.0).astype(BF) for low in lowers]
        part = [dot(a, x).astype(BF) for a, x in zip(part, inv_b)]
        inv = [x - dot(xb, a) for x, xb, a in zip(inv, inv_b, part)]
        size *= 2
    inv_b = [x.astype(BF) for x in inv]
    gap = [
        eye_s - xb.astype(F32) - dot_left(low, xb) for low, xb in zip(lowers, inv_b)
    ]
    inv = [xb.astype(F32) + dot(xb, g.astype(BF)) for xb, g in zip(inv_b, gap)]

    eye_k = jnp.where(r_s == c_s, 1.0, 0.0).astype(F32)
    solved = []
    for head in range(2):
        b = rate[head]
        grow = b * jnp.exp(sums[head]) * scale
        right = jnp.concatenate(
            [grow * keys_f, b * values[:, head * DV : (head + 1) * DV]], axis=1
        )
        top = dot_fine(inv[2 * head], right[:HALF])
        solved.append((top, right[HALF:]))
    for head in range(2):
        top, below = solved[head]
        below = below - dot_fine(corners[head], top)
        below = dot_fine(inv[2 * head + 1], below)
        solved[head] = jnp.concatenate([top, below], axis=0)
    maps = []
    for head in range(2):
        closing = sums[head][TOK - 1 :, :]
        weight = scale * jnp.exp(closing - sums[head])
        moved = dot_right(keys, weight * solved[head], ((0,), (0,)))
        transit = eye_k * jnp.exp(closing) - moved[:, :DK]
        maps.append(jnp.concatenate([transit, moved[:, DK:]], axis=1).astype(BF))
    for place in range(maps_ref.shape[0]):
        maps_ref[place] = maps[place % 2]
    for head in range(2):
        solved_ref[head] = solved[head]
    for copy in copies[4:]:
        copy.wait()


def read_kernel(
    q_ref, k_ref, decay_ref, gate_ref, gain_ref, solved_ref, keep_ref, send_ref
):
    core = places()[2]
    queries = q_ref[...]
    keys = k_ref[...]
    row, col = grid_iota(TOK, TOK)
    eye = row == col
    inclusive = row >= col
    unit_q = unit_scale(queries)
    scores = dot(queries, keys, ((1,), (1,))) * unit_q * to_row(eye, unit_scale(keys))
    sums = decay_sums(decay_ref[...])
    read = []
    for head in range(2):
        sum_row, sum_column = sums[head]
        fall = jnp.exp(jnp.minimum(sum_column - sum_row, 0.0))
        weights = jnp.where(inclusive, scores * fall, 0.0)
        both = dot_fine(weights, solved_ref[head])
        outer = jnp.exp(sum_column) * unit_q * queries.astype(F32) - both[:, :DK]
        gate = gate_ref[:, head * DV : (head + 1) * DV].astype(F32)
        gated = gain_ref[...] * (gate / (1.0 + jnp.exp(-gate)))
        read.append((both[:, DK:], outer, gated))
    for i in range(3):
        keep_ref[i] = jnp.where(core == 0, read[0][i], read[1][i])
        send_ref[i] = jnp.where(core == 0, read[1][i], read[0][i]).astype(BF)


def after(later_t, later_h, earlier, fine):
    moved = dot_fine(later_t, earlier) if fine else dot_right(later_t, earlier)
    return jnp.concatenate([moved[:, :DK], moved[:, DK:] + later_h], axis=1)


def row_kernel(parts_ref, total_ref, ahead_ref, first_ref):
    x = places()[1]

    def pair(i):
        later = parts_ref[2 * i + 1]
        moved = dot(later[:, :DK], parts_ref[2 * i])
        return jnp.concatenate(
            [moved[:, :DK], moved[:, DK:] + later[:, DK:].astype(F32)], axis=1
        )

    pairs = [pair(i) for i in range(4)]
    upto2 = pairs[0]
    upto4 = after(pairs[1][:, :DK], pairs[1][:, DK:], upto2, True)
    last2 = after(pairs[3][:, :DK], pairs[3][:, DK:], pairs[2], True)
    upto6 = after(pairs[2][:, :DK], pairs[2][:, DK:], upto4, True)
    total = after(last2[:, :DK], last2[:, DK:], upto4, True).astype(BF)
    for place in range(4):
        total_ref[place] = total
    row, col = grid_iota(DK, DK + DV)
    none = jnp.where(row == col, 1.0, 0.0).astype(F32)
    ahead_ref[...] = jnp.where(
        x == 0, none, jnp.where(x == 1, upto2, jnp.where(x == 2, upto4, upto6))
    )
    first_ref[...] = parts_ref[2 * x]


def token_of(group, label):
    return 4 * group + (label if group < 2 else 3 - label)


def out_kernel(rows_ref, ahead_ref, first_ref, keep_ref, came_ref, out_ref):
    y, _, core = places()

    def onward(later, state):
        return dot_right(later[:, :DK], state) + later[:, DK:].astype(F32)

    one = rows_ref[0][:, DK:].astype(F32)
    two = onward(rows_ref[1], one)
    three = onward(rows_ref[2], two)
    start = jnp.where(
        y == 0, jnp.zeros_like(one), jnp.where(y == 1, one, jnp.where(y == 2, two, three))
    )
    ahead = ahead_ref[...]
    chip = dot_fine(ahead[:, :DK], start) + ahead[:, DK:]
    second = onward(first_ref[...], chip)

    def finish(state, inner, outer, gated):
        reached = inner + dot_left(outer, state.astype(BF))
        mean = jnp.sum(reached * reached, axis=1, keepdims=True) * (1.0 / DV)
        return (reached * lax.rsqrt(mean + 1e-06) * gated).astype(BF)

    own = finish(jnp.where(core == 0, chip, second), keep_ref[0], keep_ref[1], keep_ref[2])
    came = [came_ref[i].astype(F32) for i in range(3)]
    other = finish(jnp.where(core == 0, second, chip), *came)
    shards = (jnp.where(core == 0, own, other), jnp.where(core == 0, other, own))
    for label in range(4):
        for shard in range(2):
            for group in range(4):
                source = 16 * token_of(group, label)
                target = 64 * shard + 16 * group
                out_ref[label, target : target + 16] = shards[shard][source : source + 16]


def project_kernel(
    normed_ref, own_ref, near_ref, half3_ref, side_ref, side3_ref, keep_ref, send_ref
):
    _, x, core = places()
    along = lax.axis_index("tp")

    def rows_from(i):
        near = (along % 4) ^ i
        return normed_ref[jnp.where(along < 8, near, 3 - near)]

    total = dot(rows_from(0), own_ref[...])
    halves = ((near_ref[0], side_ref[0]), (near_ref[1], side_ref[1]), (half3_ref[...], side3_ref[...]))
    for i, (mine, other) in enumerate(halves):
        left = rows_from(i + 1).astype(F32)
        swapped = jnp.concatenate([left[:, DV // 2 :], left[:, : DV // 2]], axis=1)
        left = jnp.where(x % 2 == 0, left, swapped).astype(BF)
        total = total + dot(left, jnp.concatenate([mine, other], axis=0))
    keep_ref[...] = jnp.where(core == 0, total[:64], total[64:])
    send_ref[...] = jnp.where(core == 0, total[64:], total[:64]).astype(BF)


def join_kernel(keep_ref, came_ref, out_ref):
    total = (keep_ref[...] + came_ref[...].astype(F32)).astype(BF)
    for group in range(4):
        out_ref[group] = total[16 * group : 16 * (group + 1)]


def sum_kernel(parts_ref, out_ref):
    total = parts_ref[0].astype(F32)
    for group in range(1, 4):
        total = total + parts_ref[group].astype(F32)
    out_ref[...] = total.astype(BF)


def places():
    at = lax.axis_index("ctx")
    return at // 8, (at // 2) % 4, at % 2


def in_vmem():
    return pl.BlockSpec(memory_space=pltpu.VMEM)


def in_hbm():
    return pl.BlockSpec(memory_space=pltpu.HBM)


def call(kernel, outs, *args, flops=10**3, name=None, ins=None, out_specs=None, scratch=(), room=32):
    if ins is None:
        ins = [in_vmem()] * len(args)
    return pl.pallas_call(
        kernel,
        out_shape=outs,
        in_specs=ins,
        out_specs=jax.tree.map(lambda _: in_vmem(), outs) if out_specs is None else out_specs,
        scratch_shapes=scratch,
        compiler_params=pltpu.CompilerParams(vmem_limit_bytes=room * 1024 * 1024),
        cost_estimate=pl.CostEstimate(flops=flops, bytes_accessed=10**3, transcendentals=0),
        name=name,
    )(*args)


def shape(dims, kind):
    return jax.ShapeDtypeStruct(dims, kind)


def local(
    queries, key_vectors, value_vectors, output_gate, write_rate, log_decay, norm_gain, out_weight
):
    width = out_weight.shape[1]
    rate, decay = write_rate.T, log_decay.T

    maps, solved, w0, half0 = call(
        map_kernel,
        (
            shape((8, DK, DK + DV), BF),
            shape((2, TOK, DK + DV), F32),
            shape((DV, width), BF),
            shape((DV // 2, width), BF),
        ),
        key_vectors,
        value_vectors,
        rate,
        decay,
        out_weight,
        ins=[in_hbm()] * 5,
        out_specs=(in_vmem(), in_vmem(), in_vmem(), in_vmem()),
        scratch=[
            pltpu.VMEM((TOK, DK), BF),
            pltpu.VMEM((TOK, 2 * DV), BF),
            pltpu.VMEM((2, TOK), F32),
            pltpu.VMEM((2, TOK), F32),
            pltpu.SemaphoreType.DMA((6,)),
        ],
        flops=10**9,
        room=60,
        name="shard_maps",
    )
    lines = [[8 * y + i for i in range(8)] for y in range(4)]
    parts = lax.all_to_all(maps, "ctx", 0, 0, axis_index_groups=lines)
    keep, send = call(
        read_kernel,
        (shape((3, TOK, DV), F32), shape((3, TOK, DV), BF)),
        queries,
        key_vectors,
        decay,
        output_gate,
        norm_gain.reshape(1, DV),
        solved,
        flops=10**9,
        name="read_parts",
    )
    across = [(i, i ^ 1) for i in range(32)]
    came = lax.ppermute(send, "ctx", across)

    one_off = [(j, j ^ 1) for j in range(16)]
    half1 = lax.ppermute(half0, "tp", one_off)
    half2 = lax.ppermute(half0, "tp", [(j, j ^ 2) for j in range(16)])

    total, ahead, first = call(
        row_kernel,
        (shape((4, DK, DK + DV), BF), shape((DK, DK + DV), F32), shape((DK, DK + DV), BF)),
        parts,
        name="row_maps",
    )
    half0, ahead = lax.optimization_barrier((half0, ahead))
    half3 = lax.ppermute(half0, "tp", [(j, j ^ 3) for j in range(16)])
    sideways = [(i, i ^ 2) for i in range(32)]
    near12 = jnp.stack([half1, half2])
    side12 = lax.ppermute(near12, "ctx", sideways)
    columns = [[8 * y + i for y in range(4)] for i in range(8)]
    rows = lax.all_to_all(total, "ctx", 0, 0, axis_index_groups=columns)
    normed = call(
        out_kernel,
        shape((4, 128, DV), BF),
        rows,
        ahead,
        first,
        keep,
        came,
        name="gated_norm",
    )
    close = [[token_of(g, m) for m in range(4)] for g in range(4)]
    half3, normed = lax.optimization_barrier((half3, normed))
    side3 = lax.ppermute(half3, "ctx", sideways)
    gathered = lax.all_to_all(normed, "tp", 0, 0, axis_index_groups=close)
    half, other_half = call(
        project_kernel,
        (shape((64, width), F32), shape((64, width), BF)),
        gathered,
        w0,
        near12,
        half3,
        side12,
        side3,
        name="project",
    )
    other_half = lax.ppermute(other_half, "ctx", across)
    partial = call(join_kernel, shape((4, 16, width), BF), half, other_half, name="join")
    far = [[token_of(g, m) for g in range(4)] for m in range(4)]
    shares = lax.all_to_all(partial, "tp", 0, 0, axis_index_groups=far)
    return call(sum_kernel, shape((16, width), BF), shares, name="sum_shares")


def solution(mesh):
    placed = (
        P("ctx", "tp"),
        P("ctx", "tp"),
        P("ctx", "tp"),
        P("ctx", "tp"),
        P("ctx", "tp"),
        P("ctx", "tp"),
        P(),
        P("tp", None),
    )
    return jax.shard_map(
        local, mesh=mesh, in_specs=placed, out_specs=P(("ctx", "tp"), None), check_vma=False
    )
```

```python
import jax
import jax.numpy as jnp
from jax import lax
from jax.experimental import pallas as pl
from jax.experimental.pallas import tpu as pltpu
from jax.sharding import PartitionSpec as P

F32 = jnp.float32
BF = jnp.bfloat16
TOK = 256
DK = 128
DV = 128
HALF = 128


def dot(a, b, dims=((1,), (0,))):
    return lax.dot_general(a, b, (dims, ((), ())), preferred_element_type=F32)


def split(a):
    hi = a.astype(BF)
    return hi, (a - hi.astype(F32)).astype(BF)


def dot_fine(a, b, dims=((1,), (0,))):
    ah, al = split(a)
    bh, bl = split(b)
    return dot(ah, bh, dims) + (dot(ah, bl, dims) + dot(al, bh, dims))


def dot_left(a, b, dims=((1,), (0,))):
    ah, al = split(a)
    return dot(ah, b, dims) + dot(al, b, dims)


def dot_right(a, b, dims=((1,), (0,))):
    bh, bl = split(b)
    return dot(a, bh, dims) + dot(a, bl, dims)


def grid_iota(rows, cols):
    return (
        lax.broadcasted_iota(jnp.int32, (rows, cols), 0),
        lax.broadcasted_iota(jnp.int32, (rows, cols), 1),
    )


def to_row(eye, column):
    return jnp.sum(jnp.where(eye, column, 0.0), axis=0, keepdims=True)


def to_column(eye, row):
    return jnp.sum(jnp.where(eye, row, 0.0), axis=1, keepdims=True)


def decay_sums(decay):
    row, col = grid_iota(TOK, TOK)
    ones = jnp.where(row <= col, 1.0, 0.0).astype(BF)
    eye = row == col
    hi = decay.astype(BF).astype(F32)
    rest = decay - hi
    mid = rest.astype(BF).astype(F32)
    low = rest - mid
    parts = jnp.concatenate([hi, mid, low, jnp.zeros((2, TOK), F32)], axis=0)
    sums = dot(parts.astype(BF), ones)
    rows = sums[0:2] + (sums[2:4] + sums[4:6])
    return [(rows[h : h + 1], to_column(eye, rows[h : h + 1])) for h in range(2)]


def unit_scale(source):
    full = source.astype(F32)
    return lax.rsqrt(jnp.sum(full * full, axis=1, keepdims=True) + 1e-06)


def map_kernel(
    k_far,
    v_far,
    rate_far,
    decay_far,
    weight_far,
    maps_ref,
    solved_ref,
    rows_ref,
    half_ref,
    k_ref,
    v_ref,
    rate_ref,
    decay_ref,
    sems,
):
    _, x, core = places()
    rows, some = rows_ref.shape[0], half_ref.shape[0]
    begin = pl.multiple_of(core * rows, rows)
    begin_half = pl.multiple_of(core * rows + (x % 2) * some, some)
    copies = [
        pltpu.make_async_copy(k_far, k_ref, sems.at[0]),
        pltpu.make_async_copy(decay_far, decay_ref, sems.at[1]),
        pltpu.make_async_copy(rate_far, rate_ref, sems.at[2]),
        pltpu.make_async_copy(v_far, v_ref, sems.at[3]),
        pltpu.make_async_copy(weight_far.at[pl.ds(begin, rows)], rows_ref, sems.at[4]),
        pltpu.make_async_copy(weight_far.at[pl.ds(begin_half, some)], half_ref, sems.at[5]),
    ]
    for copy in copies:
        copy.start()
    for copy in copies[:4]:
        copy.wait()
    keys = k_ref[...]
    keys_f = keys.astype(F32)
    values = v_ref[...].astype(F32)
    row, col = grid_iota(TOK, TOK)
    eye = row == col
    strict = row > col
    rate = [to_column(eye, rate_ref[h : h + 1, :]) for h in range(2)]
    gram = dot(keys, keys, ((1,), (1,)))
    scale = unit_scale(keys)
    gram = gram * scale * to_row(eye, scale)
    sum_rows, sums = zip(*decay_sums(decay_ref[...]))
    r_s, c_s = grid_iota(HALF, HALF)
    eye_s = jnp.where(r_s == c_s, 1.0, 0.0).astype(F32)

    lowers, corners = [], []
    for head in range(2):
        fall = jnp.exp(jnp.minimum(sums[head] - sum_rows[head], 0.0))
        low = jnp.where(strict, rate[head] * gram * fall, 0.0)
        lowers += [low[:HALF, :HALF], low[HALF:, HALF:]]
        corners.append(low[HALF:, :HALF])

    small = (r_s // 8) == (c_s // 8)
    first = [jnp.where(small, low, 0.0) for low in lowers]
    first_b = [a.astype(BF) for a in first]
    square = [dot(a, a).astype(BF) for a in first_b]
    fourth = [dot(a, a).astype(BF) for a in square]
    inv = [eye_s - a for a in first]
    inv = [x + dot(x.astype(BF), a) for x, a in zip(inv, square)]
    inv = [x + dot(x.astype(BF), a) for x, a in zip(inv, fourth)]
    size = 8
    while size < HALF:
        off = ((r_s // (2 * size)) == (c_s // (2 * size))) & ((r_s // size) > (c_s // size))
        inv_b = [x.astype(BF) for x in inv]
        part = [jnp.where(off, low, 0.0).astype(BF) for low in lowers]
        part = [dot(a, x).astype(BF) for a, x in zip(part, inv_b)]
        inv = [x - dot(xb, a) for x, xb, a in zip(inv, inv_b, part)]
        size *= 2
    inv_b = [x.astype(BF) for x in inv]
    gap = [
        eye_s - xb.astype(F32) - dot_left(low, xb) for low, xb in zip(lowers, inv_b)
    ]
    inv = [xb.astype(F32) + dot(xb, g.astype(BF)) for xb, g in zip(inv_b, gap)]

    eye_k = jnp.where(r_s == c_s, 1.0, 0.0).astype(F32)
    solved = []
    for head in range(2):
        b = rate[head]
        grow = b * jnp.exp(sums[head]) * scale
        right = jnp.concatenate(
            [grow * keys_f, b * values[:, head * DV : (head + 1) * DV]], axis=1
        )
        top = dot_fine(inv[2 * head], right[:HALF])
        solved.append((top, right[HALF:]))
    for head in range(2):
        top, below = solved[head]
        below = below - dot_fine(corners[head], top)
        below = dot_fine(inv[2 * head + 1], below)
        solved[head] = jnp.concatenate([top, below], axis=0)
    maps = []
    for head in range(2):
        closing = sums[head][TOK - 1 :, :]
        weight = scale * jnp.exp(closing - sums[head])
        moved = dot_right(keys, weight * solved[head], ((0,), (0,)))
        transit = eye_k * jnp.exp(closing) - moved[:, :DK]
        maps.append(jnp.concatenate([transit, moved[:, DK:]], axis=1).astype(BF))
    for place in range(maps_ref.shape[0]):
        maps_ref[place] = maps[place % 2]
    for head in range(2):
        solved_ref[head] = solved[head]
    for copy in copies[4:]:
        copy.wait()


def read_kernel(
    q_ref, k_ref, decay_ref, gate_ref, gain_ref, solved_ref, keep_ref, send_ref
):
    core = places()[2]
    queries = q_ref[...]
    keys = k_ref[...]
    row, col = grid_iota(TOK, TOK)
    eye = row == col
    inclusive = row >= col
    unit_q = unit_scale(queries)
    scores = dot(queries, keys, ((1,), (1,))) * unit_q * to_row(eye, unit_scale(keys))
    sums = decay_sums(decay_ref[...])
    read = []
    for head in range(2):
        sum_row, sum_column = sums[head]
        fall = jnp.exp(jnp.minimum(sum_column - sum_row, 0.0))
        weights = jnp.where(inclusive, scores * fall, 0.0)
        both = dot_fine(weights, solved_ref[head])
        outer = jnp.exp(sum_column) * unit_q * queries.astype(F32) - both[:, :DK]
        gate = gate_ref[:, head * DV : (head + 1) * DV].astype(F32)
        gated = gain_ref[...] * (gate / (1.0 + jnp.exp(-gate)))
        read.append((both[:, DK:], outer, gated))
    for i in range(3):
        keep_ref[i] = jnp.where(core == 0, read[0][i], read[1][i])
        send_ref[i] = jnp.where(core == 0, read[1][i], read[0][i]).astype(BF)


def after(later_t, later_h, earlier, fine):
    moved = dot_fine(later_t, earlier) if fine else dot_right(later_t, earlier)
    return jnp.concatenate([moved[:, :DK], moved[:, DK:] + later_h], axis=1)


def row_kernel(parts_ref, total_ref, ahead_ref, first_ref):
    x = places()[1]

    def pair(i):
        later = parts_ref[2 * i + 1]
        moved = dot(later[:, :DK], parts_ref[2 * i])
        return jnp.concatenate(
            [moved[:, :DK], moved[:, DK:] + later[:, DK:].astype(F32)], axis=1
        )

    pairs = [pair(i) for i in range(4)]
    upto2 = pairs[0]
    upto4 = after(pairs[1][:, :DK], pairs[1][:, DK:], upto2, True)
    last2 = after(pairs[3][:, :DK], pairs[3][:, DK:], pairs[2], True)
    upto6 = after(pairs[2][:, :DK], pairs[2][:, DK:], upto4, True)
    total = after(last2[:, :DK], last2[:, DK:], upto4, True).astype(BF)
    for place in range(4):
        total_ref[place] = total
    row, col = grid_iota(DK, DK + DV)
    none = jnp.where(row == col, 1.0, 0.0).astype(F32)
    ahead_ref[...] = jnp.where(
        x == 0, none, jnp.where(x == 1, upto2, jnp.where(x == 2, upto4, upto6))
    )
    first_ref[...] = parts_ref[2 * x]


def token_of(group, label):
    return 4 * group + (label if group < 2 else 3 - label)


def out_kernel(rows_ref, ahead_ref, first_ref, keep_ref, came_ref, out_ref):
    y, _, core = places()

    def onward(later, state):
        return dot_right(later[:, :DK], state) + later[:, DK:].astype(F32)

    one = rows_ref[0][:, DK:].astype(F32)
    two = onward(rows_ref[1], one)
    three = onward(rows_ref[2], two)
    start = jnp.where(
        y == 0, jnp.zeros_like(one), jnp.where(y == 1, one, jnp.where(y == 2, two, three))
    )
    ahead = ahead_ref[...]
    chip = dot_fine(ahead[:, :DK], start) + ahead[:, DK:]
    second = onward(first_ref[...], chip)

    def finish(state, inner, outer, gated):
        reached = inner + dot_left(outer, state.astype(BF))
        mean = jnp.sum(reached * reached, axis=1, keepdims=True) * (1.0 / DV)
        return (reached * lax.rsqrt(mean + 1e-06) * gated).astype(BF)

    own = finish(jnp.where(core == 0, chip, second), keep_ref[0], keep_ref[1], keep_ref[2])
    came = [came_ref[i].astype(F32) for i in range(3)]
    other = finish(jnp.where(core == 0, second, chip), *came)
    shards = (jnp.where(core == 0, own, other), jnp.where(core == 0, other, own))
    for label in range(4):
        for shard in range(2):
            for group in range(4):
                source = 16 * token_of(group, label)
                target = 64 * shard + 16 * group
                out_ref[label, target : target + 16] = shards[shard][source : source + 16]


def project_kernel(
    normed_ref, own_ref, near_ref, half3_ref, side_ref, side3_ref, keep_ref, send_ref
):
    _, x, core = places()
    along = lax.axis_index("tp")

    def rows_from(i):
        near = (along % 4) ^ i
        return normed_ref[jnp.where(along < 8, near, 3 - near)]

    total = dot(rows_from(0), own_ref[...])
    halves = ((near_ref[0], side_ref[0]), (near_ref[1], side_ref[1]), (half3_ref[...], side3_ref[...]))
    for i, (mine, other) in enumerate(halves):
        left = rows_from(i + 1).astype(F32)
        swapped = jnp.concatenate([left[:, DV // 2 :], left[:, : DV // 2]], axis=1)
        left = jnp.where(x % 2 == 0, left, swapped).astype(BF)
        total = total + dot(left, jnp.concatenate([mine, other], axis=0))
    keep_ref[...] = jnp.where(core == 0, total[:64], total[64:])
    send_ref[...] = jnp.where(core == 0, total[64:], total[:64]).astype(BF)


def join_kernel(keep_ref, came_ref, out_ref):
    total = (keep_ref[...] + came_ref[...].astype(F32)).astype(BF)
    for group in range(4):
        out_ref[group] = total[16 * group : 16 * (group + 1)]


def sum_kernel(parts_ref, out_ref):
    total = parts_ref[0].astype(F32)
    for group in range(1, 4):
        total = total + parts_ref[group].astype(F32)
    out_ref[...] = total.astype(BF)


def places():
    at = lax.axis_index("ctx")
    return at // 8, (at // 2) % 4, at % 2


def in_vmem():
    return pl.BlockSpec(memory_space=pltpu.VMEM)


def in_hbm():
    return pl.BlockSpec(memory_space=pltpu.HBM)


def call(kernel, outs, *args, flops=10**3, name=None, ins=None, out_specs=None, scratch=(), room=32):
    if ins is None:
        ins = [in_vmem()] * len(args)
    return pl.pallas_call(
        kernel,
        out_shape=outs,
        in_specs=ins,
        out_specs=jax.tree.map(lambda _: in_vmem(), outs) if out_specs is None else out_specs,
        scratch_shapes=scratch,
        compiler_params=pltpu.CompilerParams(vmem_limit_bytes=room * 1024 * 1024),
        cost_estimate=pl.CostEstimate(flops=flops, bytes_accessed=10**3, transcendentals=0),
        name=name,
    )(*args)


def shape(dims, kind):
    return jax.ShapeDtypeStruct(dims, kind)


def local(
    queries, key_vectors, value_vectors, output_gate, write_rate, log_decay, norm_gain, out_weight
):
    width = out_weight.shape[1]
    rate, decay = write_rate.T, log_decay.T

    maps, solved, w0, half0 = call(
        map_kernel,
        (
            shape((8, DK, DK + DV), BF),
            shape((2, TOK, DK + DV), F32),
            shape((DV, width), BF),
            shape((DV // 2, width), BF),
        ),
        key_vectors,
        value_vectors,
        rate,
        decay,
        out_weight,
        ins=[in_hbm()] * 5,
        out_specs=(in_vmem(), in_vmem(), in_vmem(), in_vmem()),
        scratch=[
            pltpu.VMEM((TOK, DK), BF),
            pltpu.VMEM((TOK, 2 * DV), BF),
            pltpu.VMEM((2, TOK), F32),
            pltpu.VMEM((2, TOK), F32),
            pltpu.SemaphoreType.DMA((6,)),
        ],
        flops=10**9,
        room=60,
        name="shard_maps",
    )
    lines = [[8 * y + i for i in range(8)] for y in range(4)]
    parts = lax.all_to_all(maps, "ctx", 0, 0, axis_index_groups=lines)
    keep, send = call(
        read_kernel,
        (shape((3, TOK, DV), F32), shape((3, TOK, DV), BF)),
        queries,
        key_vectors,
        decay,
        output_gate,
        norm_gain.reshape(1, DV),
        solved,
        flops=10**9,
        name="read_parts",
    )
    across = [(i, i ^ 1) for i in range(32)]
    came = lax.ppermute(send, "ctx", across)

    one_off = [(j, j ^ 1) for j in range(16)]
    half1 = lax.ppermute(half0, "tp", one_off)
    half2 = lax.ppermute(half0, "tp", [(j, j ^ 2) for j in range(16)])

    total, ahead, first = call(
        row_kernel,
        (shape((4, DK, DK + DV), BF), shape((DK, DK + DV), F32), shape((DK, DK + DV), BF)),
        parts,
        name="row_maps",
    )
    half3 = lax.ppermute(half0, "tp", [(j, j ^ 3) for j in range(16)])
    sideways = [(i, i ^ 2) for i in range(32)]
    near12 = jnp.stack([half1, half2])
    side12 = lax.ppermute(near12, "ctx", sideways)
    columns = [[8 * y + i for y in range(4)] for i in range(8)]
    rows = lax.all_to_all(total, "ctx", 0, 0, axis_index_groups=columns)
    normed = call(
        out_kernel,
        shape((4, 128, DV), BF),
        rows,
        ahead,
        first,
        keep,
        came,
        name="gated_norm",
    )
    close = [[token_of(g, m) for m in range(4)] for g in range(4)]
    side3 = lax.ppermute(half3, "ctx", sideways)
    gathered = lax.all_to_all(normed, "tp", 0, 0, axis_index_groups=close)
    half, other_half = call(
        project_kernel,
        (shape((64, width), F32), shape((64, width), BF)),
        gathered,
        w0,
        near12,
        half3,
        side12,
        side3,
        name="project",
    )
    other_half = lax.ppermute(other_half, "ctx", across)
    partial = call(join_kernel, shape((4, 16, width), BF), half, other_half, name="join")
    far = [[token_of(g, m) for g in range(4)] for m in range(4)]
    shares = lax.all_to_all(partial, "tp", 0, 0, axis_index_groups=far)
    return call(sum_kernel, shape((16, width), BF), shares, name="sum_shares")


def solution(mesh):
    placed = (
        P("ctx", "tp"),
        P("ctx", "tp"),
        P("ctx", "tp"),
        P("ctx", "tp"),
        P("ctx", "tp"),
        P("ctx", "tp"),
        P(),
        P("tp", None),
    )
    return jax.shard_map(
        local, mesh=mesh, in_specs=placed, out_specs=P(("ctx", "tp"), None), check_vma=False
    )
```

```python
import jax
import jax.numpy as jnp
from jax import lax
from jax.experimental import pallas as pl
from jax.experimental.pallas import tpu as pltpu
from jax.sharding import PartitionSpec as P

F32 = jnp.float32
BF = jnp.bfloat16
TOK = 256
DK = 128
DV = 128
HALF = 128


def dot(a, b, dims=((1,), (0,))):
    return lax.dot_general(a, b, (dims, ((), ())), preferred_element_type=F32)


def split(a):
    hi = a.astype(BF)
    return hi, (a - hi.astype(F32)).astype(BF)


def dot_fine(a, b, dims=((1,), (0,))):
    ah, al = split(a)
    bh, bl = split(b)
    return dot(ah, bh, dims) + (dot(ah, bl, dims) + dot(al, bh, dims))


def dot_left(a, b, dims=((1,), (0,))):
    ah, al = split(a)
    return dot(ah, b, dims) + dot(al, b, dims)


def dot_right(a, b, dims=((1,), (0,))):
    bh, bl = split(b)
    return dot(a, bh, dims) + dot(a, bl, dims)


def grid_iota(rows, cols):
    return (
        lax.broadcasted_iota(jnp.int32, (rows, cols), 0),
        lax.broadcasted_iota(jnp.int32, (rows, cols), 1),
    )


def to_row(eye, column):
    return jnp.sum(jnp.where(eye, column, 0.0), axis=0, keepdims=True)


def to_column(eye, row):
    return jnp.sum(jnp.where(eye, row, 0.0), axis=1, keepdims=True)


def decay_sums(decay):
    row, col = grid_iota(TOK, TOK)
    ones = jnp.where(row <= col, 1.0, 0.0).astype(BF)
    eye = row == col
    hi = decay.astype(BF).astype(F32)
    rest = decay - hi
    mid = rest.astype(BF).astype(F32)
    low = rest - mid
    parts = jnp.concatenate([hi, mid, low, jnp.zeros((2, TOK), F32)], axis=0)
    sums = dot(parts.astype(BF), ones)
    rows = sums[0:2] + (sums[2:4] + sums[4:6])
    return [(rows[h : h + 1], to_column(eye, rows[h : h + 1])) for h in range(2)]


def unit_scale(source):
    full = source.astype(F32)
    return lax.rsqrt(jnp.sum(full * full, axis=1, keepdims=True) + 1e-06)


def map_kernel(
    k_far,
    v_far,
    rate_far,
    decay_far,
    weight_far,
    maps_ref,
    solved_ref,
    half_ref,
    k_ref,
    v_ref,
    rate_ref,
    decay_ref,
    sems,
):
    _, x, core = places()
    rows, columns = half_ref.shape
    begin = pl.multiple_of(core * rows, rows)
    left = pl.multiple_of((x % 2) * columns, columns)
    copies = [
        pltpu.make_async_copy(k_far, k_ref, sems.at[0]),
        pltpu.make_async_copy(decay_far, decay_ref, sems.at[1]),
        pltpu.make_async_copy(rate_far, rate_ref, sems.at[2]),
        pltpu.make_async_copy(v_far, v_ref, sems.at[3]),
        pltpu.make_async_copy(
            weight_far.at[pl.ds(begin, rows), pl.ds(left, columns)], half_ref, sems.at[4]
        ),
    ]
    for copy in copies:
        copy.start()
    for copy in copies[:4]:
        copy.wait()
    keys = k_ref[...]
    keys_f = keys.astype(F32)
    values = v_ref[...].astype(F32)
    row, col = grid_iota(TOK, TOK)
    eye = row == col
    strict = row > col
    rate = [to_column(eye, rate_ref[h : h + 1, :]) for h in range(2)]
    gram = dot(keys, keys, ((1,), (1,)))
    scale = unit_scale(keys)
    gram = gram * scale * to_row(eye, scale)
    sum_rows, sums = zip(*decay_sums(decay_ref[...]))
    r_s, c_s = grid_iota(HALF, HALF)
    eye_s = jnp.where(r_s == c_s, 1.0, 0.0).astype(F32)

    lowers, corners = [], []
    for head in range(2):
        fall = jnp.exp(jnp.minimum(sums[head] - sum_rows[head], 0.0))
        low = jnp.where(strict, rate[head] * gram * fall, 0.0)
        lowers += [low[:HALF, :HALF], low[HALF:, HALF:]]
        corners.append(low[HALF:, :HALF])

    small = (r_s // 8) == (c_s // 8)
    first = [jnp.where(small, low, 0.0) for low in lowers]
    first_b = [a.astype(BF) for a in first]
    square = [dot(a, a).astype(BF) for a in first_b]
    fourth = [dot(a, a).astype(BF) for a in square]
    inv = [eye_s - a for a in first]
    inv = [x + dot(x.astype(BF), a) for x, a in zip(inv, square)]
    inv = [x + dot(x.astype(BF), a) for x, a in zip(inv, fourth)]
    size = 8
    while size < HALF:
        off = ((r_s // (2 * size)) == (c_s // (2 * size))) & ((r_s // size) > (c_s // size))
        inv_b = [x.astype(BF) for x in inv]
        part = [jnp.where(off, low, 0.0).astype(BF) for low in lowers]
        part = [dot(a, x).astype(BF) for a, x in zip(part, inv_b)]
        inv = [x - dot(xb, a) for x, xb, a in zip(inv, inv_b, part)]
        size *= 2
    inv_b = [x.astype(BF) for x in inv]
    gap = [
        eye_s - xb.astype(F32) - dot_left(low, xb) for low, xb in zip(lowers, inv_b)
    ]
    inv = [xb.astype(F32) + dot(xb, g.astype(BF)) for xb, g in zip(inv_b, gap)]

    eye_k = jnp.where(r_s == c_s, 1.0, 0.0).astype(F32)
    solved = []
    for head in range(2):
        b = rate[head]
        grow = b * jnp.exp(sums[head]) * scale
        right = jnp.concatenate(
            [grow * keys_f, b * values[:, head * DV : (head + 1) * DV]], axis=1
        )
        top = dot_fine(inv[2 * head], right[:HALF])
        solved.append((top, right[HALF:]))
    for head in range(2):
        top, below = solved[head]
        below = below - dot_fine(corners[head], top)
        below = dot_fine(inv[2 * head + 1], below)
        solved[head] = jnp.concatenate([top, below], axis=0)
    maps = []
    for head in range(2):
        closing = sums[head][TOK - 1 :, :]
        weight = scale * jnp.exp(closing - sums[head])
        moved = dot_right(keys, weight * solved[head], ((0,), (0,)))
        transit = eye_k * jnp.exp(closing) - moved[:, :DK]
        maps.append(jnp.concatenate([transit, moved[:, DK:]], axis=1).astype(BF))
    for place in range(maps_ref.shape[0]):
        maps_ref[place] = maps[place % 2]
    for head in range(2):
        solved_ref[head] = solved[head]
    copies[4].wait()


def read_kernel(
    q_ref, k_ref, decay_ref, gate_ref, gain_ref, solved_ref, keep_ref, send_ref
):
    core = places()[2]
    queries = q_ref[...]
    keys = k_ref[...]
    row, col = grid_iota(TOK, TOK)
    eye = row == col
    inclusive = row >= col
    unit_q = unit_scale(queries)
    scores = dot(queries, keys, ((1,), (1,))) * unit_q * to_row(eye, unit_scale(keys))
    sums = decay_sums(decay_ref[...])
    read = []
    for head in range(2):
        sum_row, sum_column = sums[head]
        fall = jnp.exp(jnp.minimum(sum_column - sum_row, 0.0))
        weights = jnp.where(inclusive, scores * fall, 0.0)
        both = dot_fine(weights, solved_ref[head])
        outer = jnp.exp(sum_column) * unit_q * queries.astype(F32) - both[:, :DK]
        gate = gate_ref[:, head * DV : (head + 1) * DV].astype(F32)
        gated = gain_ref[...] * (gate / (1.0 + jnp.exp(-gate)))
        read.append((both[:, DK:], outer, gated))
    for i in range(3):
        keep_ref[i] = jnp.where(core == 0, read[0][i], read[1][i])
        send_ref[i] = jnp.where(core == 0, read[1][i], read[0][i]).astype(BF)


def after(later_t, later_h, earlier, fine):
    moved = dot_fine(later_t, earlier) if fine else dot_right(later_t, earlier)
    return jnp.concatenate([moved[:, :DK], moved[:, DK:] + later_h], axis=1)


def row_kernel(parts_ref, total_ref, ahead_ref, first_ref):
    x = places()[1]

    def pair(i):
        later = parts_ref[2 * i + 1]
        moved = dot(later[:, :DK], parts_ref[2 * i])
        return jnp.concatenate(
            [moved[:, :DK], moved[:, DK:] + later[:, DK:].astype(F32)], axis=1
        )

    pairs = [pair(i) for i in range(4)]
    upto2 = pairs[0]
    upto4 = after(pairs[1][:, :DK], pairs[1][:, DK:], upto2, True)
    last2 = after(pairs[3][:, :DK], pairs[3][:, DK:], pairs[2], True)
    upto6 = after(pairs[2][:, :DK], pairs[2][:, DK:], upto4, True)
    total = after(last2[:, :DK], last2[:, DK:], upto4, True).astype(BF)
    for place in range(4):
        total_ref[place] = total
    row, col = grid_iota(DK, DK + DV)
    none = jnp.where(row == col, 1.0, 0.0).astype(F32)
    ahead_ref[...] = jnp.where(
        x == 0, none, jnp.where(x == 1, upto2, jnp.where(x == 2, upto4, upto6))
    )
    first_ref[...] = parts_ref[2 * x]


def token_of(group, label):
    return 4 * group + (label if group < 2 else 3 - label)


def out_kernel(rows_ref, ahead_ref, first_ref, keep_ref, came_ref, out_ref):
    y, _, core = places()

    def onward(later, state):
        return dot_right(later[:, :DK], state) + later[:, DK:].astype(F32)

    one = rows_ref[0][:, DK:].astype(F32)
    two = onward(rows_ref[1], one)
    three = onward(rows_ref[2], two)
    start = jnp.where(
        y == 0, jnp.zeros_like(one), jnp.where(y == 1, one, jnp.where(y == 2, two, three))
    )
    ahead = ahead_ref[...]
    chip = dot_fine(ahead[:, :DK], start) + ahead[:, DK:]
    second = onward(first_ref[...], chip)

    def finish(state, inner, outer, gated):
        reached = inner + dot_left(outer, state.astype(BF))
        mean = jnp.sum(reached * reached, axis=1, keepdims=True) * (1.0 / DV)
        return (reached * lax.rsqrt(mean + 1e-06) * gated).astype(BF)

    own = finish(jnp.where(core == 0, chip, second), keep_ref[0], keep_ref[1], keep_ref[2])
    came = [came_ref[i].astype(F32) for i in range(3)]
    other = finish(jnp.where(core == 0, second, chip), *came)
    shards = (jnp.where(core == 0, own, other), jnp.where(core == 0, other, own))
    for label in range(4):
        for shard in range(2):
            for group in range(4):
                source = 16 * token_of(group, label)
                target = 64 * shard + 16 * group
                piece = shards[shard][source : source + 16]
                for side in range(2):
                    out_ref[4 * side + label, target : target + 16] = piece


def project_kernel(normed_ref, w0_ref, w1_ref, w2_ref, w3_ref, keep_ref, send_ref):
    _, _, core = places()
    along = lax.axis_index("tp")
    weights = [ref[...] for ref in (w0_ref, w1_ref, w2_ref, w3_ref)]
    for side in range(2):
        total = None
        for i, weight in enumerate(weights):
            near = (along % 4) ^ i
            label = jnp.where(along < 8, near, 3 - near)
            term = dot(normed_ref[4 * side + label], weight)
            total = term if total is None else total + term
        keep_ref[side] = jnp.where(core == 0, total[:64], total[64:])
        send_ref[side] = jnp.where(core == 0, total[64:], total[:64]).astype(BF)


def join_kernel(keep_ref, came_ref, out_ref):
    for side in range(2):
        total = (keep_ref[side] + came_ref[side].astype(F32)).astype(BF)
        for group in range(4):
            out_ref[4 * side + group] = total[16 * group : 16 * (group + 1)]


def sum_kernel(parts_ref, out_ref):
    columns = parts_ref.shape[2]
    for side in range(2):
        total = parts_ref[4 * side].astype(F32)
        for group in range(1, 4):
            total = total + parts_ref[4 * side + group].astype(F32)
        out_ref[:, side * columns : (side + 1) * columns] = total.astype(BF)


def places():
    at = lax.axis_index("ctx")
    return at // 8, (at // 2) % 4, at % 2


def in_vmem():
    return pl.BlockSpec(memory_space=pltpu.VMEM)


def in_hbm():
    return pl.BlockSpec(memory_space=pltpu.HBM)


def call(kernel, outs, *args, flops=10**3, name=None, ins=None, out_specs=None, scratch=(), room=32):
    if ins is None:
        ins = [in_vmem()] * len(args)
    return pl.pallas_call(
        kernel,
        out_shape=outs,
        in_specs=ins,
        out_specs=jax.tree.map(lambda _: in_vmem(), outs) if out_specs is None else out_specs,
        scratch_shapes=scratch,
        compiler_params=pltpu.CompilerParams(vmem_limit_bytes=room * 1024 * 1024),
        cost_estimate=pl.CostEstimate(flops=flops, bytes_accessed=10**3, transcendentals=0),
        name=name,
    )(*args)


def shape(dims, kind):
    return jax.ShapeDtypeStruct(dims, kind)


def local(
    queries, key_vectors, value_vectors, output_gate, write_rate, log_decay, norm_gain, out_weight
):
    width = out_weight.shape[1]
    half_width = width // 2
    rate, decay = write_rate.T, log_decay.T

    maps, solved, w0 = call(
        map_kernel,
        (
            shape((8, DK, DK + DV), BF),
            shape((2, TOK, DK + DV), F32),
            shape((DV, half_width), BF),
        ),
        key_vectors,
        value_vectors,
        rate,
        decay,
        out_weight,
        ins=[in_hbm()] * 5,
        out_specs=(in_vmem(), in_vmem(), in_vmem()),
        scratch=[
            pltpu.VMEM((TOK, DK), BF),
            pltpu.VMEM((TOK, 2 * DV), BF),
            pltpu.VMEM((2, TOK), F32),
            pltpu.VMEM((2, TOK), F32),
            pltpu.SemaphoreType.DMA((5,)),
        ],
        flops=10**9,
        room=60,
        name="shard_maps",
    )
    lines = [[8 * y + i for i in range(8)] for y in range(4)]
    parts = lax.all_to_all(maps, "ctx", 0, 0, axis_index_groups=lines)
    keep, send = call(
        read_kernel,
        (shape((3, TOK, DV), F32), shape((3, TOK, DV), BF)),
        queries,
        key_vectors,
        decay,
        output_gate,
        norm_gain.reshape(1, DV),
        solved,
        flops=10**9,
        name="read_parts",
    )
    across = [(i, i ^ 1) for i in range(32)]
    came = lax.ppermute(send, "ctx", across)

    w1 = lax.ppermute(w0, "tp", [(j, j ^ 1) for j in range(16)])
    w2 = lax.ppermute(w0, "tp", [(j, j ^ 2) for j in range(16)])

    total, ahead, first = call(
        row_kernel,
        (shape((4, DK, DK + DV), BF), shape((DK, DK + DV), F32), shape((DK, DK + DV), BF)),
        parts,
        name="row_maps",
    )
    w2, ahead = lax.optimization_barrier((w2, ahead))
    w3 = lax.ppermute(w2, "tp", [(j, j ^ 1) for j in range(16)])
    columns = [[8 * y + i for y in range(4)] for i in range(8)]
    rows = lax.all_to_all(total, "ctx", 0, 0, axis_index_groups=columns)
    rows, w1 = lax.optimization_barrier((rows, w1))
    normed = call(
        out_kernel,
        shape((8, 128, DV), BF),
        rows,
        ahead,
        first,
        keep,
        came,
        name="gated_norm",
    )
    pairs = [[8 * y + 4 * pair + 2 * side + core for side in range(2)]
             for y in range(4) for pair in range(2) for core in range(2)]
    close = [[16 * at + token_of(g, m) for at in pair for m in range(4)]
             for pair in pairs for g in range(4)]
    far = [[16 * at + token_of(g, m) for at in pair for g in range(4)]
           for pair in pairs for m in range(4)]
    both = ("ctx", "tp")
    normed, w3 = lax.optimization_barrier((normed, w3))
    gathered = lax.all_to_all(normed, both, 0, 0, axis_index_groups=close)
    part, other_part = call(
        project_kernel,
        (shape((2, 64, half_width), F32), shape((2, 64, half_width), BF)),
        gathered,
        w0,
        w1,
        w2,
        w3,
        name="project",
    )
    other_part = lax.ppermute(other_part, "ctx", across)
    partial = call(join_kernel, shape((8, 16, half_width), BF), part, other_part, name="join")
    shares = lax.all_to_all(partial, both, 0, 0, axis_index_groups=far)
    return call(sum_kernel, shape((16, width), BF), shares, name="sum_shares")


def solution(mesh):
    placed = (
        P("ctx", "tp"),
        P("ctx", "tp"),
        P("ctx", "tp"),
        P("ctx", "tp"),
        P("ctx", "tp"),
        P("ctx", "tp"),
        P(),
        P("tp", None),
    )
    return jax.shard_map(
        local, mesh=mesh, in_specs=placed, out_specs=P(("ctx", "tp"), None), check_vma=False
    )
```

```python
import jax
import jax.numpy as jnp
from jax import lax
from jax.experimental import pallas as pl
from jax.experimental.pallas import tpu as pltpu
from jax.sharding import PartitionSpec as P

F32 = jnp.float32
BF = jnp.bfloat16
TOK = 256
DK = 128
DV = 128
HALF = 128


def dot(a, b, dims=((1,), (0,))):
    return lax.dot_general(a, b, (dims, ((), ())), preferred_element_type=F32)


def split(a):
    hi = a.astype(BF)
    return hi, (a - hi.astype(F32)).astype(BF)


def dot_fine(a, b, dims=((1,), (0,))):
    ah, al = split(a)
    bh, bl = split(b)
    return dot(ah, bh, dims) + (dot(ah, bl, dims) + dot(al, bh, dims))


def dot_left(a, b, dims=((1,), (0,))):
    ah, al = split(a)
    return dot(ah, b, dims) + dot(al, b, dims)


def dot_right(a, b, dims=((1,), (0,))):
    bh, bl = split(b)
    return dot(a, bh, dims) + dot(a, bl, dims)


def grid_iota(rows, cols):
    return (
        lax.broadcasted_iota(jnp.int32, (rows, cols), 0),
        lax.broadcasted_iota(jnp.int32, (rows, cols), 1),
    )


def to_row(eye, column):
    return jnp.sum(jnp.where(eye, column, 0.0), axis=0, keepdims=True)


def to_column(eye, row):
    return jnp.sum(jnp.where(eye, row, 0.0), axis=1, keepdims=True)


def decay_sums(decay):
    row, col = grid_iota(TOK, TOK)
    ones = jnp.where(row <= col, 1.0, 0.0).astype(BF)
    eye = row == col
    hi = decay.astype(BF).astype(F32)
    rest = decay - hi
    mid = rest.astype(BF).astype(F32)
    low = rest - mid
    parts = jnp.concatenate([hi, mid, low, jnp.zeros((2, TOK), F32)], axis=0)
    sums = dot(parts.astype(BF), ones)
    rows = sums[0:2] + (sums[2:4] + sums[4:6])
    return [(rows[h : h + 1], to_column(eye, rows[h : h + 1])) for h in range(2)]


def unit_scale(source):
    full = source.astype(F32)
    return lax.rsqrt(jnp.sum(full * full, axis=1, keepdims=True) + 1e-06)


def map_kernel(
    k_far,
    v_far,
    rate_far,
    decay_far,
    weight_far,
    maps_ref,
    solved_ref,
    half_ref,
    k_ref,
    v_ref,
    rate_ref,
    decay_ref,
    sems,
):
    _, x, core = places()
    rows, columns = half_ref.shape
    begin = pl.multiple_of(core * rows, rows)
    left = pl.multiple_of((x % 2) * columns, columns)
    copies = [
        pltpu.make_async_copy(k_far, k_ref, sems.at[0]),
        pltpu.make_async_copy(decay_far, decay_ref, sems.at[1]),
        pltpu.make_async_copy(rate_far, rate_ref, sems.at[2]),
        pltpu.make_async_copy(v_far, v_ref, sems.at[3]),
        pltpu.make_async_copy(
            weight_far.at[pl.ds(begin, rows), pl.ds(left, columns)], half_ref, sems.at[4]
        ),
    ]
    for copy in copies:
        copy.start()
    for copy in copies[:4]:
        copy.wait()
    keys = k_ref[...]
    keys_f = keys.astype(F32)
    values = v_ref[...].astype(F32)
    row, col = grid_iota(TOK, TOK)
    eye = row == col
    strict = row > col
    rate = [to_column(eye, rate_ref[h : h + 1, :]) for h in range(2)]
    gram = dot(keys, keys, ((1,), (1,)))
    scale = unit_scale(keys)
    gram = gram * scale * to_row(eye, scale)
    sum_rows, sums = zip(*decay_sums(decay_ref[...]))
    r_s, c_s = grid_iota(HALF, HALF)
    eye_s = jnp.where(r_s == c_s, 1.0, 0.0).astype(F32)

    lowers, corners = [], []
    for head in range(2):
        fall = jnp.exp(jnp.minimum(sums[head] - sum_rows[head], 0.0))
        low = jnp.where(strict, rate[head] * gram * fall, 0.0)
        lowers += [low[:HALF, :HALF], low[HALF:, HALF:]]
        corners.append(low[HALF:, :HALF])

    small = (r_s // 8) == (c_s // 8)
    first = [jnp.where(small, low, 0.0) for low in lowers]
    first_b = [a.astype(BF) for a in first]
    square = [dot(a, a).astype(BF) for a in first_b]
    fourth = [dot(a, a).astype(BF) for a in square]
    inv = [eye_s - a for a in first]
    inv = [x + dot(x.astype(BF), a) for x, a in zip(inv, square)]
    inv = [x + dot(x.astype(BF), a) for x, a in zip(inv, fourth)]
    size = 8
    while size < HALF:
        off = ((r_s // (2 * size)) == (c_s // (2 * size))) & ((r_s // size) > (c_s // size))
        inv_b = [x.astype(BF) for x in inv]
        part = [jnp.where(off, low, 0.0).astype(BF) for low in lowers]
        part = [dot(a, x).astype(BF) for a, x in zip(part, inv_b)]
        inv = [x - dot(xb, a) for x, xb, a in zip(inv, inv_b, part)]
        size *= 2
    inv_b = [x.astype(BF) for x in inv]
    gap = [
        eye_s - xb.astype(F32) - dot_left(low, xb) for low, xb in zip(lowers, inv_b)
    ]
    inv = [xb.astype(F32) + dot(xb, g.astype(BF)) for xb, g in zip(inv_b, gap)]

    eye_k = jnp.where(r_s == c_s, 1.0, 0.0).astype(F32)
    solved = []
    for head in range(2):
        b = rate[head]
        grow = b * jnp.exp(sums[head]) * scale
        right = jnp.concatenate(
            [grow * keys_f, b * values[:, head * DV : (head + 1) * DV]], axis=1
        )
        top = dot_fine(inv[2 * head], right[:HALF])
        solved.append((top, right[HALF:]))
    for head in range(2):
        top, below = solved[head]
        below = below - dot_fine(corners[head], top)
        below = dot_fine(inv[2 * head + 1], below)
        solved[head] = jnp.concatenate([top, below], axis=0)
    maps = []
    for head in range(2):
        closing = sums[head][TOK - 1 :, :]
        weight = scale * jnp.exp(closing - sums[head])
        moved = dot_right(keys, weight * solved[head], ((0,), (0,)))
        transit = eye_k * jnp.exp(closing) - moved[:, :DK]
        maps.append(jnp.concatenate([transit, moved[:, DK:]], axis=1).astype(BF))
    for place in range(maps_ref.shape[0]):
        maps_ref[place] = maps[place % 2]
    for head in range(2):
        solved_ref[head] = solved[head]
    copies[4].wait()


def read_kernel(
    q_ref, k_ref, decay_ref, gate_ref, gain_ref, solved_ref, keep_ref, send_ref
):
    core = places()[2]
    queries = q_ref[...]
    keys = k_ref[...]
    row, col = grid_iota(TOK, TOK)
    eye = row == col
    inclusive = row >= col
    unit_q = unit_scale(queries)
    scores = dot(queries, keys, ((1,), (1,))) * unit_q * to_row(eye, unit_scale(keys))
    sums = decay_sums(decay_ref[...])
    read = []
    for head in range(2):
        sum_row, sum_column = sums[head]
        fall = jnp.exp(jnp.minimum(sum_column - sum_row, 0.0))
        weights = jnp.where(inclusive, scores * fall, 0.0)
        both = dot_fine(weights, solved_ref[head])
        outer = jnp.exp(sum_column) * unit_q * queries.astype(F32) - both[:, :DK]
        gate = gate_ref[:, head * DV : (head + 1) * DV].astype(F32)
        gated = gain_ref[...] * (gate / (1.0 + jnp.exp(-gate)))
        read.append((both[:, DK:], outer, gated))
    for i in range(3):
        keep_ref[i] = jnp.where(core == 0, read[0][i], read[1][i])
        send_ref[i] = jnp.where(core == 0, read[1][i], read[0][i]).astype(BF)


def after(later_t, later_h, earlier, fine):
    moved = dot_fine(later_t, earlier) if fine else dot_right(later_t, earlier)
    return jnp.concatenate([moved[:, :DK], moved[:, DK:] + later_h], axis=1)


def row_kernel(parts_ref, total_ref, ahead_ref, first_ref):
    x = places()[1]

    def pair(i):
        later = parts_ref[2 * i + 1]
        moved = dot(later[:, :DK], parts_ref[2 * i])
        return jnp.concatenate(
            [moved[:, :DK], moved[:, DK:] + later[:, DK:].astype(F32)], axis=1
        )

    pairs = [pair(i) for i in range(4)]
    upto2 = pairs[0]
    upto4 = after(pairs[1][:, :DK], pairs[1][:, DK:], upto2, True)
    last2 = after(pairs[3][:, :DK], pairs[3][:, DK:], pairs[2], True)
    upto6 = after(pairs[2][:, :DK], pairs[2][:, DK:], upto4, True)
    total = after(last2[:, :DK], last2[:, DK:], upto4, True).astype(BF)
    for place in range(4):
        total_ref[place] = total
    row, col = grid_iota(DK, DK + DV)
    none = jnp.where(row == col, 1.0, 0.0).astype(F32)
    ahead_ref[...] = jnp.where(
        x == 0, none, jnp.where(x == 1, upto2, jnp.where(x == 2, upto4, upto6))
    )
    first_ref[...] = parts_ref[2 * x]


def token_of(group, label):
    return 4 * group + (label if group < 2 else 3 - label)


def out_kernel(rows_ref, ahead_ref, first_ref, keep_ref, came_ref, out_ref):
    y, _, core = places()

    def onward(later, state):
        return dot_right(later[:, :DK], state) + later[:, DK:].astype(F32)

    one = rows_ref[0][:, DK:].astype(F32)
    two = onward(rows_ref[1], one)
    three = onward(rows_ref[2], two)
    start = jnp.where(
        y == 0, jnp.zeros_like(one), jnp.where(y == 1, one, jnp.where(y == 2, two, three))
    )
    ahead = ahead_ref[...]
    chip = dot_fine(ahead[:, :DK], start) + ahead[:, DK:]
    second = onward(first_ref[...], chip)

    def finish(state, inner, outer, gated):
        reached = inner + dot_left(outer, state.astype(BF))
        mean = jnp.sum(reached * reached, axis=1, keepdims=True) * (1.0 / DV)
        return (reached * lax.rsqrt(mean + 1e-06) * gated).astype(BF)

    own = finish(jnp.where(core == 0, chip, second), keep_ref[0], keep_ref[1], keep_ref[2])
    came = [came_ref[i].astype(F32) for i in range(3)]
    other = finish(jnp.where(core == 0, second, chip), *came)
    shards = (jnp.where(core == 0, own, other), jnp.where(core == 0, other, own))
    for label in range(4):
        for shard in range(2):
            for group in range(4):
                source = 16 * token_of(group, label)
                target = 64 * shard + 16 * group
                piece = shards[shard][source : source + 16]
                for side in range(2):
                    out_ref[4 * side + label, target : target + 16] = piece


def project_kernel(normed_ref, w0_ref, w1_ref, w2_ref, w3_ref, keep_ref, send_ref):
    _, _, core = places()
    along = lax.axis_index("tp")
    weights = [ref[...] for ref in (w0_ref, w1_ref, w2_ref, w3_ref)]
    for side in range(2):
        total = None
        for i, weight in enumerate(weights):
            near = (along % 4) ^ i
            label = jnp.where(along < 8, near, 3 - near)
            term = dot(normed_ref[4 * side + label], weight)
            total = term if total is None else total + term
        keep_ref[side] = jnp.where(core == 0, total[:64], total[64:])
        send_ref[side] = jnp.where(core == 0, total[64:], total[:64]).astype(BF)


def join_kernel(keep_ref, came_ref, out_ref):
    for side in range(2):
        total = (keep_ref[side] + came_ref[side].astype(F32)).astype(BF)
        for group in range(4):
            out_ref[4 * side + group] = total[16 * group : 16 * (group + 1)]


def sum_kernel(parts_ref, out_ref):
    columns = parts_ref.shape[2]
    for side in range(2):
        total = parts_ref[4 * side].astype(F32)
        for group in range(1, 4):
            total = total + parts_ref[4 * side + group].astype(F32)
        out_ref[:, side * columns : (side + 1) * columns] = total.astype(BF)


def places():
    at = lax.axis_index("ctx")
    return at // 8, (at // 2) % 4, at % 2


def in_vmem():
    return pl.BlockSpec(memory_space=pltpu.VMEM)


def in_hbm():
    return pl.BlockSpec(memory_space=pltpu.HBM)


def call(kernel, outs, *args, flops=10**3, name=None, ins=None, out_specs=None, scratch=(), room=32):
    if ins is None:
        ins = [in_vmem()] * len(args)
    return pl.pallas_call(
        kernel,
        out_shape=outs,
        in_specs=ins,
        out_specs=jax.tree.map(lambda _: in_vmem(), outs) if out_specs is None else out_specs,
        scratch_shapes=scratch,
        compiler_params=pltpu.CompilerParams(vmem_limit_bytes=room * 1024 * 1024),
        cost_estimate=pl.CostEstimate(flops=flops, bytes_accessed=10**3, transcendentals=0),
        name=name,
    )(*args)


def shape(dims, kind):
    return jax.ShapeDtypeStruct(dims, kind)


def local(
    queries, key_vectors, value_vectors, output_gate, write_rate, log_decay, norm_gain, out_weight
):
    width = out_weight.shape[1]
    half_width = width // 2
    rate, decay = write_rate.T, log_decay.T

    maps, solved, w0 = call(
        map_kernel,
        (
            shape((8, DK, DK + DV), BF),
            shape((2, TOK, DK + DV), F32),
            shape((DV, half_width), BF),
        ),
        key_vectors,
        value_vectors,
        rate,
        decay,
        out_weight,
        ins=[in_hbm()] * 5,
        out_specs=(in_vmem(), in_vmem(), in_vmem()),
        scratch=[
            pltpu.VMEM((TOK, DK), BF),
            pltpu.VMEM((TOK, 2 * DV), BF),
            pltpu.VMEM((2, TOK), F32),
            pltpu.VMEM((2, TOK), F32),
            pltpu.SemaphoreType.DMA((5,)),
        ],
        flops=10**9,
        room=60,
        name="shard_maps",
    )
    lines = [[8 * y + i for i in range(8)] for y in range(4)]
    parts = lax.all_to_all(maps, "ctx", 0, 0, axis_index_groups=lines)
    keep, send = call(
        read_kernel,
        (shape((3, TOK, DV), F32), shape((3, TOK, DV), BF)),
        queries,
        key_vectors,
        decay,
        output_gate,
        norm_gain.reshape(1, DV),
        solved,
        flops=10**9,
        name="read_parts",
    )
    across = [(i, i ^ 1) for i in range(32)]
    came = lax.ppermute(send, "ctx", across)

    w1 = lax.ppermute(w0, "tp", [(j, j ^ 1) for j in range(16)])
    w2 = lax.ppermute(w0, "tp", [(j, j ^ 2) for j in range(16)])

    parts, keep, send = lax.optimization_barrier((parts, keep, send))
    total, ahead, first = call(
        row_kernel,
        (shape((4, DK, DK + DV), BF), shape((DK, DK + DV), F32), shape((DK, DK + DV), BF)),
        parts,
        name="row_maps",
    )
    w2, ahead = lax.optimization_barrier((w2, ahead))
    w3 = lax.ppermute(w2, "tp", [(j, j ^ 1) for j in range(16)])
    columns = [[8 * y + i for y in range(4)] for i in range(8)]
    rows = lax.all_to_all(total, "ctx", 0, 0, axis_index_groups=columns)
    rows, w1 = lax.optimization_barrier((rows, w1))
    normed = call(
        out_kernel,
        shape((8, 128, DV), BF),
        rows,
        ahead,
        first,
        keep,
        came,
        flops=10**9,
        name="gated_norm",
    )
    pairs = [[8 * y + 4 * pair + 2 * side + core for side in range(2)]
             for y in range(4) for pair in range(2) for core in range(2)]
    close = [[16 * at + token_of(g, m) for at in pair for m in range(4)]
             for pair in pairs for g in range(4)]
    far = [[16 * at + token_of(g, m) for at in pair for g in range(4)]
           for pair in pairs for m in range(4)]
    both = ("ctx", "tp")
    normed, w3 = lax.optimization_barrier((normed, w3))
    gathered = lax.all_to_all(normed, both, 0, 0, axis_index_groups=close)
    part, other_part = call(
        project_kernel,
        (shape((2, 64, half_width), F32), shape((2, 64, half_width), BF)),
        gathered,
        w0,
        w1,
        w2,
        w3,
        name="project",
    )
    other_part = lax.ppermute(other_part, "ctx", across)
    partial = call(join_kernel, shape((8, 16, half_width), BF), part, other_part, name="join")
    shares = lax.all_to_all(partial, both, 0, 0, axis_index_groups=far)
    return call(sum_kernel, shape((16, width), BF), shares, name="sum_shares")


def solution(mesh):
    placed = (
        P("ctx", "tp"),
        P("ctx", "tp"),
        P("ctx", "tp"),
        P("ctx", "tp"),
        P("ctx", "tp"),
        P("ctx", "tp"),
        P(),
        P("tp", None),
    )
    return jax.shard_map(
        local, mesh=mesh, in_specs=placed, out_specs=P(("ctx", "tp"), None), check_vma=False
    )
```

```python
import jax
import jax.numpy as jnp
from jax import lax
from jax.experimental import pallas as pl
from jax.experimental.pallas import tpu as pltpu
from jax.sharding import PartitionSpec as P

F32 = jnp.float32
BF = jnp.bfloat16
TOK = 256
DK = 128
DV = 128
HALF = 128


def dot(a, b, dims=((1,), (0,))):
    return lax.dot_general(a, b, (dims, ((), ())), preferred_element_type=F32)


def split(a):
    hi = a.astype(BF)
    return hi, (a - hi.astype(F32)).astype(BF)


def dot_fine(a, b, dims=((1,), (0,))):
    ah, al = split(a)
    bh, bl = split(b)
    return dot(ah, bh, dims) + (dot(ah, bl, dims) + dot(al, bh, dims))


def dot_left(a, b, dims=((1,), (0,))):
    ah, al = split(a)
    return dot(ah, b, dims) + dot(al, b, dims)


def dot_right(a, b, dims=((1,), (0,))):
    bh, bl = split(b)
    return dot(a, bh, dims) + dot(a, bl, dims)


def grid_iota(rows, cols):
    return (
        lax.broadcasted_iota(jnp.int32, (rows, cols), 0),
        lax.broadcasted_iota(jnp.int32, (rows, cols), 1),
    )


def to_row(eye, column):
    return jnp.sum(jnp.where(eye, column, 0.0), axis=0, keepdims=True)


def to_column(eye, row):
    return jnp.sum(jnp.where(eye, row, 0.0), axis=1, keepdims=True)


def decay_sums(decay):
    row, col = grid_iota(TOK, TOK)
    ones = jnp.where(row <= col, 1.0, 0.0).astype(BF)
    eye = row == col
    hi = decay.astype(BF).astype(F32)
    rest = decay - hi
    mid = rest.astype(BF).astype(F32)
    low = rest - mid
    parts = jnp.concatenate([hi, mid, low, jnp.zeros((2, TOK), F32)], axis=0)
    sums = dot(parts.astype(BF), ones)
    rows = sums[0:2] + (sums[2:4] + sums[4:6])
    return [(rows[h : h + 1], to_column(eye, rows[h : h + 1])) for h in range(2)]


def unit_scale(source):
    full = source.astype(F32)
    return lax.rsqrt(jnp.sum(full * full, axis=1, keepdims=True) + 1e-06)


def map_kernel(
    k_far,
    v_far,
    rate_far,
    decay_far,
    weight_far,
    maps_ref,
    solved_ref,
    half_ref,
    k_ref,
    v_ref,
    rate_ref,
    decay_ref,
    sems,
):
    _, x, core = places()
    rows, columns = half_ref.shape
    begin = pl.multiple_of(core * rows, rows)
    left = pl.multiple_of((x % 2) * columns, columns)
    copies = [
        pltpu.make_async_copy(k_far, k_ref, sems.at[0]),
        pltpu.make_async_copy(decay_far, decay_ref, sems.at[1]),
        pltpu.make_async_copy(rate_far, rate_ref, sems.at[2]),
        pltpu.make_async_copy(v_far, v_ref, sems.at[3]),
        pltpu.make_async_copy(
            weight_far.at[pl.ds(begin, rows), pl.ds(left, columns)], half_ref, sems.at[4]
        ),
    ]
    for copy in copies:
        copy.start()
    for copy in copies[:4]:
        copy.wait()
    keys = k_ref[...]
    keys_f = keys.astype(F32)
    values = v_ref[...].astype(F32)
    row, col = grid_iota(TOK, TOK)
    eye = row == col
    strict = row > col
    rate = [to_column(eye, rate_ref[h : h + 1, :]) for h in range(2)]
    gram = dot(keys, keys, ((1,), (1,)))
    scale = unit_scale(keys)
    gram = gram * scale * to_row(eye, scale)
    sum_rows, sums = zip(*decay_sums(decay_ref[...]))
    r_s, c_s = grid_iota(HALF, HALF)
    eye_s = jnp.where(r_s == c_s, 1.0, 0.0).astype(F32)

    lowers, corners = [], []
    for head in range(2):
        fall = jnp.exp(jnp.minimum(sums[head] - sum_rows[head], 0.0))
        low = jnp.where(strict, rate[head] * gram * fall, 0.0)
        lowers += [low[:HALF, :HALF], low[HALF:, HALF:]]
        corners.append(low[HALF:, :HALF])

    small = (r_s // 8) == (c_s // 8)
    first = [jnp.where(small, low, 0.0) for low in lowers]
    first_b = [a.astype(BF) for a in first]
    square = [dot(a, a).astype(BF) for a in first_b]
    fourth = [dot(a, a).astype(BF) for a in square]
    inv = [eye_s - a for a in first]
    inv = [x + dot(x.astype(BF), a) for x, a in zip(inv, square)]
    inv = [x + dot(x.astype(BF), a) for x, a in zip(inv, fourth)]
    size = 8
    while size < HALF:
        off = ((r_s // (2 * size)) == (c_s // (2 * size))) & ((r_s // size) > (c_s // size))
        inv_b = [x.astype(BF) for x in inv]
        part = [jnp.where(off, low, 0.0).astype(BF) for low in lowers]
        part = [dot(a, x).astype(BF) for a, x in zip(part, inv_b)]
        inv = [x - dot(xb, a) for x, xb, a in zip(inv, inv_b, part)]
        size *= 2
    inv_b = [x.astype(BF) for x in inv]
    gap = [
        eye_s - xb.astype(F32) - dot_left(low, xb) for low, xb in zip(lowers, inv_b)
    ]
    inv = [xb.astype(F32) + dot(xb, g.astype(BF)) for xb, g in zip(inv_b, gap)]

    eye_k = jnp.where(r_s == c_s, 1.0, 0.0).astype(F32)
    solved = []
    for head in range(2):
        b = rate[head]
        grow = b * jnp.exp(sums[head]) * scale
        right = jnp.concatenate(
            [grow * keys_f, b * values[:, head * DV : (head + 1) * DV]], axis=1
        )
        top = dot_fine(inv[2 * head], right[:HALF])
        solved.append((top, right[HALF:]))
    for head in range(2):
        top, below = solved[head]
        below = below - dot_fine(corners[head], top)
        below = dot_fine(inv[2 * head + 1], below)
        solved[head] = jnp.concatenate([top, below], axis=0)
    maps = []
    for head in range(2):
        closing = sums[head][TOK - 1 :, :]
        weight = scale * jnp.exp(closing - sums[head])
        moved = dot_right(keys, weight * solved[head], ((0,), (0,)))
        transit = eye_k * jnp.exp(closing) - moved[:, :DK]
        maps.append(jnp.concatenate([transit, moved[:, DK:]], axis=1).astype(BF))
    for place in range(maps_ref.shape[0]):
        maps_ref[place] = maps[place % 2]
    for head in range(2):
        solved_ref[head] = solved[head]
    copies[4].wait()


def read_kernel(
    q_ref, k_ref, decay_ref, gate_ref, gain_ref, solved_ref, keep_ref, send_ref
):
    core = places()[2]
    queries = q_ref[...]
    keys = k_ref[...]
    row, col = grid_iota(TOK, TOK)
    eye = row == col
    inclusive = row >= col
    unit_q = unit_scale(queries)
    scores = dot(queries, keys, ((1,), (1,))) * unit_q * to_row(eye, unit_scale(keys))
    sums = decay_sums(decay_ref[...])
    read = []
    for head in range(2):
        sum_row, sum_column = sums[head]
        fall = jnp.exp(jnp.minimum(sum_column - sum_row, 0.0))
        weights = jnp.where(inclusive, scores * fall, 0.0)
        both = dot_fine(weights, solved_ref[head])
        outer = jnp.exp(sum_column) * unit_q * queries.astype(F32) - both[:, :DK]
        gate = gate_ref[:, head * DV : (head + 1) * DV].astype(F32)
        gated = gain_ref[...] * (gate / (1.0 + jnp.exp(-gate)))
        read.append((both[:, DK:], outer, gated))
    for i in range(3):
        keep_ref[i] = jnp.where(core == 0, read[0][i], read[1][i])
        send_ref[i] = jnp.where(core == 0, read[1][i], read[0][i]).astype(BF)


def after(later_t, later_h, earlier, fine):
    moved = dot_fine(later_t, earlier) if fine else dot_right(later_t, earlier)
    return jnp.concatenate([moved[:, :DK], moved[:, DK:] + later_h], axis=1)


def row_kernel(parts_ref, total_ref, ahead_ref, first_ref):
    x = places()[1]

    def pair(i):
        later = parts_ref[2 * i + 1]
        moved = dot(later[:, :DK], parts_ref[2 * i])
        return jnp.concatenate(
            [moved[:, :DK], moved[:, DK:] + later[:, DK:].astype(F32)], axis=1
        )

    pairs = [pair(i) for i in range(4)]
    upto2 = pairs[0]
    upto4 = after(pairs[1][:, :DK], pairs[1][:, DK:], upto2, True)
    last2 = after(pairs[3][:, :DK], pairs[3][:, DK:], pairs[2], True)
    upto6 = after(pairs[2][:, :DK], pairs[2][:, DK:], upto4, True)
    total = after(last2[:, :DK], last2[:, DK:], upto4, True).astype(BF)
    for place in range(4):
        total_ref[place] = total
    row, col = grid_iota(DK, DK + DV)
    none = jnp.where(row == col, 1.0, 0.0).astype(F32)
    ahead_ref[...] = jnp.where(
        x == 0, none, jnp.where(x == 1, upto2, jnp.where(x == 2, upto4, upto6))
    )
    first_ref[...] = parts_ref[2 * x]


def token_of(group, label):
    return 4 * group + (label if group < 2 else 3 - label)


def out_kernel(rows_ref, ahead_ref, first_ref, keep_ref, came_ref, out_ref):
    y, _, core = places()

    def onward(later, state):
        return dot_right(later[:, :DK], state) + later[:, DK:].astype(F32)

    one = rows_ref[0][:, DK:].astype(F32)
    two = onward(rows_ref[1], one)
    three = onward(rows_ref[2], two)
    start = jnp.where(
        y == 0, jnp.zeros_like(one), jnp.where(y == 1, one, jnp.where(y == 2, two, three))
    )
    ahead = ahead_ref[...]
    chip = dot_fine(ahead[:, :DK], start) + ahead[:, DK:]
    second = onward(first_ref[...], chip)

    def finish(state, inner, outer, gated):
        reached = inner + dot_left(outer, state.astype(BF))
        mean = jnp.sum(reached * reached, axis=1, keepdims=True) * (1.0 / DV)
        return (reached * lax.rsqrt(mean + 1e-06) * gated).astype(BF)

    own = finish(jnp.where(core == 0, chip, second), keep_ref[0], keep_ref[1], keep_ref[2])
    came = [came_ref[i].astype(F32) for i in range(3)]
    other = finish(jnp.where(core == 0, second, chip), *came)
    shards = (jnp.where(core == 0, own, other), jnp.where(core == 0, other, own))
    for label in range(4):
        for shard in range(2):
            for group in range(4):
                source = 16 * token_of(group, label)
                target = 64 * shard + 16 * group
                piece = shards[shard][source : source + 16]
                for side in range(2):
                    out_ref[4 * side + label, target : target + 16] = piece


def project_kernel(normed_ref, w0_ref, w1_ref, w2_ref, w3_ref, keep_ref, send_ref):
    _, _, core = places()
    along = lax.axis_index("tp")
    weights = [ref[...] for ref in (w0_ref, w1_ref, w2_ref, w3_ref)]
    for side in range(2):
        total = None
        for i, weight in enumerate(weights):
            near = (along % 4) ^ i
            label = jnp.where(along < 8, near, 3 - near)
            term = dot(normed_ref[4 * side + label], weight)
            total = term if total is None else total + term
        keep_ref[side] = jnp.where(core == 0, total[:64], total[64:])
        send_ref[side] = jnp.where(core == 0, total[64:], total[:64]).astype(BF)


def join_kernel(keep_ref, came_ref, out_ref):
    for side in range(2):
        total = (keep_ref[side] + came_ref[side].astype(F32)).astype(BF)
        for group in range(4):
            out_ref[4 * side + group] = total[16 * group : 16 * (group + 1)]


def sum_kernel(parts_ref, out_ref):
    columns = parts_ref.shape[2]
    for side in range(2):
        total = parts_ref[4 * side].astype(F32)
        for group in range(1, 4):
            total = total + parts_ref[4 * side + group].astype(F32)
        out_ref[:, side * columns : (side + 1) * columns] = total.astype(BF)


def places():
    at = lax.axis_index("ctx")
    return at // 8, (at // 2) % 4, at % 2


def in_vmem():
    return pl.BlockSpec(memory_space=pltpu.VMEM)


def in_hbm():
    return pl.BlockSpec(memory_space=pltpu.HBM)


def call(kernel, outs, *args, flops=10**3, name=None, ins=None, out_specs=None, scratch=(), room=32):
    if ins is None:
        ins = [in_vmem()] * len(args)
    return pl.pallas_call(
        kernel,
        out_shape=outs,
        in_specs=ins,
        out_specs=jax.tree.map(lambda _: in_vmem(), outs) if out_specs is None else out_specs,
        scratch_shapes=scratch,
        compiler_params=pltpu.CompilerParams(vmem_limit_bytes=room * 1024 * 1024),
        cost_estimate=pl.CostEstimate(flops=flops, bytes_accessed=10**3, transcendentals=0),
        name=name,
    )(*args)


def shape(dims, kind):
    return jax.ShapeDtypeStruct(dims, kind)


def local(
    queries, key_vectors, value_vectors, output_gate, write_rate, log_decay, norm_gain, out_weight
):
    width = out_weight.shape[1]
    half_width = width // 2
    rate, decay = write_rate.T, log_decay.T

    maps, solved, w0 = call(
        map_kernel,
        (
            shape((8, DK, DK + DV), BF),
            shape((2, TOK, DK + DV), F32),
            shape((DV, half_width), BF),
        ),
        key_vectors,
        value_vectors,
        rate,
        decay,
        out_weight,
        ins=[in_hbm()] * 5,
        out_specs=(in_vmem(), in_vmem(), in_vmem()),
        scratch=[
            pltpu.VMEM((TOK, DK), BF),
            pltpu.VMEM((TOK, 2 * DV), BF),
            pltpu.VMEM((2, TOK), F32),
            pltpu.VMEM((2, TOK), F32),
            pltpu.SemaphoreType.DMA((5,)),
        ],
        flops=10**9,
        room=60,
        name="shard_maps",
    )
    lines = [[8 * y + i for i in range(8)] for y in range(4)]
    parts = lax.all_to_all(maps, "ctx", 0, 0, axis_index_groups=lines)
    keep, send = call(
        read_kernel,
        (shape((3, TOK, DV), F32), shape((3, TOK, DV), BF)),
        queries,
        key_vectors,
        decay,
        output_gate,
        norm_gain.reshape(1, DV),
        solved,
        flops=10**9,
        name="read_parts",
    )
    across = [(i, i ^ 1) for i in range(32)]
    came = lax.ppermute(send, "ctx", across)

    w1 = lax.ppermute(w0, "tp", [(j, j ^ 1) for j in range(16)])
    w2 = lax.ppermute(w0, "tp", [(j, j ^ 2) for j in range(16)])

    parts, keep, came = lax.optimization_barrier((parts, keep, came))
    total, ahead, first = call(
        row_kernel,
        (shape((4, DK, DK + DV), BF), shape((DK, DK + DV), F32), shape((DK, DK + DV), BF)),
        parts,
        name="row_maps",
    )
    w2, ahead = lax.optimization_barrier((w2, ahead))
    w3 = lax.ppermute(w2, "tp", [(j, j ^ 1) for j in range(16)])
    columns = [[8 * y + i for y in range(4)] for i in range(8)]
    rows = lax.all_to_all(total, "ctx", 0, 0, axis_index_groups=columns)
    rows, w1 = lax.optimization_barrier((rows, w1))
    normed = call(
        out_kernel,
        shape((8, 128, DV), BF),
        rows,
        ahead,
        first,
        keep,
        came,
        flops=10**9,
        name="gated_norm",
    )
    pairs = [[8 * y + 4 * pair + 2 * side + core for side in range(2)]
             for y in range(4) for pair in range(2) for core in range(2)]
    close = [[16 * at + token_of(g, m) for at in pair for m in range(4)]
             for pair in pairs for g in range(4)]
    far = [[16 * at + token_of(g, m) for at in pair for g in range(4)]
           for pair in pairs for m in range(4)]
    both = ("ctx", "tp")
    normed, w3 = lax.optimization_barrier((normed, w3))
    gathered = lax.all_to_all(normed, both, 0, 0, axis_index_groups=close)
    part, other_part = call(
        project_kernel,
        (shape((2, 64, half_width), F32), shape((2, 64, half_width), BF)),
        gathered,
        w0,
        w1,
        w2,
        w3,
        name="project",
    )
    other_part = lax.ppermute(other_part, "ctx", across)
    partial = call(join_kernel, shape((8, 16, half_width), BF), part, other_part, name="join")
    shares = lax.all_to_all(partial, both, 0, 0, axis_index_groups=far)
    return call(sum_kernel, shape((16, width), BF), shares, name="sum_shares")


def solution(mesh):
    placed = (
        P("ctx", "tp"),
        P("ctx", "tp"),
        P("ctx", "tp"),
        P("ctx", "tp"),
        P("ctx", "tp"),
        P("ctx", "tp"),
        P(),
        P("tp", None),
    )
    return jax.shard_map(
        local, mesh=mesh, in_specs=placed, out_specs=P(("ctx", "tp"), None), check_vma=False
    )
```

```python
import jax
import jax.numpy as jnp
from jax import lax
from jax.experimental import pallas as pl
from jax.experimental.pallas import tpu as pltpu
from jax.sharding import PartitionSpec as P

F32 = jnp.float32
BF = jnp.bfloat16
TOK = 256
DK = 128
DV = 128
HALF = 128


def dot(a, b, dims=((1,), (0,))):
    return lax.dot_general(a, b, (dims, ((), ())), preferred_element_type=F32)


def split(a):
    hi = a.astype(BF)
    return hi, (a - hi.astype(F32)).astype(BF)


def dot_fine(a, b, dims=((1,), (0,))):
    ah, al = split(a)
    bh, bl = split(b)
    return dot(ah, bh, dims) + (dot(ah, bl, dims) + dot(al, bh, dims))


def dot_left(a, b, dims=((1,), (0,))):
    ah, al = split(a)
    return dot(ah, b, dims) + dot(al, b, dims)


def dot_right(a, b, dims=((1,), (0,))):
    bh, bl = split(b)
    return dot(a, bh, dims) + dot(a, bl, dims)


def grid_iota(rows, cols):
    return (
        lax.broadcasted_iota(jnp.int32, (rows, cols), 0),
        lax.broadcasted_iota(jnp.int32, (rows, cols), 1),
    )


def to_row(eye, column):
    return jnp.sum(jnp.where(eye, column, 0.0), axis=0, keepdims=True)


def to_column(eye, row):
    return jnp.sum(jnp.where(eye, row, 0.0), axis=1, keepdims=True)


def decay_sums(decay):
    row, col = grid_iota(TOK, TOK)
    ones = jnp.where(row <= col, 1.0, 0.0).astype(BF)
    eye = row == col
    hi = decay.astype(BF).astype(F32)
    rest = decay - hi
    mid = rest.astype(BF).astype(F32)
    low = rest - mid
    parts = jnp.concatenate([hi, mid, low, jnp.zeros((2, TOK), F32)], axis=0)
    sums = dot(parts.astype(BF), ones)
    rows = sums[0:2] + (sums[2:4] + sums[4:6])
    return [(rows[h : h + 1], to_column(eye, rows[h : h + 1])) for h in range(2)]


def unit_scale(source):
    full = source.astype(F32)
    return lax.rsqrt(jnp.sum(full * full, axis=1, keepdims=True) + 1e-06)


def map_kernel(
    k_far,
    v_far,
    rate_far,
    decay_far,
    weight_far,
    maps_ref,
    solved_ref,
    half_ref,
    k_ref,
    v_ref,
    rate_ref,
    decay_ref,
    sems,
):
    _, x, core = places()
    rows, columns = half_ref.shape
    begin = pl.multiple_of(core * rows, rows)
    left = pl.multiple_of((x % 2) * columns, columns)
    copies = [
        pltpu.make_async_copy(k_far, k_ref, sems.at[0]),
        pltpu.make_async_copy(decay_far, decay_ref, sems.at[1]),
        pltpu.make_async_copy(rate_far, rate_ref, sems.at[2]),
        pltpu.make_async_copy(v_far, v_ref, sems.at[3]),
        pltpu.make_async_copy(
            weight_far.at[pl.ds(begin, rows), pl.ds(left, columns)], half_ref, sems.at[4]
        ),
    ]
    for copy in copies:
        copy.start()
    for copy in copies[:4]:
        copy.wait()
    keys = k_ref[...]
    keys_f = keys.astype(F32)
    values = v_ref[...].astype(F32)
    row, col = grid_iota(TOK, TOK)
    eye = row == col
    strict = row > col
    rate = [to_column(eye, rate_ref[h : h + 1, :]) for h in range(2)]
    gram = dot(keys, keys, ((1,), (1,)))
    scale = unit_scale(keys)
    gram = gram * scale * to_row(eye, scale)
    sum_rows, sums = zip(*decay_sums(decay_ref[...]))
    r_s, c_s = grid_iota(HALF, HALF)
    eye_s = jnp.where(r_s == c_s, 1.0, 0.0).astype(F32)

    lowers, corners = [], []
    for head in range(2):
        fall = jnp.exp(jnp.minimum(sums[head] - sum_rows[head], 0.0))
        low = jnp.where(strict, rate[head] * gram * fall, 0.0)
        lowers += [low[:HALF, :HALF], low[HALF:, HALF:]]
        corners.append(low[HALF:, :HALF])

    small = (r_s // 8) == (c_s // 8)
    first = [jnp.where(small, low, 0.0) for low in lowers]
    first_b = [a.astype(BF) for a in first]
    square = [dot(a, a).astype(BF) for a in first_b]
    fourth = [dot(a, a).astype(BF) for a in square]
    inv = [eye_s - a for a in first]
    inv = [x + dot(x.astype(BF), a) for x, a in zip(inv, square)]
    inv = [x + dot(x.astype(BF), a) for x, a in zip(inv, fourth)]
    size = 8
    while size < HALF:
        off = ((r_s // (2 * size)) == (c_s // (2 * size))) & ((r_s // size) > (c_s // size))
        inv_b = [x.astype(BF) for x in inv]
        part = [jnp.where(off, low, 0.0).astype(BF) for low in lowers]
        part = [dot(a, x).astype(BF) for a, x in zip(part, inv_b)]
        inv = [x - dot(xb, a) for x, xb, a in zip(inv, inv_b, part)]
        size *= 2
    inv_b = [x.astype(BF) for x in inv]
    gap = [
        eye_s - xb.astype(F32) - dot_left(low, xb) for low, xb in zip(lowers, inv_b)
    ]
    inv = [xb.astype(F32) + dot(xb, g.astype(BF)) for xb, g in zip(inv_b, gap)]

    eye_k = jnp.where(r_s == c_s, 1.0, 0.0).astype(F32)
    solved = []
    for head in range(2):
        b = rate[head]
        grow = b * jnp.exp(sums[head]) * scale
        right = jnp.concatenate(
            [grow * keys_f, b * values[:, head * DV : (head + 1) * DV]], axis=1
        )
        top = dot_fine(inv[2 * head], right[:HALF])
        solved.append((top, right[HALF:]))
    for head in range(2):
        top, below = solved[head]
        below = below - dot_fine(corners[head], top)
        below = dot_fine(inv[2 * head + 1], below)
        solved[head] = jnp.concatenate([top, below], axis=0)
    maps = []
    for head in range(2):
        closing = sums[head][TOK - 1 :, :]
        weight = scale * jnp.exp(closing - sums[head])
        moved = dot_right(keys, weight * solved[head], ((0,), (0,)))
        transit = eye_k * jnp.exp(closing) - moved[:, :DK]
        maps.append(jnp.concatenate([transit, moved[:, DK:]], axis=1).astype(BF))
    for place in range(maps_ref.shape[0]):
        maps_ref[place] = maps[place % 2]
    for head in range(2):
        solved_ref[head] = solved[head]
    copies[4].wait()


def read_kernel(
    q_ref, k_ref, decay_ref, gate_ref, gain_ref, solved_ref, keep_ref, send_ref
):
    core = places()[2]
    queries = q_ref[...]
    keys = k_ref[...]
    row, col = grid_iota(TOK, TOK)
    eye = row == col
    inclusive = row >= col
    unit_q = unit_scale(queries)
    scores = dot(queries, keys, ((1,), (1,))) * unit_q * to_row(eye, unit_scale(keys))
    sums = decay_sums(decay_ref[...])
    read = []
    for head in range(2):
        sum_row, sum_column = sums[head]
        fall = jnp.exp(jnp.minimum(sum_column - sum_row, 0.0))
        weights = jnp.where(inclusive, scores * fall, 0.0)
        both = dot_fine(weights, solved_ref[head])
        outer = jnp.exp(sum_column) * unit_q * queries.astype(F32) - both[:, :DK]
        gate = gate_ref[:, head * DV : (head + 1) * DV].astype(F32)
        gated = gain_ref[...] * (gate / (1.0 + jnp.exp(-gate)))
        read.append((both[:, DK:], outer, gated))
    for i in range(3):
        keep_ref[i] = jnp.where(core == 0, read[0][i], read[1][i])
        send_ref[i] = jnp.where(core == 0, read[1][i], read[0][i]).astype(BF)


def after(later_t, later_h, earlier, fine):
    moved = dot_fine(later_t, earlier) if fine else dot_right(later_t, earlier)
    return jnp.concatenate([moved[:, :DK], moved[:, DK:] + later_h], axis=1)


def row_kernel(parts_ref, total_ref, ahead_ref, first_ref):
    x = places()[1]

    def pair(i):
        later = parts_ref[2 * i + 1]
        moved = dot(later[:, :DK], parts_ref[2 * i])
        return jnp.concatenate(
            [moved[:, :DK], moved[:, DK:] + later[:, DK:].astype(F32)], axis=1
        )

    pairs = [pair(i) for i in range(4)]
    upto2 = pairs[0]
    upto4 = after(pairs[1][:, :DK], pairs[1][:, DK:], upto2, True)
    last2 = after(pairs[3][:, :DK], pairs[3][:, DK:], pairs[2], True)
    upto6 = after(pairs[2][:, :DK], pairs[2][:, DK:], upto4, True)
    total = after(last2[:, :DK], last2[:, DK:], upto4, True).astype(BF)
    for place in range(4):
        total_ref[place] = total
    row, col = grid_iota(DK, DK + DV)
    none = jnp.where(row == col, 1.0, 0.0).astype(F32)
    ahead_ref[...] = jnp.where(
        x == 0, none, jnp.where(x == 1, upto2, jnp.where(x == 2, upto4, upto6))
    )
    first_ref[...] = parts_ref[2 * x]


def token_of(group, label):
    return 4 * group + (label if group < 2 else 3 - label)


def out_kernel(rows_ref, ahead_ref, first_ref, keep_ref, came_ref, out_ref):
    y, _, core = places()

    def onward(later, state):
        return dot_right(later[:, :DK], state) + later[:, DK:].astype(F32)

    one = rows_ref[0][:, DK:].astype(F32)
    two = onward(rows_ref[1], one)
    three = onward(rows_ref[2], two)
    start = jnp.where(
        y == 0, jnp.zeros_like(one), jnp.where(y == 1, one, jnp.where(y == 2, two, three))
    )
    ahead = ahead_ref[...]
    chip = dot_fine(ahead[:, :DK], start) + ahead[:, DK:]
    second = onward(first_ref[...], chip)

    def finish(state, inner, outer, gated):
        reached = inner + dot_left(outer, state.astype(BF))
        mean = jnp.sum(reached * reached, axis=1, keepdims=True) * (1.0 / DV)
        return (reached * lax.rsqrt(mean + 1e-06) * gated).astype(BF)

    own = finish(jnp.where(core == 0, chip, second), keep_ref[0], keep_ref[1], keep_ref[2])
    came = [came_ref[i].astype(F32) for i in range(3)]
    other = finish(jnp.where(core == 0, second, chip), *came)
    shards = (jnp.where(core == 0, own, other), jnp.where(core == 0, other, own))
    for label in range(4):
        for shard in range(2):
            for group in range(4):
                source = 16 * token_of(group, label)
                target = 64 * shard + 16 * group
                piece = shards[shard][source : source + 16]
                for side in range(2):
                    out_ref[4 * side + label, target : target + 16] = piece


def lay_kernel(w1_ref, w3_ref, out_ref):
    out_ref[0] = w1_ref[...]
    out_ref[1] = w3_ref[...]


def project_kernel(normed_ref, w0_ref, w2_ref, far_ref, keep_ref, send_ref):
    _, _, core = places()
    along = lax.axis_index("tp")
    weights = [w0_ref[...], far_ref[0], w2_ref[...], far_ref[1]]
    for side in range(2):
        total = None
        for i, weight in enumerate(weights):
            near = (along % 4) ^ i
            label = jnp.where(along < 8, near, 3 - near)
            term = dot(normed_ref[4 * side + label], weight)
            total = term if total is None else total + term
        keep_ref[side] = jnp.where(core == 0, total[:64], total[64:])
        send_ref[side] = jnp.where(core == 0, total[64:], total[:64]).astype(BF)


def join_kernel(keep_ref, came_ref, out_ref):
    for side in range(2):
        total = (keep_ref[side] + came_ref[side].astype(F32)).astype(BF)
        for group in range(4):
            out_ref[4 * side + group] = total[16 * group : 16 * (group + 1)]


def sum_kernel(parts_ref, out_ref):
    columns = parts_ref.shape[2]
    for side in range(2):
        total = parts_ref[4 * side].astype(F32)
        for group in range(1, 4):
            total = total + parts_ref[4 * side + group].astype(F32)
        out_ref[:, side * columns : (side + 1) * columns] = total.astype(BF)


def places():
    at = lax.axis_index("ctx")
    return at // 8, (at // 2) % 4, at % 2


def in_vmem():
    return pl.BlockSpec(memory_space=pltpu.VMEM)


def in_hbm():
    return pl.BlockSpec(memory_space=pltpu.HBM)


def call(kernel, outs, *args, flops=10**3, name=None, ins=None, out_specs=None, scratch=(), room=32):
    if ins is None:
        ins = [in_vmem()] * len(args)
    return pl.pallas_call(
        kernel,
        out_shape=outs,
        in_specs=ins,
        out_specs=jax.tree.map(lambda _: in_vmem(), outs) if out_specs is None else out_specs,
        scratch_shapes=scratch,
        compiler_params=pltpu.CompilerParams(vmem_limit_bytes=room * 1024 * 1024),
        cost_estimate=pl.CostEstimate(flops=flops, bytes_accessed=10**3, transcendentals=0),
        name=name,
    )(*args)


def shape(dims, kind):
    return jax.ShapeDtypeStruct(dims, kind)


def local(
    queries, key_vectors, value_vectors, output_gate, write_rate, log_decay, norm_gain, out_weight
):
    width = out_weight.shape[1]
    half_width = width // 2
    rate, decay = write_rate.T, log_decay.T

    maps, solved, w0 = call(
        map_kernel,
        (
            shape((8, DK, DK + DV), BF),
            shape((2, TOK, DK + DV), F32),
            shape((DV, half_width), BF),
        ),
        key_vectors,
        value_vectors,
        rate,
        decay,
        out_weight,
        ins=[in_hbm()] * 5,
        out_specs=(in_vmem(), in_vmem(), in_vmem()),
        scratch=[
            pltpu.VMEM((TOK, DK), BF),
            pltpu.VMEM((TOK, 2 * DV), BF),
            pltpu.VMEM((2, TOK), F32),
            pltpu.VMEM((2, TOK), F32),
            pltpu.SemaphoreType.DMA((5,)),
        ],
        flops=10**9,
        room=60,
        name="shard_maps",
    )
    lines = [[8 * y + i for i in range(8)] for y in range(4)]
    parts = lax.all_to_all(maps, "ctx", 0, 0, axis_index_groups=lines)
    keep, send = call(
        read_kernel,
        (shape((3, TOK, DV), F32), shape((3, TOK, DV), BF)),
        queries,
        key_vectors,
        decay,
        output_gate,
        norm_gain.reshape(1, DV),
        solved,
        flops=10**9,
        name="read_parts",
    )
    across = [(i, i ^ 1) for i in range(32)]
    came = lax.ppermute(send, "ctx", across)

    w1 = lax.ppermute(w0, "tp", [(j, j ^ 1) for j in range(16)])
    w2 = lax.ppermute(w0, "tp", [(j, j ^ 2) for j in range(16)])

    parts, keep, send = lax.optimization_barrier((parts, keep, send))
    total, ahead, first = call(
        row_kernel,
        (shape((4, DK, DK + DV), BF), shape((DK, DK + DV), F32), shape((DK, DK + DV), BF)),
        parts,
        name="row_maps",
    )
    w2, ahead = lax.optimization_barrier((w2, ahead))
    w3 = lax.ppermute(w2, "tp", [(j, j ^ 1) for j in range(16)])
    columns = [[8 * y + i for y in range(4)] for i in range(8)]
    rows = lax.all_to_all(total, "ctx", 0, 0, axis_index_groups=columns)
    normed = call(
        out_kernel,
        shape((8, 128, DV), BF),
        rows,
        ahead,
        first,
        keep,
        came,
        flops=10**9,
        name="gated_norm",
    )
    pairs = [[8 * y + 4 * pair + 2 * side + core for side in range(2)]
             for y in range(4) for pair in range(2) for core in range(2)]
    close = [[16 * at + token_of(g, m) for at in pair for m in range(4)]
             for pair in pairs for g in range(4)]
    far = [[16 * at + token_of(g, m) for at in pair for g in range(4)]
           for pair in pairs for m in range(4)]
    both = ("ctx", "tp")
    gathered = lax.all_to_all(normed, both, 0, 0, axis_index_groups=close)
    far_rows = call(
        lay_kernel,
        shape((2, DV, half_width), BF),
        w1,
        w3,
        flops=10**10,
        name="lay_rows",
    )
    part, other_part = call(
        project_kernel,
        (shape((2, 64, half_width), F32), shape((2, 64, half_width), BF)),
        gathered,
        w0,
        w2,
        far_rows,
        name="project",
    )
    other_part = lax.ppermute(other_part, "ctx", across)
    partial = call(join_kernel, shape((8, 16, half_width), BF), part, other_part, name="join")
    shares = lax.all_to_all(partial, both, 0, 0, axis_index_groups=far)
    return call(sum_kernel, shape((16, width), BF), shares, name="sum_shares")


def solution(mesh):
    placed = (
        P("ctx", "tp"),
        P("ctx", "tp"),
        P("ctx", "tp"),
        P("ctx", "tp"),
        P("ctx", "tp"),
        P("ctx", "tp"),
        P(),
        P("tp", None),
    )
    return jax.shard_map(
        local, mesh=mesh, in_specs=placed, out_specs=P(("ctx", "tp"), None), check_vma=False
    )
```

```python
import jax
import jax.numpy as jnp
from jax import lax
from jax.experimental import pallas as pl
from jax.experimental.pallas import tpu as pltpu
from jax.sharding import PartitionSpec as P

F32 = jnp.float32
BF = jnp.bfloat16
TOK = 256
DK = 128
DV = 128
HALF = 128


def dot(a, b, dims=((1,), (0,))):
    return lax.dot_general(a, b, (dims, ((), ())), preferred_element_type=F32)


def split(a):
    hi = a.astype(BF)
    return hi, (a - hi.astype(F32)).astype(BF)


def dot_fine(a, b, dims=((1,), (0,))):
    ah, al = split(a)
    bh, bl = split(b)
    return dot(ah, bh, dims) + (dot(ah, bl, dims) + dot(al, bh, dims))


def dot_left(a, b, dims=((1,), (0,))):
    ah, al = split(a)
    return dot(ah, b, dims) + dot(al, b, dims)


def dot_right(a, b, dims=((1,), (0,))):
    bh, bl = split(b)
    return dot(a, bh, dims) + dot(a, bl, dims)


def grid_iota(rows, cols):
    return (
        lax.broadcasted_iota(jnp.int32, (rows, cols), 0),
        lax.broadcasted_iota(jnp.int32, (rows, cols), 1),
    )


def to_row(eye, column):
    return jnp.sum(jnp.where(eye, column, 0.0), axis=0, keepdims=True)


def to_column(eye, row):
    return jnp.sum(jnp.where(eye, row, 0.0), axis=1, keepdims=True)


def decay_sums(decay):
    row, col = grid_iota(TOK, TOK)
    ones = jnp.where(row <= col, 1.0, 0.0).astype(BF)
    eye = row == col
    hi = decay.astype(BF).astype(F32)
    rest = decay - hi
    mid = rest.astype(BF).astype(F32)
    low = rest - mid
    parts = jnp.concatenate([hi, mid, low, jnp.zeros((2, TOK), F32)], axis=0)
    sums = dot(parts.astype(BF), ones)
    rows = sums[0:2] + (sums[2:4] + sums[4:6])
    return [(rows[h : h + 1], to_column(eye, rows[h : h + 1])) for h in range(2)]


def unit_scale(source):
    full = source.astype(F32)
    return lax.rsqrt(jnp.sum(full * full, axis=1, keepdims=True) + 1e-06)


def map_kernel(
    k_far,
    v_far,
    rate_far,
    decay_far,
    weight_far,
    maps_ref,
    solved_ref,
    half_ref,
    k_ref,
    v_ref,
    rate_ref,
    decay_ref,
    sems,
):
    _, x, core = places()
    rows, columns = half_ref.shape
    begin = pl.multiple_of(core * rows, rows)
    left = pl.multiple_of((x % 2) * columns, columns)
    copies = [
        pltpu.make_async_copy(k_far, k_ref, sems.at[0]),
        pltpu.make_async_copy(decay_far, decay_ref, sems.at[1]),
        pltpu.make_async_copy(rate_far, rate_ref, sems.at[2]),
        pltpu.make_async_copy(v_far, v_ref, sems.at[3]),
        pltpu.make_async_copy(
            weight_far.at[pl.ds(begin, rows), pl.ds(left, columns)], half_ref, sems.at[4]
        ),
    ]
    for copy in copies:
        copy.start()
    for copy in copies[:4]:
        copy.wait()
    keys = k_ref[...]
    keys_f = keys.astype(F32)
    values = v_ref[...].astype(F32)
    row, col = grid_iota(TOK, TOK)
    eye = row == col
    strict = row > col
    rate = [to_column(eye, rate_ref[h : h + 1, :]) for h in range(2)]
    gram = dot(keys, keys, ((1,), (1,)))
    scale = unit_scale(keys)
    gram = gram * scale * to_row(eye, scale)
    sum_rows, sums = zip(*decay_sums(decay_ref[...]))
    r_s, c_s = grid_iota(HALF, HALF)
    eye_s = jnp.where(r_s == c_s, 1.0, 0.0).astype(F32)

    lowers, corners = [], []
    for head in range(2):
        fall = jnp.exp(jnp.minimum(sums[head] - sum_rows[head], 0.0))
        low = jnp.where(strict, rate[head] * gram * fall, 0.0)
        lowers += [low[:HALF, :HALF], low[HALF:, HALF:]]
        corners.append(low[HALF:, :HALF])

    small = (r_s // 8) == (c_s // 8)
    first = [jnp.where(small, low, 0.0) for low in lowers]
    first_b = [a.astype(BF) for a in first]
    square = [dot(a, a).astype(BF) for a in first_b]
    fourth = [dot(a, a).astype(BF) for a in square]
    inv = [eye_s - a for a in first]
    inv = [x + dot(x.astype(BF), a) for x, a in zip(inv, square)]
    inv = [x + dot(x.astype(BF), a) for x, a in zip(inv, fourth)]
    size = 8
    while size < HALF:
        off = ((r_s // (2 * size)) == (c_s // (2 * size))) & ((r_s // size) > (c_s // size))
        inv_b = [x.astype(BF) for x in inv]
        part = [jnp.where(off, low, 0.0).astype(BF) for low in lowers]
        part = [dot(a, x).astype(BF) for a, x in zip(part, inv_b)]
        inv = [x - dot(xb, a) for x, xb, a in zip(inv, inv_b, part)]
        size *= 2
    inv_b = [x.astype(BF) for x in inv]
    gap = [
        eye_s - xb.astype(F32) - dot_left(low, xb) for low, xb in zip(lowers, inv_b)
    ]
    inv = [xb.astype(F32) + dot(xb, g.astype(BF)) for xb, g in zip(inv_b, gap)]

    eye_k = jnp.where(r_s == c_s, 1.0, 0.0).astype(F32)
    solved = []
    for head in range(2):
        b = rate[head]
        grow = b * jnp.exp(sums[head]) * scale
        right = jnp.concatenate(
            [grow * keys_f, b * values[:, head * DV : (head + 1) * DV]], axis=1
        )
        top = dot_fine(inv[2 * head], right[:HALF])
        solved.append((top, right[HALF:]))
    for head in range(2):
        top, below = solved[head]
        below = below - dot_fine(corners[head], top)
        below = dot_fine(inv[2 * head + 1], below)
        solved[head] = jnp.concatenate([top, below], axis=0)
    maps = []
    for head in range(2):
        closing = sums[head][TOK - 1 :, :]
        weight = scale * jnp.exp(closing - sums[head])
        moved = dot_right(keys, weight * solved[head], ((0,), (0,)))
        transit = eye_k * jnp.exp(closing) - moved[:, :DK]
        maps.append(jnp.concatenate([transit, moved[:, DK:]], axis=1).astype(BF))
    for place in range(maps_ref.shape[0]):
        maps_ref[place] = maps[place % 2]
    for head in range(2):
        solved_ref[head] = solved[head]
    copies[4].wait()


def read_kernel(
    q_ref, k_ref, decay_ref, gate_ref, gain_ref, solved_ref, keep_ref, send_ref
):
    core = places()[2]
    queries = q_ref[...]
    keys = k_ref[...]
    row, col = grid_iota(TOK, TOK)
    eye = row == col
    inclusive = row >= col
    unit_q = unit_scale(queries)
    scores = dot(queries, keys, ((1,), (1,))) * unit_q * to_row(eye, unit_scale(keys))
    sums = decay_sums(decay_ref[...])
    read = []
    for head in range(2):
        sum_row, sum_column = sums[head]
        fall = jnp.exp(jnp.minimum(sum_column - sum_row, 0.0))
        weights = jnp.where(inclusive, scores * fall, 0.0)
        both = dot_fine(weights, solved_ref[head])
        outer = jnp.exp(sum_column) * unit_q * queries.astype(F32) - both[:, :DK]
        gate = gate_ref[:, head * DV : (head + 1) * DV].astype(F32)
        gated = gain_ref[...] * (gate / (1.0 + jnp.exp(-gate)))
        read.append((both[:, DK:], outer, gated))
    for i in range(3):
        keep_ref[i] = jnp.where(core == 0, read[0][i], read[1][i])
        send_ref[i] = jnp.where(core == 0, read[1][i], read[0][i]).astype(BF)


def after(later_t, later_h, earlier, fine):
    moved = dot_fine(later_t, earlier) if fine else dot_right(later_t, earlier)
    return jnp.concatenate([moved[:, :DK], moved[:, DK:] + later_h], axis=1)


def row_kernel(parts_ref, total_ref, ahead_ref, first_ref):
    x = places()[1]

    def pair(i):
        later = parts_ref[2 * i + 1]
        moved = dot(later[:, :DK], parts_ref[2 * i])
        return jnp.concatenate(
            [moved[:, :DK], moved[:, DK:] + later[:, DK:].astype(F32)], axis=1
        )

    pairs = [pair(i) for i in range(4)]
    upto2 = pairs[0]
    upto4 = after(pairs[1][:, :DK], pairs[1][:, DK:], upto2, True)
    last2 = after(pairs[3][:, :DK], pairs[3][:, DK:], pairs[2], True)
    upto6 = after(pairs[2][:, :DK], pairs[2][:, DK:], upto4, True)
    total = after(last2[:, :DK], last2[:, DK:], upto4, True).astype(BF)
    for place in range(4):
        total_ref[place] = total
    row, col = grid_iota(DK, DK + DV)
    none = jnp.where(row == col, 1.0, 0.0).astype(F32)
    ahead_ref[...] = jnp.where(
        x == 0, none, jnp.where(x == 1, upto2, jnp.where(x == 2, upto4, upto6))
    )
    first_ref[...] = parts_ref[2 * x]


def token_of(group, label):
    return 4 * group + (label if group < 2 else 3 - label)


def out_kernel(rows_ref, ahead_ref, first_ref, keep_ref, came_ref, out_ref):
    y, _, core = places()

    def onward(later, state):
        return dot_right(later[:, :DK], state) + later[:, DK:].astype(F32)

    one = rows_ref[0][:, DK:].astype(F32)
    two = onward(rows_ref[1], one)
    three = onward(rows_ref[2], two)
    start = jnp.where(
        y == 0, jnp.zeros_like(one), jnp.where(y == 1, one, jnp.where(y == 2, two, three))
    )
    ahead = ahead_ref[...]
    chip = dot_fine(ahead[:, :DK], start) + ahead[:, DK:]
    second = onward(first_ref[...], chip)

    def finish(state, inner, outer, gated):
        reached = inner + dot_left(outer, state.astype(BF))
        mean = jnp.sum(reached * reached, axis=1, keepdims=True) * (1.0 / DV)
        return (reached * lax.rsqrt(mean + 1e-06) * gated).astype(BF)

    own = finish(jnp.where(core == 0, chip, second), keep_ref[0], keep_ref[1], keep_ref[2])
    came = [came_ref[i].astype(F32) for i in range(3)]
    other = finish(jnp.where(core == 0, second, chip), *came)
    shards = (jnp.where(core == 0, own, other), jnp.where(core == 0, other, own))
    for label in range(4):
        for shard in range(2):
            for group in range(4):
                source = 16 * token_of(group, label)
                target = 64 * shard + 16 * group
                piece = shards[shard][source : source + 16]
                for side in range(2):
                    out_ref[4 * side + label, target : target + 16] = piece


def lay_kernel(rows_ref, out_ref):
    out_ref[...] = rows_ref[...]


def project_kernel(normed_ref, w0_ref, w2_ref, far_ref, keep_ref, send_ref):
    _, _, core = places()
    along = lax.axis_index("tp")
    weights = [w0_ref[...], far_ref[0], w2_ref[...], far_ref[1]]
    for side in range(2):
        total = None
        for i, weight in enumerate(weights):
            near = (along % 4) ^ i
            label = jnp.where(along < 8, near, 3 - near)
            term = dot(normed_ref[4 * side + label], weight)
            total = term if total is None else total + term
        keep_ref[side] = jnp.where(core == 0, total[:64], total[64:])
        send_ref[side] = jnp.where(core == 0, total[64:], total[:64]).astype(BF)


def join_kernel(keep_ref, came_ref, out_ref):
    for side in range(2):
        total = (keep_ref[side] + came_ref[side].astype(F32)).astype(BF)
        for group in range(4):
            out_ref[4 * side + group] = total[16 * group : 16 * (group + 1)]


def sum_kernel(parts_ref, out_ref):
    columns = parts_ref.shape[2]
    for side in range(2):
        total = parts_ref[4 * side].astype(F32)
        for group in range(1, 4):
            total = total + parts_ref[4 * side + group].astype(F32)
        out_ref[:, side * columns : (side + 1) * columns] = total.astype(BF)


def places():
    at = lax.axis_index("ctx")
    return at // 8, (at // 2) % 4, at % 2


def in_vmem():
    return pl.BlockSpec(memory_space=pltpu.VMEM)


def in_hbm():
    return pl.BlockSpec(memory_space=pltpu.HBM)


def call(kernel, outs, *args, flops=10**3, name=None, ins=None, out_specs=None, scratch=(), room=32):
    if ins is None:
        ins = [in_vmem()] * len(args)
    return pl.pallas_call(
        kernel,
        out_shape=outs,
        in_specs=ins,
        out_specs=jax.tree.map(lambda _: in_vmem(), outs) if out_specs is None else out_specs,
        scratch_shapes=scratch,
        compiler_params=pltpu.CompilerParams(vmem_limit_bytes=room * 1024 * 1024),
        cost_estimate=pl.CostEstimate(flops=flops, bytes_accessed=10**3, transcendentals=0),
        name=name,
    )(*args)


def shape(dims, kind):
    return jax.ShapeDtypeStruct(dims, kind)


def local(
    queries, key_vectors, value_vectors, output_gate, write_rate, log_decay, norm_gain, out_weight
):
    width = out_weight.shape[1]
    half_width = width // 2
    rate, decay = write_rate.T, log_decay.T

    maps, solved, w0 = call(
        map_kernel,
        (
            shape((8, DK, DK + DV), BF),
            shape((2, TOK, DK + DV), F32),
            shape((DV, half_width), BF),
        ),
        key_vectors,
        value_vectors,
        rate,
        decay,
        out_weight,
        ins=[in_hbm()] * 5,
        out_specs=(in_vmem(), in_vmem(), in_vmem()),
        scratch=[
            pltpu.VMEM((TOK, DK), BF),
            pltpu.VMEM((TOK, 2 * DV), BF),
            pltpu.VMEM((2, TOK), F32),
            pltpu.VMEM((2, TOK), F32),
            pltpu.SemaphoreType.DMA((5,)),
        ],
        flops=10**9,
        room=60,
        name="shard_maps",
    )
    lines = [[8 * y + i for i in range(8)] for y in range(4)]
    parts = lax.all_to_all(maps, "ctx", 0, 0, axis_index_groups=lines)
    keep, send = call(
        read_kernel,
        (shape((3, TOK, DV), F32), shape((3, TOK, DV), BF)),
        queries,
        key_vectors,
        decay,
        output_gate,
        norm_gain.reshape(1, DV),
        solved,
        flops=10**9,
        name="read_parts",
    )
    across = [(i, i ^ 1) for i in range(32)]
    came = lax.ppermute(send, "ctx", across)

    w2 = lax.ppermute(w0, "tp", [(j, j ^ 2) for j in range(16)])

    parts, keep, send = lax.optimization_barrier((parts, keep, send))
    total, ahead, first = call(
        row_kernel,
        (shape((4, DK, DK + DV), BF), shape((DK, DK + DV), F32), shape((DK, DK + DV), BF)),
        parts,
        name="row_maps",
    )
    w2, ahead = lax.optimization_barrier((w2, ahead))
    near13 = lax.ppermute(jnp.stack([w0, w2]), "tp", [(j, j ^ 1) for j in range(16)])
    columns = [[8 * y + i for y in range(4)] for i in range(8)]
    rows = lax.all_to_all(total, "ctx", 0, 0, axis_index_groups=columns)
    normed = call(
        out_kernel,
        shape((8, 128, DV), BF),
        rows,
        ahead,
        first,
        keep,
        came,
        flops=10*10**9,
        name="gated_norm",
    )
    pairs = [[8 * y + 4 * pair + 2 * side + core for side in range(2)]
             for y in range(4) for pair in range(2) for core in range(2)]
    close = [[16 * at + token_of(g, m) for at in pair for m in range(4)]
             for pair in pairs for g in range(4)]
    far = [[16 * at + token_of(g, m) for at in pair for g in range(4)]
           for pair in pairs for m in range(4)]
    both = ("ctx", "tp")
    gathered = lax.all_to_all(normed, both, 0, 0, axis_index_groups=close)
    far_rows = call(
        lay_kernel,
        shape((2, DV, half_width), BF),
        near13,
        flops=10*10**9,
        name="lay_rows",
    )
    part, other_part = call(
        project_kernel,
        (shape((2, 64, half_width), F32), shape((2, 64, half_width), BF)),
        gathered,
        w0,
        w2,
        far_rows,
        name="project",
    )
    other_part = lax.ppermute(other_part, "ctx", across)
    partial = call(join_kernel, shape((8, 16, half_width), BF), part, other_part, name="join")
    shares = lax.all_to_all(partial, both, 0, 0, axis_index_groups=far)
    return call(sum_kernel, shape((16, width), BF), shares, name="sum_shares")


def solution(mesh):
    placed = (
        P("ctx", "tp"),
        P("ctx", "tp"),
        P("ctx", "tp"),
        P("ctx", "tp"),
        P("ctx", "tp"),
        P("ctx", "tp"),
        P(),
        P("tp", None),
    )
    return jax.shard_map(
        local, mesh=mesh, in_specs=placed, out_specs=P(("ctx", "tp"), None), check_vma=False
    )
```

```python
import jax
import jax.numpy as jnp
from jax import lax
from jax.experimental import pallas as pl
from jax.experimental.pallas import tpu as pltpu
from jax.sharding import PartitionSpec as P

F32 = jnp.float32
BF = jnp.bfloat16
TOK = 256
DK = 128
DV = 128
HALF = 128


def dot(a, b, dims=((1,), (0,))):
    return lax.dot_general(a, b, (dims, ((), ())), preferred_element_type=F32)


def split(a):
    hi = a.astype(BF)
    return hi, (a - hi.astype(F32)).astype(BF)


def dot_fine(a, b, dims=((1,), (0,))):
    ah, al = split(a)
    bh, bl = split(b)
    return dot(ah, bh, dims) + (dot(ah, bl, dims) + dot(al, bh, dims))


def dot_left(a, b, dims=((1,), (0,))):
    ah, al = split(a)
    return dot(ah, b, dims) + dot(al, b, dims)


def dot_right(a, b, dims=((1,), (0,))):
    bh, bl = split(b)
    return dot(a, bh, dims) + dot(a, bl, dims)


def grid_iota(rows, cols):
    return (
        lax.broadcasted_iota(jnp.int32, (rows, cols), 0),
        lax.broadcasted_iota(jnp.int32, (rows, cols), 1),
    )


def to_row(eye, column):
    return jnp.sum(jnp.where(eye, column, 0.0), axis=0, keepdims=True)


def to_column(eye, row):
    return jnp.sum(jnp.where(eye, row, 0.0), axis=1, keepdims=True)


def decay_sums(decay):
    row, col = grid_iota(TOK, TOK)
    ones = jnp.where(row <= col, 1.0, 0.0).astype(BF)
    eye = row == col
    hi = decay.astype(BF).astype(F32)
    rest = decay - hi
    mid = rest.astype(BF).astype(F32)
    low = rest - mid
    parts = jnp.concatenate([hi, mid, low, jnp.zeros((2, TOK), F32)], axis=0)
    sums = dot(parts.astype(BF), ones)
    rows = sums[0:2] + (sums[2:4] + sums[4:6])
    return [(rows[h : h + 1], to_column(eye, rows[h : h + 1])) for h in range(2)]


def unit_scale(source):
    full = source.astype(F32)
    return lax.rsqrt(jnp.sum(full * full, axis=1, keepdims=True) + 1e-06)


def map_kernel(
    k_far,
    v_far,
    rate_far,
    decay_far,
    weight_far,
    maps_ref,
    solved_ref,
    half_ref,
    k_ref,
    v_ref,
    rate_ref,
    decay_ref,
    sems,
):
    _, x, core = places()
    rows, columns = half_ref.shape
    begin = pl.multiple_of(core * rows, rows)
    left = pl.multiple_of((x % 2) * columns, columns)
    copies = [
        pltpu.make_async_copy(k_far, k_ref, sems.at[0]),
        pltpu.make_async_copy(decay_far, decay_ref, sems.at[1]),
        pltpu.make_async_copy(rate_far, rate_ref, sems.at[2]),
        pltpu.make_async_copy(v_far, v_ref, sems.at[3]),
        pltpu.make_async_copy(
            weight_far.at[pl.ds(begin, rows), pl.ds(left, columns)], half_ref, sems.at[4]
        ),
    ]
    for copy in copies:
        copy.start()
    for copy in copies[:4]:
        copy.wait()
    keys = k_ref[...]
    keys_f = keys.astype(F32)
    values = v_ref[...].astype(F32)
    row, col = grid_iota(TOK, TOK)
    eye = row == col
    strict = row > col
    rate = [to_column(eye, rate_ref[h : h + 1, :]) for h in range(2)]
    gram = dot(keys, keys, ((1,), (1,)))
    scale = unit_scale(keys)
    gram = gram * scale * to_row(eye, scale)
    sum_rows, sums = zip(*decay_sums(decay_ref[...]))
    r_s, c_s = grid_iota(HALF, HALF)
    eye_s = jnp.where(r_s == c_s, 1.0, 0.0).astype(F32)

    lowers, corners = [], []
    for head in range(2):
        fall = jnp.exp(jnp.minimum(sums[head] - sum_rows[head], 0.0))
        low = jnp.where(strict, rate[head] * gram * fall, 0.0)
        lowers += [low[:HALF, :HALF], low[HALF:, HALF:]]
        corners.append(low[HALF:, :HALF])

    small = (r_s // 8) == (c_s // 8)
    first = [jnp.where(small, low, 0.0) for low in lowers]
    first_b = [a.astype(BF) for a in first]
    square = [dot(a, a).astype(BF) for a in first_b]
    fourth = [dot(a, a).astype(BF) for a in square]
    inv = [eye_s - a for a in first]
    inv = [x + dot(x.astype(BF), a) for x, a in zip(inv, square)]
    inv = [x + dot(x.astype(BF), a) for x, a in zip(inv, fourth)]
    size = 8
    while size < HALF:
        off = ((r_s // (2 * size)) == (c_s // (2 * size))) & ((r_s // size) > (c_s // size))
        inv_b = [x.astype(BF) for x in inv]
        part = [jnp.where(off, low, 0.0).astype(BF) for low in lowers]
        part = [dot(a, x).astype(BF) for a, x in zip(part, inv_b)]
        inv = [x - dot(xb, a) for x, xb, a in zip(inv, inv_b, part)]
        size *= 2
    inv_b = [x.astype(BF) for x in inv]
    gap = [
        eye_s - xb.astype(F32) - dot_left(low, xb) for low, xb in zip(lowers, inv_b)
    ]
    inv = [xb.astype(F32) + dot(xb, g.astype(BF)) for xb, g in zip(inv_b, gap)]

    eye_k = jnp.where(r_s == c_s, 1.0, 0.0).astype(F32)
    solved = []
    for head in range(2):
        b = rate[head]
        grow = b * jnp.exp(sums[head]) * scale
        right = jnp.concatenate(
            [grow * keys_f, b * values[:, head * DV : (head + 1) * DV]], axis=1
        )
        top = dot_fine(inv[2 * head], right[:HALF])
        solved.append((top, right[HALF:]))
    for head in range(2):
        top, below = solved[head]
        below = below - dot_fine(corners[head], top)
        below = dot_fine(inv[2 * head + 1], below)
        solved[head] = jnp.concatenate([top, below], axis=0)
    maps = []
    for head in range(2):
        closing = sums[head][TOK - 1 :, :]
        weight = scale * jnp.exp(closing - sums[head])
        moved = dot_right(keys, weight * solved[head], ((0,), (0,)))
        transit = eye_k * jnp.exp(closing) - moved[:, :DK]
        maps.append(jnp.concatenate([transit, moved[:, DK:]], axis=1).astype(BF))
    for place in range(maps_ref.shape[0]):
        maps_ref[place] = maps[place % 2]
    for head in range(2):
        solved_ref[head] = solved[head]
    copies[4].wait()


def read_kernel(
    q_ref, k_ref, decay_ref, gate_ref, gain_ref, solved_ref, keep_ref, send_ref
):
    core = places()[2]
    queries = q_ref[...]
    keys = k_ref[...]
    row, col = grid_iota(TOK, TOK)
    eye = row == col
    inclusive = row >= col
    unit_q = unit_scale(queries)
    scores = dot(queries, keys, ((1,), (1,))) * unit_q * to_row(eye, unit_scale(keys))
    sums = decay_sums(decay_ref[...])
    read = []
    for head in range(2):
        sum_row, sum_column = sums[head]
        fall = jnp.exp(jnp.minimum(sum_column - sum_row, 0.0))
        weights = jnp.where(inclusive, scores * fall, 0.0)
        both = dot_fine(weights, solved_ref[head])
        outer = jnp.exp(sum_column) * unit_q * queries.astype(F32) - both[:, :DK]
        gate = gate_ref[:, head * DV : (head + 1) * DV].astype(F32)
        gated = gain_ref[...] * (gate / (1.0 + jnp.exp(-gate)))
        read.append((both[:, DK:], outer, gated))
    for i in range(3):
        keep_ref[i] = jnp.where(core == 0, read[0][i], read[1][i])
        send_ref[i] = jnp.where(core == 0, read[1][i], read[0][i]).astype(BF)


def after(later_t, later_h, earlier, fine):
    moved = dot_fine(later_t, earlier) if fine else dot_right(later_t, earlier)
    return jnp.concatenate([moved[:, :DK], moved[:, DK:] + later_h], axis=1)


def row_kernel(parts_ref, total_ref, ahead_ref, first_ref):
    x = places()[1]

    def pair(i):
        later = parts_ref[2 * i + 1]
        moved = dot(later[:, :DK], parts_ref[2 * i])
        return jnp.concatenate(
            [moved[:, :DK], moved[:, DK:] + later[:, DK:].astype(F32)], axis=1
        )

    pairs = [pair(i) for i in range(4)]
    upto2 = pairs[0]
    upto4 = after(pairs[1][:, :DK], pairs[1][:, DK:], upto2, True)
    last2 = after(pairs[3][:, :DK], pairs[3][:, DK:], pairs[2], True)
    upto6 = after(pairs[2][:, :DK], pairs[2][:, DK:], upto4, True)
    total = after(last2[:, :DK], last2[:, DK:], upto4, True).astype(BF)
    for place in range(4):
        total_ref[place] = total
    row, col = grid_iota(DK, DK + DV)
    none = jnp.where(row == col, 1.0, 0.0).astype(F32)
    ahead_ref[...] = jnp.where(
        x == 0, none, jnp.where(x == 1, upto2, jnp.where(x == 2, upto4, upto6))
    )
    first_ref[...] = parts_ref[2 * x]


def token_of(group, label):
    return 4 * group + (label if group < 2 else 3 - label)


def out_kernel(rows_ref, ahead_ref, first_ref, keep_ref, came_ref, out_ref):
    y, _, core = places()

    def onward(later, state):
        return dot_right(later[:, :DK], state) + later[:, DK:].astype(F32)

    one = rows_ref[0][:, DK:].astype(F32)
    two = onward(rows_ref[1], one)
    three = onward(rows_ref[2], two)
    start = jnp.where(
        y == 0, jnp.zeros_like(one), jnp.where(y == 1, one, jnp.where(y == 2, two, three))
    )
    ahead = ahead_ref[...]
    chip = dot_fine(ahead[:, :DK], start) + ahead[:, DK:]
    second = onward(first_ref[...], chip)

    def finish(state, inner, outer, gated):
        reached = inner + dot_left(outer, state.astype(BF))
        mean = jnp.sum(reached * reached, axis=1, keepdims=True) * (1.0 / DV)
        return (reached * lax.rsqrt(mean + 1e-06) * gated).astype(BF)

    own = finish(jnp.where(core == 0, chip, second), keep_ref[0], keep_ref[1], keep_ref[2])
    came = [came_ref[i].astype(F32) for i in range(3)]
    other = finish(jnp.where(core == 0, second, chip), *came)
    shards = (jnp.where(core == 0, own, other), jnp.where(core == 0, other, own))
    for label in range(4):
        for shard in range(2):
            for group in range(4):
                source = 16 * token_of(group, label)
                target = 64 * shard + 16 * group
                piece = shards[shard][source : source + 16]
                for side in range(2):
                    out_ref[4 * side + label, target : target + 16] = piece


def lay_kernel(rows_ref, out_ref):
    out_ref[...] = rows_ref[...]


def project_kernel(normed_ref, w0_ref, w2_ref, far_ref, keep_ref, send_ref):
    _, _, core = places()
    along = lax.axis_index("tp")
    weights = [w0_ref[...], far_ref[0], w2_ref[...], far_ref[1]]
    for side in range(2):
        total = None
        for i, weight in enumerate(weights):
            near = (along % 4) ^ i
            label = jnp.where(along < 8, near, 3 - near)
            term = dot(normed_ref[4 * side + label], weight)
            total = term if total is None else total + term
        keep_ref[side] = jnp.where(core == 0, total[:64], total[64:])
        send_ref[side] = jnp.where(core == 0, total[64:], total[:64]).astype(BF)


def join_kernel(keep_ref, came_ref, out_ref):
    for side in range(2):
        total = (keep_ref[side] + came_ref[side].astype(F32)).astype(BF)
        for group in range(4):
            out_ref[4 * side + group] = total[16 * group : 16 * (group + 1)]


def places():
    at = lax.axis_index("ctx")
    return at // 8, (at // 2) % 4, at % 2


def in_vmem():
    return pl.BlockSpec(memory_space=pltpu.VMEM)


def in_hbm():
    return pl.BlockSpec(memory_space=pltpu.HBM)


def call(kernel, outs, *args, flops=10**3, name=None, ins=None, out_specs=None, scratch=(), room=32):
    if ins is None:
        ins = [in_vmem()] * len(args)
    return pl.pallas_call(
        kernel,
        out_shape=outs,
        in_specs=ins,
        out_specs=jax.tree.map(lambda _: in_vmem(), outs) if out_specs is None else out_specs,
        scratch_shapes=scratch,
        compiler_params=pltpu.CompilerParams(vmem_limit_bytes=room * 1024 * 1024),
        cost_estimate=pl.CostEstimate(flops=flops, bytes_accessed=10**3, transcendentals=0),
        name=name,
    )(*args)


def shape(dims, kind):
    return jax.ShapeDtypeStruct(dims, kind)


def local(
    queries, key_vectors, value_vectors, output_gate, write_rate, log_decay, norm_gain, out_weight
):
    width = out_weight.shape[1]
    half_width = width // 2
    rate, decay = write_rate.T, log_decay.T

    maps, solved, w0 = call(
        map_kernel,
        (
            shape((8, DK, DK + DV), BF),
            shape((2, TOK, DK + DV), F32),
            shape((DV, half_width), BF),
        ),
        key_vectors,
        value_vectors,
        rate,
        decay,
        out_weight,
        ins=[in_hbm()] * 5,
        out_specs=(in_vmem(), in_vmem(), in_vmem()),
        scratch=[
            pltpu.VMEM((TOK, DK), BF),
            pltpu.VMEM((TOK, 2 * DV), BF),
            pltpu.VMEM((2, TOK), F32),
            pltpu.VMEM((2, TOK), F32),
            pltpu.SemaphoreType.DMA((5,)),
        ],
        flops=10**9,
        room=60,
        name="shard_maps",
    )
    lines = [[8 * y + i for i in range(8)] for y in range(4)]
    parts = lax.all_to_all(maps, "ctx", 0, 0, axis_index_groups=lines)
    keep, send = call(
        read_kernel,
        (shape((3, TOK, DV), F32), shape((3, TOK, DV), BF)),
        queries,
        key_vectors,
        decay,
        output_gate,
        norm_gain.reshape(1, DV),
        solved,
        flops=10**9,
        name="read_parts",
    )
    across = [(i, i ^ 1) for i in range(32)]
    came = lax.ppermute(send, "ctx", across)

    w2 = lax.ppermute(w0, "tp", [(j, j ^ 2) for j in range(16)])

    parts, keep, send = lax.optimization_barrier((parts, keep, send))
    total, ahead, first = call(
        row_kernel,
        (shape((4, DK, DK + DV), BF), shape((DK, DK + DV), F32), shape((DK, DK + DV), BF)),
        parts,
        name="row_maps",
    )
    w2, ahead = lax.optimization_barrier((w2, ahead))
    near13 = lax.ppermute(jnp.stack([w0, w2]), "tp", [(j, j ^ 1) for j in range(16)])
    columns = [[8 * y + i for y in range(4)] for i in range(8)]
    rows = lax.all_to_all(total, "ctx", 0, 0, axis_index_groups=columns)
    normed = call(
        out_kernel,
        shape((8, 128, DV), BF),
        rows,
        ahead,
        first,
        keep,
        came,
        flops=10*10**9,
        name="gated_norm",
    )
    pairs = [[8 * y + 4 * pair + 2 * side + core for side in range(2)]
             for y in range(4) for pair in range(2) for core in range(2)]
    close = [[16 * at + token_of(g, m) for at in pair for m in range(4)]
             for pair in pairs for g in range(4)]
    far = [[16 * at + token_of(g, m) for at in pair for g in range(4)]
           for pair in pairs for m in range(4)]
    both = ("ctx", "tp")
    gathered = lax.all_to_all(normed, both, 0, 0, axis_index_groups=close)
    far_rows = call(
        lay_kernel,
        shape((2, DV, half_width), BF),
        near13,
        flops=10*10**9,
        name="lay_rows",
    )
    part, other_part = call(
        project_kernel,
        (shape((2, 64, half_width), F32), shape((2, 64, half_width), BF)),
        gathered,
        w0,
        w2,
        far_rows,
        name="project",
    )
    other_part = lax.ppermute(other_part, "ctx", across)
    partial = call(join_kernel, shape((8, 16, half_width), BF), part, other_part, name="join")
    shares = lax.all_to_all(partial, both, 0, 0, axis_index_groups=far)
    sides = [
        sum(shares[4 * side + g].astype(F32) for g in range(4)).astype(BF) for side in range(2)
    ]
    return jnp.concatenate(sides, axis=1)


def solution(mesh):
    placed = (
        P("ctx", "tp"),
        P("ctx", "tp"),
        P("ctx", "tp"),
        P("ctx", "tp"),
        P("ctx", "tp"),
        P("ctx", "tp"),
        P(),
        P("tp", None),
    )
    return jax.shard_map(
        local, mesh=mesh, in_specs=placed, out_specs=P(("ctx", "tp"), None), check_vma=False
    )
```

```python
import jax
import jax.numpy as jnp
from jax import lax
from jax.experimental import pallas as pl
from jax.experimental.pallas import tpu as pltpu
from jax.sharding import PartitionSpec as P

F32 = jnp.float32
BF = jnp.bfloat16
TOK = 256
DK = 128
DV = 128
HALF = 128


def dot(a, b, dims=((1,), (0,))):
    return lax.dot_general(a, b, (dims, ((), ())), preferred_element_type=F32)


def split(a):
    hi = a.astype(BF)
    return hi, (a - hi.astype(F32)).astype(BF)


def dot_fine(a, b, dims=((1,), (0,))):
    ah, al = split(a)
    bh, bl = split(b)
    return dot(ah, bh, dims) + (dot(ah, bl, dims) + dot(al, bh, dims))


def dot_left(a, b, dims=((1,), (0,))):
    ah, al = split(a)
    return dot(ah, b, dims) + dot(al, b, dims)


def dot_right(a, b, dims=((1,), (0,))):
    bh, bl = split(b)
    return dot(a, bh, dims) + dot(a, bl, dims)


def grid_iota(rows, cols):
    return (
        lax.broadcasted_iota(jnp.int32, (rows, cols), 0),
        lax.broadcasted_iota(jnp.int32, (rows, cols), 1),
    )


def to_row(eye, column):
    return jnp.sum(jnp.where(eye, column, 0.0), axis=0, keepdims=True)


def to_column(eye, row):
    return jnp.sum(jnp.where(eye, row, 0.0), axis=1, keepdims=True)


def decay_sums(decay):
    row, col = grid_iota(TOK, TOK)
    ones = jnp.where(row <= col, 1.0, 0.0).astype(BF)
    eye = row == col
    hi = decay.astype(BF).astype(F32)
    rest = decay - hi
    mid = rest.astype(BF).astype(F32)
    low = rest - mid
    parts = jnp.concatenate([hi, mid, low, jnp.zeros((2, TOK), F32)], axis=0)
    sums = dot(parts.astype(BF), ones)
    rows = sums[0:2] + (sums[2:4] + sums[4:6])
    return [(rows[h : h + 1], to_column(eye, rows[h : h + 1])) for h in range(2)]


def unit_scale(source):
    full = source.astype(F32)
    return lax.rsqrt(jnp.sum(full * full, axis=1, keepdims=True) + 1e-06)


def map_kernel(
    k_far,
    v_far,
    rate_far,
    decay_far,
    weight_far,
    maps_ref,
    solved_ref,
    half_ref,
    k_ref,
    v_ref,
    rate_ref,
    decay_ref,
    sems,
):
    _, x, core = places()
    rows, columns = half_ref.shape
    begin = pl.multiple_of(core * rows, rows)
    left = pl.multiple_of((x % 2) * columns, columns)
    copies = [
        pltpu.make_async_copy(k_far, k_ref, sems.at[0]),
        pltpu.make_async_copy(decay_far, decay_ref, sems.at[1]),
        pltpu.make_async_copy(rate_far, rate_ref, sems.at[2]),
        pltpu.make_async_copy(v_far, v_ref, sems.at[3]),
        pltpu.make_async_copy(
            weight_far.at[pl.ds(begin, rows), pl.ds(left, columns)], half_ref, sems.at[4]
        ),
    ]
    for copy in copies:
        copy.start()
    for copy in copies[:4]:
        copy.wait()
    keys = k_ref[...]
    keys_f = keys.astype(F32)
    values = v_ref[...].astype(F32)
    row, col = grid_iota(TOK, TOK)
    eye = row == col
    strict = row > col
    rate = [to_column(eye, rate_ref[h : h + 1, :]) for h in range(2)]
    gram = dot(keys, keys, ((1,), (1,)))
    scale = unit_scale(keys)
    gram = gram * scale * to_row(eye, scale)
    sum_rows, sums = zip(*decay_sums(decay_ref[...]))
    r_s, c_s = grid_iota(HALF, HALF)
    eye_s = jnp.where(r_s == c_s, 1.0, 0.0).astype(F32)

    lowers, corners = [], []
    for head in range(2):
        fall = jnp.exp(jnp.minimum(sums[head] - sum_rows[head], 0.0))
        low = jnp.where(strict, rate[head] * gram * fall, 0.0)
        lowers += [low[:HALF, :HALF], low[HALF:, HALF:]]
        corners.append(low[HALF:, :HALF])

    small = (r_s // 8) == (c_s // 8)
    first = [jnp.where(small, low, 0.0) for low in lowers]
    first_b = [a.astype(BF) for a in first]
    square = [dot(a, a).astype(BF) for a in first_b]
    fourth = [dot(a, a).astype(BF) for a in square]
    inv = [eye_s - a for a in first]
    inv = [x + dot(x.astype(BF), a) for x, a in zip(inv, square)]
    inv = [x + dot(x.astype(BF), a) for x, a in zip(inv, fourth)]
    size = 8
    while size < HALF:
        off = ((r_s // (2 * size)) == (c_s // (2 * size))) & ((r_s // size) > (c_s // size))
        inv_b = [x.astype(BF) for x in inv]
        part = [jnp.where(off, low, 0.0).astype(BF) for low in lowers]
        part = [dot(a, x).astype(BF) for a, x in zip(part, inv_b)]
        inv = [x - dot(xb, a) for x, xb, a in zip(inv, inv_b, part)]
        size *= 2
    inv_b = [x.astype(BF) for x in inv]
    gap = [
        eye_s - xb.astype(F32) - dot_left(low, xb) for low, xb in zip(lowers, inv_b)
    ]
    inv = [xb.astype(F32) + dot(xb, g.astype(BF)) for xb, g in zip(inv_b, gap)]

    eye_k = jnp.where(r_s == c_s, 1.0, 0.0).astype(F32)
    solved = []
    for head in range(2):
        b = rate[head]
        grow = b * jnp.exp(sums[head]) * scale
        right = jnp.concatenate(
            [grow * keys_f, b * values[:, head * DV : (head + 1) * DV]], axis=1
        )
        top = dot_fine(inv[2 * head], right[:HALF])
        solved.append((top, right[HALF:]))
    for head in range(2):
        top, below = solved[head]
        below = below - dot_fine(corners[head], top)
        below = dot_fine(inv[2 * head + 1], below)
        solved[head] = jnp.concatenate([top, below], axis=0)
    maps = []
    for head in range(2):
        closing = sums[head][TOK - 1 :, :]
        weight = scale * jnp.exp(closing - sums[head])
        moved = dot_right(keys, weight * solved[head], ((0,), (0,)))
        transit = eye_k * jnp.exp(closing) - moved[:, :DK]
        maps.append(jnp.concatenate([transit, moved[:, DK:]], axis=1).astype(BF))
    for place in range(maps_ref.shape[0]):
        maps_ref[place] = maps[place % 2]
    for head in range(2):
        solved_ref[head] = solved[head]
    copies[4].wait()


def read_kernel(
    q_ref, k_ref, decay_ref, gate_ref, gain_ref, solved_ref, keep_ref, send_ref
):
    core = places()[2]
    queries = q_ref[...]
    keys = k_ref[...]
    row, col = grid_iota(TOK, TOK)
    eye = row == col
    inclusive = row >= col
    unit_q = unit_scale(queries)
    scores = dot(queries, keys, ((1,), (1,))) * unit_q * to_row(eye, unit_scale(keys))
    sums = decay_sums(decay_ref[...])
    read = []
    for head in range(2):
        sum_row, sum_column = sums[head]
        fall = jnp.exp(jnp.minimum(sum_column - sum_row, 0.0))
        weights = jnp.where(inclusive, scores * fall, 0.0)
        both = dot_fine(weights, solved_ref[head])
        outer = jnp.exp(sum_column) * unit_q * queries.astype(F32) - both[:, :DK]
        gate = gate_ref[:, head * DV : (head + 1) * DV].astype(F32)
        gated = gain_ref[...] * (gate / (1.0 + jnp.exp(-gate)))
        read.append((both[:, DK:], outer, gated))
    for i in range(3):
        keep_ref[i] = jnp.where(core == 0, read[0][i], read[1][i])
        send_ref[i] = jnp.where(core == 0, read[1][i], read[0][i]).astype(BF)


def after(later_t, later_h, earlier, fine):
    moved = dot_fine(later_t, earlier) if fine else dot_right(later_t, earlier)
    return jnp.concatenate([moved[:, :DK], moved[:, DK:] + later_h], axis=1)


def row_kernel(parts_ref, total_ref, ahead_ref, first_ref):
    x = places()[1]

    def pair(i):
        later = parts_ref[2 * i + 1]
        moved = dot(later[:, :DK], parts_ref[2 * i])
        return jnp.concatenate(
            [moved[:, :DK], moved[:, DK:] + later[:, DK:].astype(F32)], axis=1
        )

    pairs = [pair(i) for i in range(4)]
    upto2 = pairs[0]
    upto4 = after(pairs[1][:, :DK], pairs[1][:, DK:], upto2, True)
    last2 = after(pairs[3][:, :DK], pairs[3][:, DK:], pairs[2], True)
    upto6 = after(pairs[2][:, :DK], pairs[2][:, DK:], upto4, True)
    total = after(last2[:, :DK], last2[:, DK:], upto4, True).astype(BF)
    for place in range(4):
        total_ref[place] = total
    row, col = grid_iota(DK, DK + DV)
    none = jnp.where(row == col, 1.0, 0.0).astype(F32)
    ahead_ref[...] = jnp.where(
        x == 0, none, jnp.where(x == 1, upto2, jnp.where(x == 2, upto4, upto6))
    )
    first_ref[...] = parts_ref[2 * x]


def token_of(group, label):
    return 4 * group + (label if group < 2 else 3 - label)


def out_kernel(rows_ref, ahead_ref, first_ref, keep_ref, came_ref, out_ref):
    y, _, core = places()

    def onward(later, state):
        return dot_right(later[:, :DK], state) + later[:, DK:].astype(F32)

    one = rows_ref[0][:, DK:].astype(F32)
    two = onward(rows_ref[1], one)
    three = onward(rows_ref[2], two)
    start = jnp.where(
        y == 0, jnp.zeros_like(one), jnp.where(y == 1, one, jnp.where(y == 2, two, three))
    )
    ahead = ahead_ref[...]
    chip = dot_fine(ahead[:, :DK], start) + ahead[:, DK:]
    second = onward(first_ref[...], chip)

    def finish(state, inner, outer, gated):
        reached = inner + dot_left(outer, state.astype(BF))
        mean = jnp.sum(reached * reached, axis=1, keepdims=True) * (1.0 / DV)
        return (reached * lax.rsqrt(mean + 1e-06) * gated).astype(BF)

    own = finish(jnp.where(core == 0, chip, second), keep_ref[0], keep_ref[1], keep_ref[2])
    came = [came_ref[i].astype(F32) for i in range(3)]
    other = finish(jnp.where(core == 0, second, chip), *came)
    shards = (jnp.where(core == 0, own, other), jnp.where(core == 0, other, own))
    for label in range(4):
        for shard in range(2):
            for group in range(4):
                source = 16 * token_of(group, label)
                target = 64 * shard + 16 * group
                piece = shards[shard][source : source + 16]
                for side in range(2):
                    out_ref[4 * side + label, target : target + 16] = piece


def lay_kernel(rows_ref, out_ref):
    out_ref[...] = rows_ref[...]


def project_kernel(normed_ref, w0_ref, w2_ref, far_ref, keep_ref, send_ref):
    _, _, core = places()
    along = lax.axis_index("tp")
    weights = [w0_ref[...], far_ref[0], w2_ref[...], far_ref[1]]
    for side in range(2):
        total = None
        for i, weight in enumerate(weights):
            near = (along % 4) ^ i
            label = jnp.where(along < 8, near, 3 - near)
            term = dot(normed_ref[4 * side + label], weight)
            total = term if total is None else total + term
        keep_ref[side] = jnp.where(core == 0, total[:64], total[64:])
        send_ref[side] = jnp.where(core == 0, total[64:], total[:64]).astype(BF)


def join_kernel(keep_ref, came_ref, out_ref):
    for side in range(2):
        total = (keep_ref[side] + came_ref[side].astype(F32)).astype(BF)
        for group in range(4):
            out_ref[4 * side + group] = total[16 * group : 16 * (group + 1)]


def sum_kernel(parts_ref, out_ref):
    columns = parts_ref.shape[2]
    for side in range(2):
        total = parts_ref[4 * side].astype(F32)
        for group in range(1, 4):
            total = total + parts_ref[4 * side + group].astype(F32)
        out_ref[:, side * columns : (side + 1) * columns] = total.astype(BF)


def places():
    at = lax.axis_index("ctx")
    return at // 8, (at // 2) % 4, at % 2


def in_vmem():
    return pl.BlockSpec(memory_space=pltpu.VMEM)


def in_hbm():
    return pl.BlockSpec(memory_space=pltpu.HBM)


def call(kernel, outs, *args, flops=10**3, name=None, ins=None, out_specs=None, scratch=(), room=32):
    if ins is None:
        ins = [in_vmem()] * len(args)
    return pl.pallas_call(
        kernel,
        out_shape=outs,
        in_specs=ins,
        out_specs=jax.tree.map(lambda _: in_vmem(), outs) if out_specs is None else out_specs,
        scratch_shapes=scratch,
        compiler_params=pltpu.CompilerParams(vmem_limit_bytes=room * 1024 * 1024),
        cost_estimate=pl.CostEstimate(flops=flops, bytes_accessed=10**3, transcendentals=0),
        name=name,
    )(*args)


def shape(dims, kind):
    return jax.ShapeDtypeStruct(dims, kind)


def local(
    queries, key_vectors, value_vectors, output_gate, write_rate, log_decay, norm_gain, out_weight
):
    width = out_weight.shape[1]
    half_width = width // 2
    rate, decay = write_rate.T, log_decay.T

    maps, solved, w0 = call(
        map_kernel,
        (
            shape((8, DK, DK + DV), BF),
            shape((2, TOK, DK + DV), F32),
            shape((DV, half_width), BF),
        ),
        key_vectors,
        value_vectors,
        rate,
        decay,
        out_weight,
        ins=[in_hbm()] * 5,
        out_specs=(in_vmem(), in_vmem(), in_vmem()),
        scratch=[
            pltpu.VMEM((TOK, DK), BF),
            pltpu.VMEM((TOK, 2 * DV), BF),
            pltpu.VMEM((2, TOK), F32),
            pltpu.VMEM((2, TOK), F32),
            pltpu.SemaphoreType.DMA((5,)),
        ],
        flops=10**9,
        room=60,
        name="shard_maps",
    )
    lines = [[8 * y + i for i in range(8)] for y in range(4)]
    parts = lax.all_to_all(maps, "ctx", 0, 0, axis_index_groups=lines)
    keep, send = call(
        read_kernel,
        (shape((3, TOK, DV), F32), shape((3, TOK, DV), BF)),
        queries,
        key_vectors,
        decay,
        output_gate,
        norm_gain.reshape(1, DV),
        solved,
        flops=10**9,
        room=60,
        name="read_parts",
    )
    across = [(i, i ^ 1) for i in range(32)]
    came = lax.ppermute(send, "ctx", across)

    w2 = lax.ppermute(w0, "tp", [(j, j ^ 2) for j in range(16)])

    parts, keep, send = lax.optimization_barrier((parts, keep, send))
    total, ahead, first = call(
        row_kernel,
        (shape((4, DK, DK + DV), BF), shape((DK, DK + DV), F32), shape((DK, DK + DV), BF)),
        parts,
        name="row_maps",
    )
    w2, ahead = lax.optimization_barrier((w2, ahead))
    near13 = lax.ppermute(jnp.stack([w0, w2]), "tp", [(j, j ^ 1) for j in range(16)])
    columns = [[8 * y + i for y in range(4)] for i in range(8)]
    rows = lax.all_to_all(total, "ctx", 0, 0, axis_index_groups=columns)
    normed = call(
        out_kernel,
        shape((8, 128, DV), BF),
        rows,
        ahead,
        first,
        keep,
        came,
        flops=10*10**9,
        name="gated_norm",
    )
    pairs = [[8 * y + 4 * pair + 2 * side + core for side in range(2)]
             for y in range(4) for pair in range(2) for core in range(2)]
    close = [[16 * at + token_of(g, m) for at in pair for m in range(4)]
             for pair in pairs for g in range(4)]
    far = [[16 * at + token_of(g, m) for at in pair for g in range(4)]
           for pair in pairs for m in range(4)]
    both = ("ctx", "tp")
    gathered = lax.all_to_all(normed, both, 0, 0, axis_index_groups=close)
    far_rows = call(
        lay_kernel,
        shape((2, DV, half_width), BF),
        near13,
        flops=10*10**9,
        name="lay_rows",
    )
    part, other_part = call(
        project_kernel,
        (shape((2, 64, half_width), F32), shape((2, 64, half_width), BF)),
        gathered,
        w0,
        w2,
        far_rows,
        name="project",
    )
    other_part = lax.ppermute(other_part, "ctx", across)
    partial = call(join_kernel, shape((8, 16, half_width), BF), part, other_part, name="join")
    shares = lax.all_to_all(partial, both, 0, 0, axis_index_groups=far)
    return call(sum_kernel, shape((16, width), BF), shares, name="sum_shares")


def solution(mesh):
    placed = (
        P("ctx", "tp"),
        P("ctx", "tp"),
        P("ctx", "tp"),
        P("ctx", "tp"),
        P("ctx", "tp"),
        P("ctx", "tp"),
        P(),
        P("tp", None),
    )
    return jax.shard_map(
        local, mesh=mesh, in_specs=placed, out_specs=P(("ctx", "tp"), None), check_vma=False
    )
```
